128 devices in a mesh: zon: 32 (over z, x_hi, y), mer: 4 (over x_lo, core).
Axes of the slice: x: 4 (x_hi: 2, x_lo: 2; x = x_hi * 2 + x_lo), y: 4, z: 4, core: 2. Of those that a mesh axis runs over, the one named last changes fastest.
Arguments:
- sea_level: float32 [512, 16384], P('mer', 'zon'), may hold values from -6 to 6
- forcing: float32 [512, 16384], P('mer', 'zon'), may hold values from -6 to 6
- link_weights: float32 [8, 512, 16384], P(None, 'mer', 'zon'), may hold values from 0.1 to 2
- excess: float32 [512, 16384], P('mer', 'zon'), may hold values from 0.05 to 0.5
- ocean_mask: int32 [512, 16384], P('mer', 'zon'), may hold values 0 or 1
- current: float32 [2, 512, 16384], P(None, 'mer', 'zon'), may hold values from -6 to 6
- intersection_block: int32 [128, 128, 8], P(('zon', 'mer')), may hold values from -1 to 511, as said below
- intersection_cols: int32 [128, 128, 8, 128], P(('zon', 'mer')), may hold values from -1 to 127, as said below
- ice_mass: float32 [128, 128, 8, 128], P(('zon', 'mer')), may hold values from 0.2 to 3
- coriolis: float32 [128, 128, 8, 128], P(('zon', 'mer')), may hold values from -1.5 to 1.5
- ice_start: float32 [2, 128, 128, 8, 128], P(None, ('zon', 'mer')), may hold values from -6 to 6
- wind_stress: float32 [2, 128, 128, 8, 128], P(None, ('zon', 'mer')), may hold values from -6 to 6
Outputs:
- surface: float32 [512, 16384], P('mer', 'zon')
- velocity: float32 [2, 128, 128, 8, 128], P(None, ('zon', 'mer'))
The draws below stay inside these ranges and needn't reach their ends.
Inputs may be any that keep to these rules, and one draw needn't show every extreme that they name: `intersection_block`: for each owner device and ice device, the live ocean block numbers come first among the 8 slots and empty slots hold -1; in every draw one ice device receives 8 live blocks from every owner device. `intersection_cols`: within a live intersection block the cells named by different rows are distinct; rows of empty slots are all -1.
All inputs are finite; a program needn't handle non-finite values. No bound on the sum of `ocean_mask` on one device may be relied on, other than what follows from the above.
Results may differ from the reference program's by a relative error of at most 0.00002.
Values sent between devices are 32-bit elements; how exact they have to be, the bound alone decides.
No kernel may reach another device: no remote copies, remote signals or barrier semaphores. Data moves between devices by JAX's collectives and lax.ppermute only.
A program may use at most 256 MiB of HBM per device.

```python
import math
import jax
import jax.numpy as jnp
from jax import lax

LAT_DEV = 128
LON_DEV = 512
BLOCK = 128
SWEEPS = 2
ICE_SWEEPS = 3
NY = 512
NX = 16384
OCEAN_BLOCKS = 512
PAIR_SLOTS = 8
N_ZON = 32
N_MER = 4
DEVICES = 128


def intersection_lists(key):
    base = jax.random.fold_in(key, 7)
    subkeys = jax.random.split(base, 5)
    counts = jax.random.randint(subkeys[0], (DEVICES, DEVICES), 0, PAIR_SLOTS + 1)
    full_target = jax.random.randint(subkeys[1], (), 0, DEVICES)
    ice_index = jnp.arange(DEVICES)
    counts = jnp.where(ice_index[None, :] == full_target, PAIR_SLOTS, counts)
    empty_target = (full_target + 1) % DEVICES
    counts = counts.at[0, empty_target].set(0)
    slot_index = jnp.arange(PAIR_SLOTS)
    is_live = slot_index[None, None, :] < counts[:, :, None]
    chosen = jax.random.randint(subkeys[2], (DEVICES, DEVICES, PAIR_SLOTS), 0, OCEAN_BLOCKS)
    chosen = chosen.at[0, full_target, 0].set(OCEAN_BLOCKS - 1)
    blocks = jnp.where(is_live, chosen, -1)
    scores = jax.random.randint(subkeys[3], (DEVICES, DEVICES, PAIR_SLOTS, BLOCK), 0, 1 << 20) * BLOCK + jnp.arange(BLOCK)
    shuffled = jnp.argsort(scores, axis=-1).astype(jnp.int32)
    keep_row = jax.random.randint(subkeys[4], (DEVICES, DEVICES, PAIR_SLOTS, BLOCK), 0, 8) > 0
    columns = jnp.where(is_live[..., None] & keep_row, shuffled, -1)
    return (blocks.astype(jnp.int32), columns.astype(jnp.int32))


def draw_intersection_block(key, part):
    return intersection_lists(key)[0]


def draw_intersection_cols(key, part):
    return intersection_lists(key)[1]


def set_ends(entries, stream_key, low, top_value):
    longest = entries.shape.index(max(entries.shape))
    spots = []
    for shift in (0, 1):
        where = [jax.random.randint(jax.random.fold_in(stream_key, axis), (), 0, length) for axis, length in enumerate(entries.shape)]
        where[longest] = (where[longest] + shift) % entries.shape[longest]
        spots.append(tuple(where))
    return entries.at[spots[0]].set(low).at[spots[1]].set(top_value)


def block_scale(own_key, shape, cuts, smallest, high):
    gain = 1.0
    for axis_at, parts in cuts:
        steps = jax.random.uniform(jax.random.fold_in(jax.random.fold_in(own_key, 6), axis_at), (parts,), jnp.float32, smallest / len(cuts), high / len(cuts))
        gain = gain * jnp.repeat(jnp.exp(steps), shape[axis_at] // parts).reshape((-1,) + (1,) * (len(shape) - 1 - axis_at))
    return gain


def noise(stream_key, shape, deviation, limit, cuts=(), kind=jnp.bfloat16):
    array = deviation * jax.random.normal(stream_key, shape, jnp.float32)
    if cuts:
        array = array * block_scale(stream_key, shape, cuts, -0.22, 0.18)
    return jnp.clip(array, -limit, limit).astype(kind)


def setup_inputs(seed: int = 0) -> dict:
    splits = jax.random.split(jax.random.key(seed), 13)
    return {
        "sea_level": noise(splits[0], (NY, NX), 1.0, 6.0, ((0, 4), (1, 32)), jnp.float32),
        "forcing": noise(splits[1], (NY, NX), 1.0, 6.0, ((0, 4), (1, 32)), jnp.float32),
        "link_weights": jnp.clip(jnp.exp(math.log(2.0) - 2.9957323 * jax.random.uniform(splits[2], (8, NY, NX), jnp.float32) ** block_scale(splits[2], (8, NY, NX), ((1, 4), (2, 32)), -0.2, 0.2)), 0.1, 2.0),
        "excess": jnp.clip(jnp.exp(math.log(0.5) - 2.3025851 * jax.random.uniform(splits[3], (NY, NX), jnp.float32) ** block_scale(splits[3], (NY, NX), ((0, 4), (1, 32)), -0.2, 0.2)), 0.05, 0.5),
        "ocean_mask": set_ends((jax.random.randint(splits[4], (NY, NX), 0, 8) < 7).astype(jnp.int32), jax.random.fold_in(splits[4], 1), 0, 1),
        "current": noise(splits[5], (2, NY, NX), 1.0, 6.0, ((1, 4), (2, 32)), jnp.float32),
        "intersection_block": draw_intersection_block(jax.random.fold_in(splits[12], 71), 0),
        "intersection_cols": draw_intersection_cols(jax.random.fold_in(splits[12], 71), 0),
        "ice_mass": jnp.clip(jnp.exp(math.log(3.0) - 2.7080502 * jax.random.uniform(splits[8], (DEVICES, DEVICES, PAIR_SLOTS, BLOCK), jnp.float32) ** block_scale(splits[8], (DEVICES, DEVICES, PAIR_SLOTS, BLOCK), ((0, 128),), -0.2, 0.2)), 0.2, 3.0),
        "coriolis": jnp.clip(jax.random.uniform(splits[9], (DEVICES, DEVICES, PAIR_SLOTS, BLOCK), jnp.float32, -1.5, 1.5) * block_scale(splits[9], (DEVICES, DEVICES, PAIR_SLOTS, BLOCK), ((0, 128),), -0.4, 0.0), -1.5, 1.5),
        "ice_start": noise(splits[10], (2, DEVICES, DEVICES, PAIR_SLOTS, BLOCK), 1.0, 6.0, ((1, 128),), jnp.float32),
        "wind_stress": noise(splits[11], (2, DEVICES, DEVICES, PAIR_SLOTS, BLOCK), 1.0, 6.0, ((1, 128),), jnp.float32),
    }


drag_coeff = 1.0
link_coeff = 0.5
neighbour_steps = ((0, 1), (0, -1), (1, 0), (-1, 0), (1, 1), (1, -1), (-1, 1), (-1, -1))


def colour_sequence(sweep_count):
    return [0] + [1, 2, 3, 2, 1, 0] * sweep_count


def gauss_seidel(surface, source, link_weights, diagonal, is_ocean, pad_fn):
    row_count, col_count = surface.shape
    row_parity = lax.broadcasted_iota(jnp.int32, (row_count, col_count), 0) % 2
    col_parity = lax.broadcasted_iota(jnp.int32, (row_count, col_count), 1) % 2
    colours = 2 * row_parity + col_parity
    for colour in colour_sequence(SWEEPS):
        padded = pad_fn(surface)
        gathered = source
        for position, (row_step, col_step) in enumerate(neighbour_steps):
            gathered = gathered + link_weights[position] * padded[1 + row_step:1 + row_step + row_count, 1 + col_step:1 + col_step + col_count]
        surface = jnp.where(is_ocean & (colours == colour), gathered / diagonal, surface)
    return surface


def pad_whole(surface):
    wrapped = jnp.concatenate([surface[:, -1:], surface, surface[:, :1]], axis=1)
    return jnp.pad(wrapped, ((1, 1), (0, 0)))


def along_block(values):
    padded = jnp.pad(values, [(0, 0)] * (values.ndim - 1) + [(1, 1)])
    return padded[..., :-2] + padded[..., 2:]


def ice_momentum(ice_mass, coriolis, ice_start, wind_stress, current):
    diagonal = ice_mass + drag_coeff + 2.0 * link_coeff
    turning = coriolis * ice_mass
    determinant = diagonal * diagonal + turning * turning
    base_east = ice_mass * ice_start[0] + wind_stress[0] + drag_coeff * current[0]
    base_north = ice_mass * ice_start[1] + wind_stress[1] + drag_coeff * current[1]
    velocity = ice_start
    for sweep_index in range(ICE_SWEEPS):
        beside = along_block(velocity)
        right_east = base_east + link_coeff * beside[0]
        right_north = base_north + link_coeff * beside[1]
        velocity = jnp.stack([(diagonal * right_east + turning * right_north) / determinant,
                              (diagonal * right_north - turning * right_east) / determinant])
    return velocity


def reference(sea_level, forcing, link_weights, excess, ocean_mask, current, intersection_block, intersection_cols, ice_mass, coriolis, ice_start, wind_stress):
    blocks = current.reshape(2, N_MER, LAT_DEV, N_ZON, LON_DEV).transpose(0, 3, 1, 2, 4).reshape(2, DEVICES, OCEAN_BLOCKS, BLOCK)
    owners = jnp.arange(DEVICES, dtype=jnp.int32)[:, None, None]
    picked = blocks[:, owners, jnp.maximum(intersection_block, 0).astype(jnp.int32)]
    valid = intersection_cols >= 0
    values = jnp.take_along_axis(picked, jnp.maximum(intersection_cols, 0)[None], axis=4)
    values = jnp.where(valid[None], values, 0.0)
    ice_current = values.transpose(0, 2, 1, 3, 4)
    velocity = ice_momentum(ice_mass, coriolis, ice_start, wind_stress, ice_current)
    ice_drag = drag_coeff * (velocity - ice_current)
    owner_drag = ice_drag.transpose(2, 0, 1, 3, 4)
    target = jnp.where(valid, jnp.maximum(intersection_block, 0)[..., None] * BLOCK + intersection_cols, OCEAN_BLOCKS * BLOCK).astype(jnp.int32)

    def scatter_owner(pair):
        owner_target, owner_values = pair
        return jnp.zeros((2, OCEAN_BLOCKS * BLOCK), jnp.float32).at[:, owner_target.reshape(-1)].add(owner_values.reshape(2, -1), mode="drop")

    summed = lax.map(scatter_owner, (target, owner_drag))
    stress_grid = summed.reshape(N_ZON, N_MER, 2, LAT_DEV, LON_DEV).transpose(2, 1, 3, 0, 4).reshape(2, N_MER * LAT_DEV, N_ZON * LON_DEV)
    stress_north = stress_grid[1]
    zonal_diff = jnp.roll(stress_north, -1, axis=1) - jnp.roll(stress_north, 1, axis=1)
    padded_east = jnp.pad(stress_grid[0], ((1, 1), (0, 0)))
    meridional_diff = padded_east[2:] - padded_east[:-2]
    source = forcing + zonal_diff - meridional_diff
    is_ocean = ocean_mask > 0
    diagonal = jnp.where(is_ocean, (1.0 + excess) * jnp.sum(link_weights, axis=0), 1.0)
    surface = jnp.where(is_ocean, sea_level, 0.0)
    surface = gauss_seidel(surface, source, link_weights, diagonal, is_ocean, pad_whole)
    return surface, velocity
```

```python
import jax
import jax.numpy as jnp
from jax import lax
from jax.experimental import pallas as pl
from jax.experimental.pallas import tpu as pltpu
from jax.sharding import PartitionSpec as P

SWEEPS = 2
ICE_SWEEPS = 3
DRAG = 1.0
LINK = 0.5
STEPS = ((0, 1), (0, -1), (1, 0), (-1, 0), (1, 1), (1, -1), (-1, 1), (-1, -1))
COLOURS = (0,) + (1, 2, 3, 2, 1, 0) * SWEEPS
F32, BF16, I32 = jnp.float32, jnp.bfloat16, jnp.int32
MIB = 1 << 20
ROWS, COLS, XROWS, XCOLS = 64, 256, 72, 384


def params(vmem=48):
    return pltpu.CompilerParams(vmem_limit_bytes=vmem * MIB)


def cost(flops, moved):
    return pl.CostEstimate(flops=flops, bytes_accessed=moved, transcendentals=0)


def iota(shape, dim):
    return lax.broadcasted_iota(I32, shape, dim)


def lane_gather(values, index):
    return jnp.take_along_axis(values, index, axis=1, mode="promise_in_bounds")


def split3(values):
    high = values.astype(BF16)
    rest = values - high.astype(F32)
    middle = rest.astype(BF16)
    low = (rest - middle.astype(F32)).astype(BF16)
    return high, middle, low


def dot(a, b):
    return jnp.dot(a, b, preferred_element_type=F32)


def fetch_kernel(current, key, cols, out, table, rows):
    count = cols.shape[0]
    for c in range(2):
        for k in range(4):
            parts = split3(current[c, :, 128 * k : 128 * k + 128])
            for part in range(3):
                table[part, 128 * k : 128 * k + 128, 128 * c : 128 * c + 128] = parts[part]
    step = min(8 * count, 256)
    for start in range(0, 8 * count, step):
        hot = jnp.where(key[start : start + step] == iota((step, 512), 1), 1.0, 0.0).astype(BF16)
        rows[start : start + step] = dot(hot, table[0]) + dot(hot, table[1]) + dot(hot, table[2])

    def body(i, carry):
        index = cols[i]
        inside = jnp.maximum(index, 0)
        tile = rows[pl.ds(pl.multiple_of(8 * i, 8), 8)]
        for c in range(2):
            out[i, c] = jnp.where(index >= 0, lane_gather(tile[:, 128 * c : 128 * c + 128], inside), 0.0)
        return carry

    lax.fori_loop(0, count, body, 0, unroll=8)


def fetch(current, key, cols):
    count = cols.shape[0]
    return pl.pallas_call(
        fetch_kernel,
        out_shape=jax.ShapeDtypeStruct((count, 2, 8, 128), F32),
        scratch_shapes=[pltpu.VMEM((3, 512, 256), BF16), pltpu.VMEM((8 * count, 256), F32)],
        compiler_params=params(),
        cost_estimate=cost(10**9, 2 * MIB),
        name="fetch",
    )(current, key, cols)


def invert_kernel(cols, key, inverse, hot):
    count = cols.shape[0]
    hot[...] = jnp.where(iota((512, 8 * count), 0) == key[...], 1.0, 0.0).astype(BF16)
    lane = iota((8, 1024), 1)
    weights = jnp.where(lane // 128 == iota((8, 1024), 0), lane % 128 + 1, 0).astype(F32).astype(BF16)
    place = iota((128, 128), 0)

    def body(i, carry):
        index = cols[i]
        target = jnp.where(index >= 0, (index >> 1) + 64 * (index & 1), -1)
        masks = [
            jnp.where(place == jnp.broadcast_to(target[s : s + 1], (128, 128)), 1.0, 0.0).astype(BF16)
            for s in range(8)
        ]
        found = lax.dot_general(
            weights, jnp.concatenate(masks, axis=1), (((1,), (1,)), ((), ())), preferred_element_type=F32
        )
        inverse[i] = found.astype(I32) - 1
        return carry

    lax.fori_loop(0, count, body, 0, unroll=2)


def invert(cols, key):
    count = cols.shape[0]
    return pl.pallas_call(
        invert_kernel,
        out_shape=(jax.ShapeDtypeStruct((count, 8, 128), I32), jax.ShapeDtypeStruct((512, 8 * count), BF16)),
        compiler_params=params(),
        cost_estimate=cost(10**10, 2 * MIB),
        name="invert",
    )(cols, key)


def ice_kernel(mass_ref, coriolis_ref, start_ref, wind_ref, current_ref, velocity_ref, drag_ref):
    lane = iota((8, 128), 1)

    def beside(v):
        before = jnp.where(lane == 0, 0.0, pltpu.roll(v, 1, 1))
        after = jnp.where(lane == 127, 0.0, pltpu.roll(v, 127, 1))
        return before + after

    def body(i, carry):
        mass = mass_ref[i]
        a = mass + DRAG + 2.0 * LINK
        t = coriolis_ref[i] * mass
        inverse = 1.0 / (a * a + t * t)
        a = a * inverse
        t = t * inverse
        east, north = start_ref[0, i], start_ref[1, i]
        current = (current_ref[i, 0], current_ref[i, 1])
        base_east = mass * east + wind_ref[0, i] + DRAG * current[0]
        base_north = mass * north + wind_ref[1, i] + DRAG * current[1]
        for _ in range(ICE_SWEEPS):
            right_east = base_east + LINK * beside(east)
            right_north = base_north + LINK * beside(north)
            east = a * right_east + t * right_north
            north = a * right_north - t * right_east
        velocity_ref[0, i] = east
        velocity_ref[1, i] = north
        drag_ref[i, 0] = DRAG * (east - current[0])
        drag_ref[i, 1] = DRAG * (north - current[1])
        return carry

    lax.fori_loop(0, mass_ref.shape[0], body, 0, unroll=4)


def ice(mass, coriolis, start, wind, current):
    count = mass.shape[0]
    step = min(count, 32)
    one = pl.BlockSpec((step, 8, 128), lambda i: (i, 0, 0))
    two = pl.BlockSpec((2, step, 8, 128), lambda i: (0, i, 0, 0))
    pair = pl.BlockSpec((step, 2, 8, 128), lambda i: (i, 0, 0, 0))
    return pl.pallas_call(
        ice_kernel,
        grid=(count // step,),
        in_specs=[one, one, two, two, pair],
        out_specs=(two, pair),
        out_shape=(
            jax.ShapeDtypeStruct((2, count, 8, 128), F32),
            jax.ShapeDtypeStruct((count, 2, 8, 128), F32),
        ),
        compiler_params=params(),
        cost_estimate=cost(10**7, 6 * MIB),
        name="ice",
    )(mass, coriolis, start, wind, current)


def scatter_kernel(drag, inverse, hot, planes, side, ends, corner, parts):
    count = inverse.shape[0]
    zero = jnp.zeros((8, 128), F32)

    def body(j, carry):
        rows = pl.ds(pl.multiple_of(16 * j, 16), 16)
        for c in range(2):
            halves = []
            for i in (2 * j, 2 * j + 1):
                index = inverse[i]
                halves.append(jnp.where(index >= 0, lane_gather(drag[i, c], jnp.maximum(index, 0)), zero))
            pieces = split3(jnp.concatenate(halves, axis=0))
            for part in range(3):
                parts[part, rows, 128 * c : 128 * c + 128] = pieces[part]
        return carry

    lax.fori_loop(0, count // 2, body, 0, unroll=4)
    total = dot(hot[...], parts[0]) + dot(hot[...], parts[1]) + dot(hot[...], parts[2])
    low = iota((ROWS, 128), 1) < 64
    lane = iota((ROWS, 128), 1)
    edge = jnp.zeros((ROWS, 128), F32)
    for c in range(2):
        for py in range(2):
            for h in range(2):
                first = 256 * h + 64 * py
                a = total[first : first + 64, 128 * c : 128 * c + 128]
                b = total[first + 128 : first + 192, 128 * c : 128 * c + 128]
                even = jnp.where(low, a, pltpu.roll(b, 64, 1))
                odd = jnp.where(low, pltpu.roll(a, 64, 1), b)
                for px, value in ((0, even), (1, odd)):
                    plane = 2 * py + px
                    planes[c, plane, :, 128 * h : 128 * h + 128] = value
                    ends[c, plane, :, 128 * h : 128 * h + 128] = jnp.where(
                        iota((8, 128), 0) < 4, value[:8], value[56:]
                    )
                    item = 4 * c + plane
                    if h == 0:
                        moved = pltpu.roll(value, 8 * item, 1) if item else value
                        edge = jnp.where(lane // 8 == item, moved, edge)
                    else:
                        moved = pltpu.roll(value, (64 + 8 * item + 8) % 128, 1) if item != 7 else value
                        edge = jnp.where(lane // 8 == 8 + item, moved, edge)
    side[...] = edge
    corner[...] = jnp.where(iota((8, 128), 0) < 4, edge[:8], edge[56:])


def scatter(drag, inverse, hot):
    count = inverse.shape[0]
    return pl.pallas_call(
        scatter_kernel,
        out_shape=(
            jax.ShapeDtypeStruct((2, 4, ROWS, COLS), F32),
            jax.ShapeDtypeStruct((ROWS, 128), F32),
            jax.ShapeDtypeStruct((2, 4, 8, COLS), F32),
            jax.ShapeDtypeStruct((8, 128), F32),
        ),
        scratch_shapes=[pltpu.VMEM((3, 8 * count, 256), BF16)],
        compiler_params=params(),
        cost_estimate=cost(10**9, 3 * MIB),
        name="scatter",
    )(drag, inverse, hot)


ARRAYS = 11


def prepare_kernel(
    sea, forcing, weights, excess, mask, planes, left, right, ends, left_corner, right_corner, halves
):
    lane = iota((8, 128), 1)
    low = lane < 64
    order = jnp.where(low, 2 * lane, 2 * lane - 127)
    swapped = jnp.where(low, 2 * lane + 1, 2 * lane - 128)

    def split(t, carry):
        rows = pl.ds(pl.multiple_of(8 * t, 8), 8)
        w = [weights[k, rows, :] for k in range(8)]
        total = ((w[0] + w[1]) + (w[2] + w[3])) + ((w[4] + w[5]) + (w[6] + w[7]))
        ocean = mask[rows, :] > 0
        inverse = jnp.where(ocean, 1.0 / ((1.0 + excess[rows, :]) * total), 0.0)
        arrays = [v * inverse for v in w]
        arrays += [inverse, forcing[rows, :], jnp.where(ocean, sea[rows, :], 0.0)]
        for n, array in enumerate(arrays):
            for h in range(2):
                a = lane_gather(array[:, 256 * h : 256 * h + 128], order)
                b = lane_gather(array[:, 256 * h + 128 : 256 * h + 256], swapped)
                halves[4 * n + h, rows, :] = jnp.where(low, a, b)
                halves[4 * n + 2 + h, rows, :] = pltpu.roll(jnp.where(low, b, a), 64, 1)
        return carry

    lax.fori_loop(0, 2 * ROWS // 8, split, 0)

    def pack(t, carry):
        out_rows = pl.ds(pl.multiple_of(8 * t, 8), 8)
        for py in range(2):
            rows = pl.ds(16 * t + py, 8, stride=2)
            packed = [[jnp.zeros((8, 128), F32)] * 2, [jnp.zeros((8, 128), F32)] * 2]
            for n in range(ARRAYS):
                for px in range(2):
                    for h in range(2):
                        value = halves[4 * n + 2 * px + h, rows, :]
                        planes[n, 2 * py + px, out_rows, 128 * h : 128 * h + 128] = value
                        item = 2 * n + px
                        shift = (8 * (item % 16) + (8 if h else 0)) % 128
                        moved = pltpu.roll(value, shift, 1) if shift else value
                        packed[h][item // 16] = jnp.where(lane // 8 == item % 16, moved, packed[h][item // 16])
            for g in range(2):
                left[py, out_rows, 128 * g : 128 * g + 128] = packed[0][g]
                right[py, out_rows, 128 * g : 128 * g + 128] = packed[1][g]
        return carry

    lax.fori_loop(0, ROWS // 8, pack, 0)
    top = iota((8, 256), 0) < 4
    for n in range(ARRAYS):
        for p in range(4):
            ends[n, p] = jnp.where(top, planes[n, p, 0:8], planes[n, p, 56:64])
    for py in range(2):
        left_corner[py] = jnp.where(top, left[py, 0:8], left[py, 56:64])
        right_corner[py] = jnp.where(top, right[py, 0:8], right[py, 56:64])


def prepare(sea, forcing, weights, excess, mask):
    return pl.pallas_call(
        prepare_kernel,
        out_shape=(
            jax.ShapeDtypeStruct((ARRAYS, 4, ROWS, COLS), F32),
            jax.ShapeDtypeStruct((2, ROWS, 256), F32),
            jax.ShapeDtypeStruct((2, ROWS, 256), F32),
            jax.ShapeDtypeStruct((ARRAYS, 4, 8, COLS), F32),
            jax.ShapeDtypeStruct((2, 8, 256), F32),
            jax.ShapeDtypeStruct((2, 8, 256), F32),
        ),
        scratch_shapes=[pltpu.VMEM((4 * ARRAYS, 2 * ROWS, 128), F32)],
        compiler_params=params(),
        cost_estimate=cost(10**7, 7 * MIB),
        name="prepare",
    )(sea, forcing, weights, excess, mask)


def extend_kernel(planes, right, left, below, above, below_right, below_left, above_right, above_left, out):
    lane = iota((ROWS, 128), 1)
    lane8 = lane[:8]
    top = iota((8, 128), 0) < 4
    for n in range(ARRAYS):
        for p in range(4):
            py, px = p // 2, p % 2
            item = 2 * n + px
            group, slot = item // 16, item % 16
            span = slice(128 * group, 128 * group + 128)

            def place(from_right, from_left, lanes):
                r = pltpu.roll(from_right, (128 - 8 * slot) % 128, 1) if slot else from_right
                s = pltpu.roll(from_left, (120 - 8 * slot) % 128, 1) if slot != 15 else from_left
                return jnp.where(lanes < 8, r, jnp.where(lanes >= 120, s, 0.0))

            out[n, p, 0:ROWS, 0:COLS] = planes[n, p]
            out[n, p, 0:ROWS, COLS:XCOLS] = place(right[py, :, span], left[py, :, span], lane)
            out[n, p, ROWS:XROWS, 0:COLS] = jnp.where(iota((8, 256), 0) < 4, below[n, p], above[n, p])
            out[n, p, ROWS:XROWS, COLS:XCOLS] = place(
                jnp.where(top, below_right[py, :, span], above_right[py, :, span]),
                jnp.where(top, below_left[py, :, span], above_left[py, :, span]),
                lane8,
            )


def extend(*arrays):
    return pl.pallas_call(
        extend_kernel,
        out_shape=jax.ShapeDtypeStruct((ARRAYS, 4, XROWS, XCOLS), F32),
        compiler_params=params(),
        cost_estimate=cost(10**7, 8 * MIB),
        name="extend",
    )(*arrays)


def row_shift(value, step):
    return pltpu.roll(value, (-step) % XROWS, 0) if step else value


def col_shift(value, step):
    return pltpu.roll(value, (-step) % XCOLS, 1) if step else value


def neighbour(step, parity):
    return (step + parity) // 2


def sweep_kernel(operator, stress, right, left, below, above, below_right, below_left, above_right, above_left, out, wide, source, field, natural):
    lane = iota((ROWS, 128), 1)
    top = iota((8, 128), 0) < 4
    for c in range(2):
        for p in range(4):
            item = 4 * c + p

            def place(from_right, from_left, lanes):
                r = pltpu.roll(from_right, (128 - 8 * item) % 128, 1) if item else from_right
                s = pltpu.roll(from_left, (56 - 8 * item) % 128, 1) if item != 7 else from_left
                return jnp.where(lanes < 64, r, s)

            wide[c, p, 0:ROWS, 0:COLS] = stress[c, p]
            wide[c, p, 0:ROWS, COLS:XCOLS] = place(right[...], left[...], lane)
            wide[c, p, ROWS:XROWS, 0:COLS] = jnp.where(iota((8, 256), 0) < 4, below[c, p], above[c, p])
            wide[c, p, ROWS:XROWS, COLS:XCOLS] = place(
                jnp.where(top, below_right[...], above_right[...]),
                jnp.where(top, below_left[...], above_left[...]),
                lane[:8],
            )
    for p in range(4):
        py, px = p // 2, p % 2
        north = wide[1, 2 * py + 1 - px]
        east = wide[0, 2 * (1 - py) + px]
        zonal = col_shift(north, neighbour(1, px)) - col_shift(north, neighbour(-1, px))
        meridional = row_shift(east, neighbour(1, py)) - row_shift(east, neighbour(-1, py))
        source[p] = (operator[9, p] + zonal - meridional) * operator[8, p]
        field[p] = operator[10, p]
    for colour in COLOURS:
        py, px = colour // 2, colour % 2
        value = source[colour]
        for k, (dy, dx) in enumerate(STEPS):
            plane = 2 * (py ^ (dy & 1)) + (px ^ (dx & 1))
            v = field[plane]
            if dy:
                v = row_shift(v, neighbour(dy, py))
            if dx:
                v = col_shift(v, neighbour(dx, px))
            value = value + operator[k, colour] * v
        field[colour] = value
    lane = iota((ROWS, 128), 1)
    even_lane = lane % 2 == 0
    first = lane // 2
    for py in range(2):
        for h in range(2):
            even = field[2 * py, 0:ROWS, 128 * h : 128 * h + 128]
            odd = field[2 * py + 1, 0:ROWS, 128 * h : 128 * h + 128]
            for b in range(2):
                for t in range(ROWS // 8):
                    index = first[:8] + 64 * b
                    e = lane_gather(even[8 * t : 8 * t + 8], index)
                    o = lane_gather(odd[8 * t : 8 * t + 8], index)
                    natural[2 * h + b, pl.ds(16 * t + py, 8, stride=2), :] = jnp.where(even_lane[:8], e, o)
    for k in range(4):
        out[:, 128 * k : 128 * k + 128] = natural[k]


def sweep(*arrays):
    return pl.pallas_call(
        sweep_kernel,
        out_shape=jax.ShapeDtypeStruct((128, 512), F32),
        scratch_shapes=[
            pltpu.VMEM((2, 4, XROWS, XCOLS), F32),
            pltpu.VMEM((4, XROWS, XCOLS), F32),
            pltpu.VMEM((4, XROWS, XCOLS), F32),
            pltpu.VMEM((4, 128, 128), F32),
        ],
        compiler_params=params(),
        cost_estimate=cost(10**8, 6 * MIB),
        name="sweep",
    )(*arrays)


AXES = ("zon", "mer")


def exchange(values):
    return lax.all_to_all(values, AXES, split_axis=0, concat_axis=0, tiled=True)


def from_neighbour(values, dz, dm):
    nz, nm = lax.axis_size("zon"), lax.axis_size("mer")
    pairs = [
        (((z + dz) % nz) * nm + m + dm, z * nm + m)
        for z in range(nz)
        for m in range(nm)
        if 0 <= m + dm < nm
    ]
    return lax.ppermute(values, AXES, pairs)


def surround(left_edge, right_edge, ends, left_corner, right_corner):
    return (
        from_neighbour(left_edge, 1, 0),
        from_neighbour(right_edge, -1, 0),
        from_neighbour(ends, 0, 1),
        from_neighbour(ends, 0, -1),
        from_neighbour(left_corner, 1, 1),
        from_neighbour(right_corner, -1, 1),
        from_neighbour(left_corner, 1, -1),
        from_neighbour(right_corner, -1, -1),
    )


def local(
    sea_level,
    forcing,
    link_weights,
    excess,
    ocean_mask,
    current,
    intersection_block,
    intersection_cols,
    ice_mass,
    coriolis,
    ice_start,
    wind_stress,
):
    blocks = intersection_block[0]
    cols = intersection_cols[0]
    slots = blocks.size
    row, part = blocks >> 2, blocks & 3
    fetch_key = jnp.where(blocks >= 0, part * 128 + row, -1).reshape(slots, 1)
    scatter_key = jnp.where(blocks >= 0, part * 128 + (row & 1) * 64 + (row >> 1), -1).reshape(1, slots)

    ice_current = exchange(fetch(current, fetch_key, cols))
    planes, *edges = prepare(sea_level, forcing, link_weights, excess, ocean_mask)
    operator = extend(planes, *surround(*edges))
    inverse, hot = invert(cols, scatter_key)
    velocity, drag = ice(ice_mass[0], coriolis[0], ice_start[:, 0], wind_stress[:, 0], ice_current)
    stress, side, ends, corner = scatter(exchange(drag), inverse, hot)
    surface = sweep(operator, stress, *surround(side, side, ends, corner, corner))
    return surface, velocity[:, None]


def solution(mesh):
    return jax.shard_map(
        local,
        mesh=mesh,
        in_specs=(
            P("mer", "zon"),
            P("mer", "zon"),
            P(None, "mer", "zon"),
            P("mer", "zon"),
            P("mer", "zon"),
            P(None, "mer", "zon"),
            P(("zon", "mer"), None, None),
            P(("zon", "mer"), None, None, None),
            P(("zon", "mer"), None, None, None),
            P(("zon", "mer"), None, None, None),
            P(None, ("zon", "mer"), None, None, None),
            P(None, ("zon", "mer"), None, None, None),
        ),
        out_specs=(P("mer", "zon"), P(None, ("zon", "mer"), None, None, None)),
        check_vma=False,
    )
```

```python
import jax
import jax.numpy as jnp
from jax import lax
from jax.experimental import pallas as pl
from jax.experimental.pallas import tpu as pltpu
from jax.sharding import PartitionSpec as P

SWEEPS = 2
ICE_SWEEPS = 3
DRAG = 1.0
LINK = 0.5
STEPS = ((0, 1), (0, -1), (1, 0), (-1, 0), (1, 1), (1, -1), (-1, 1), (-1, -1))
COLOURS = (0,) + (1, 2, 3, 2, 1, 0) * SWEEPS
F32, BF16, I32 = jnp.float32, jnp.bfloat16, jnp.int32
MIB = 1 << 20
ROWS, COLS, XROWS, XCOLS = 64, 256, 72, 384


def params(vmem=48):
    return pltpu.CompilerParams(vmem_limit_bytes=vmem * MIB)


def cost(flops, moved):
    return pl.CostEstimate(flops=flops, bytes_accessed=moved, transcendentals=0)


def iota(shape, dim):
    return lax.broadcasted_iota(I32, shape, dim)


def lane_gather(values, index):
    return jnp.take_along_axis(values, index, axis=1, mode="promise_in_bounds")


def split3(values):
    high = values.astype(BF16)
    rest = values - high.astype(F32)
    middle = rest.astype(BF16)
    low = (rest - middle.astype(F32)).astype(BF16)
    return high, middle, low


def dot(a, b):
    return jnp.dot(a, b, preferred_element_type=F32)


def beside(values, lane):
    before = jnp.where(lane == 0, 0.0, pltpu.roll(values, 1, 1))
    after = jnp.where(lane == 127, 0.0, pltpu.roll(values, 127, 1))
    return LINK * (before + after)


def turn(a, t, east, north):
    return a * east + t * north, a * north - t * east


def sweep_ice(a, t, east, north, base_east, base_north, lane):
    return turn(a, t, base_east + beside(east, lane), base_north + beside(north, lane))


def respond(a, t, current_east, current_north, lane):
    east, north = turn(a, t, current_east, current_north)
    for _ in range(ICE_SWEEPS - 1):
        east, north = sweep_ice(a, t, east, north, current_east, current_north, lane)
    return east, north


GROUP = 8


def send_kernel(current, key, cols, mass_ref, coriolis_ref, start_ref, wind_ref, out, table, rows):
    count = cols.shape[0]

    @pl.when(pl.program_id(0) == 0)
    def _():
        for c in range(2):
            for k in range(4):
                parts = split3(current[c, :, 128 * k : 128 * k + 128])
                for part in range(3):
                    table[part, 128 * k : 128 * k + 128, 128 * c : 128 * c + 128] = parts[part]

    hot = jnp.where(key[...] == iota((8 * count, 512), 1), 1.0, 0.0).astype(BF16)
    rows[...] = dot(hot, table[0]) + dot(hot, table[1]) + dot(hot, table[2])
    tall = 8 * GROUP
    lane = iota((tall, 128), 1)

    def body(g, carry):
        group = pl.ds(GROUP * g, GROUP)
        tile = rows[pl.ds(pl.multiple_of(tall * g, tall), tall)]
        index = cols[group].reshape(tall, 128)
        inside = jnp.maximum(index, 0)
        for c in range(2):
            got = jnp.concatenate(
                [lane_gather(tile[8 * i : 8 * i + 8, 128 * c : 128 * c + 128], inside[8 * i : 8 * i + 8]) for i in range(GROUP)],
                axis=0,
            )
            out[group, 4 + c] = jnp.where(index >= 0, DRAG * got, 0.0).reshape(GROUP, 8, 128)
        mass = mass_ref[group].reshape(tall, 128)
        a = mass + DRAG + 2.0 * LINK
        t = coriolis_ref[group].reshape(tall, 128) * mass
        inverse = 1.0 / (a * a + t * t)
        a = a * inverse
        t = t * inverse
        east = start_ref[0, group].reshape(tall, 128)
        north = start_ref[1, group].reshape(tall, 128)
        base_east = mass * east + wind_ref[0, group].reshape(tall, 128)
        base_north = mass * north + wind_ref[1, group].reshape(tall, 128)
        for _ in range(ICE_SWEEPS):
            east, north = sweep_ice(a, t, east, north, base_east, base_north, lane)
        for n, value in enumerate((east, north, a, t)):
            out[group, n] = value.reshape(GROUP, 8, 128)
        return carry

    lax.fori_loop(0, count // GROUP, body, 0)


def chunked(count):
    step = min(count, 32)
    one = pl.BlockSpec((step, 8, 128), lambda i: (i, 0, 0))
    two = pl.BlockSpec((2, step, 8, 128), lambda i: (0, i, 0, 0))
    response = pl.BlockSpec((step, 4, 8, 128), lambda i: (i, 0, 0, 0))
    current = pl.BlockSpec((step, 2, 8, 128), lambda i: (i, 2, 0, 0))
    return step, count // step, one, two, response, current


def send(current, key, cols, mass, coriolis, start, wind):
    count = cols.shape[0]
    step, grid, one, two, _, _ = chunked(count)
    return pl.pallas_call(
        send_kernel,
        grid=(grid,),
        in_specs=[
            pl.BlockSpec((2, 128, 512), lambda i: (0, 0, 0)),
            pl.BlockSpec((8 * step, 1), lambda i: (i, 0)),
            one,
            one,
            one,
            two,
            two,
        ],
        out_specs=pl.BlockSpec((step, 6, 8, 128), lambda i: (i, 0, 0, 0)),
        out_shape=jax.ShapeDtypeStruct((count, 6, 8, 128), F32),
        scratch_shapes=[pltpu.VMEM((3, 512, 256), BF16), pltpu.VMEM((8 * step, 256), F32)],
        compiler_params=params(16),
        cost_estimate=cost(10**9, 8 * MIB),
        name="send",
    )(current, key, cols, mass, coriolis, start, wind)


def velocity_kernel(response, current_ref, out):
    tall = 8 * GROUP
    lane = iota((tall, 128), 1)

    def body(g, carry):
        group = pl.ds(GROUP * g, GROUP)
        base_east, base_north, a, t = (response[group, n].reshape(tall, 128) for n in range(4))
        current = [current_ref[group, c].reshape(tall, 128) for c in range(2)]
        east, north = respond(a, t, *current, lane)
        out[0, group] = (base_east + east).reshape(GROUP, 8, 128)
        out[1, group] = (base_north + north).reshape(GROUP, 8, 128)
        return carry

    lax.fori_loop(0, response.shape[0] // GROUP, body, 0)


def velocities(sent, received):
    count = sent.shape[0]
    _, grid, _, two, response, current = chunked(count)
    return pl.pallas_call(
        velocity_kernel,
        grid=(grid,),
        in_specs=[response, current],
        out_specs=two,
        out_shape=jax.ShapeDtypeStruct((2, count, 8, 128), F32),
        compiler_params=params(16),
        cost_estimate=cost(10**7, 4 * MIB),
        name="velocities",
    )(sent, received)


def invert_kernel(cols, key, inverse, hot):
    count = cols.shape[0]
    hot[...] = jnp.where(iota((512, 8 * count), 0) == key[...], 1.0, 0.0).astype(BF16)
    lane = iota((8, 1024), 1)
    weights = jnp.where(lane // 128 == iota((8, 1024), 0), lane % 128 + 1, 0).astype(F32).astype(BF16)
    place = iota((128, 128), 0)

    def body(i, carry):
        index = cols[i]
        target = jnp.where(index >= 0, (index >> 1) + 64 * (index & 1), -1)
        masks = [
            jnp.where(place == jnp.broadcast_to(target[s : s + 1], (128, 128)), 1.0, 0.0).astype(BF16)
            for s in range(8)
        ]
        found = lax.dot_general(
            weights, jnp.concatenate(masks, axis=1), (((1,), (1,)), ((), ())), preferred_element_type=F32
        )
        inverse[i] = found.astype(I32) - 1
        return carry

    lax.fori_loop(0, count, body, 0, unroll=2)


def invert(cols, key):
    count = cols.shape[0]
    return pl.pallas_call(
        invert_kernel,
        out_shape=(jax.ShapeDtypeStruct((count, 8, 128), I32), jax.ShapeDtypeStruct((512, 8 * count), BF16)),
        compiler_params=params(16),
        cost_estimate=cost(10**10, 2 * MIB),
        name="invert",
    )(cols, key)


def stress_kernel(response, current_ref, inverse, hot, planes, side, ends, parts):
    count = inverse.shape[0]
    tall = 8 * GROUP
    lane = iota((tall, 128), 1)
    chunk = pl.program_id(0)

    def body(g, carry):
        group = pl.ds(GROUP * g, GROUP)
        rows = pl.ds(pl.multiple_of(8 * count * chunk + tall * g, tall), tall)
        base_east, base_north, a, t = (response[group, n].reshape(tall, 128) for n in range(4))
        current = [current_ref[group, c].reshape(tall, 128) for c in range(2)]
        east, north = respond(a, t, *current, lane)
        index = inverse[group].reshape(tall, 128)
        inside = jnp.maximum(index, 0)
        for c, drag in enumerate((base_east + east - current[0], base_north + north - current[1])):
            drag = DRAG * drag
            got = jnp.concatenate(
                [lane_gather(drag[8 * i : 8 * i + 8], inside[8 * i : 8 * i + 8]) for i in range(GROUP)], axis=0
            )
            pieces = split3(jnp.where(index >= 0, got, 0.0))
            for part in range(3):
                parts[part, rows, 128 * c : 128 * c + 128] = pieces[part]
        return carry

    lax.fori_loop(0, count // GROUP, body, 0)

    @pl.when(chunk == pl.num_programs(0) - 1)
    def _():
        total = dot(hot[...], parts[0]) + dot(hot[...], parts[1]) + dot(hot[...], parts[2])
        lane = iota((ROWS, 128), 1)
        low = lane < 64
        top = iota((8, 128), 0) < 4
        edge = jnp.zeros((ROWS, 128), F32)
        for c in range(2):
            for py in range(2):
                for h in range(2):
                    first = 256 * h + 64 * py
                    a = total[first : first + 64, 128 * c : 128 * c + 128]
                    b = total[first + 128 : first + 192, 128 * c : 128 * c + 128]
                    even = jnp.where(low, a, pltpu.roll(b, 64, 1))
                    odd = jnp.where(low, pltpu.roll(a, 64, 1), b)
                    for px, value in ((0, even), (1, odd)):
                        plane = 2 * py + px
                        planes[c, plane, :, 128 * h : 128 * h + 128] = value
                        ends[c, plane, :, 128 * h : 128 * h + 128] = jnp.where(top, value[:8], value[56:])
                        item = 4 * c + plane
                        if h == 0:
                            moved = pltpu.roll(value, 8 * item, 1) if item else value
                            edge = jnp.where(lane // 8 == item, moved, edge)
                        else:
                            moved = pltpu.roll(value, (64 + 8 * item + 8) % 128, 1) if item != 7 else value
                            edge = jnp.where(lane // 8 == 8 + item, moved, edge)
        side[...] = edge


def stresses(sent, received, inverse, hot):
    count = inverse.shape[0]
    step, grid, one, _, response, current = chunked(count)

    def whole(shape):
        return pl.BlockSpec(shape, lambda i: (0,) * len(shape))

    shapes = ((2, 4, ROWS, COLS), (ROWS, 128), (2, 4, 8, COLS))
    return pl.pallas_call(
        stress_kernel,
        grid=(grid,),
        in_specs=[response, current, one, whole((512, 8 * count))],
        out_specs=tuple(whole(shape) for shape in shapes),
        out_shape=tuple(jax.ShapeDtypeStruct(shape, F32) for shape in shapes),
        scratch_shapes=[pltpu.VMEM((3, 8 * count, 256), BF16)],
        compiler_params=params(16),
        cost_estimate=cost(10**9, 4 * MIB),
        name="stresses",
    )(received, sent, inverse, hot)


def widen_kernel(ends, right, left, out):
    lane = iota((8, 128), 1)
    top = iota((8, 128), 0) < 4
    from_right = jnp.where(top, right[0:8], right[56:64])
    from_left = jnp.where(top, left[0:8], left[56:64])
    for c in range(2):
        for p in range(4):
            item = 4 * c + p
            r = pltpu.roll(from_right, (128 - 8 * item) % 128, 1) if item else from_right
            s = pltpu.roll(from_left, (56 - 8 * item) % 128, 1) if item != 7 else from_left
            out[c, p, :, 0:COLS] = ends[c, p]
            out[c, p, :, COLS:XCOLS] = jnp.where(lane < 64, r, s)


def widen(ends, right, left):
    return pl.pallas_call(
        widen_kernel,
        out_shape=jax.ShapeDtypeStruct((2, 4, 8, XCOLS), F32),
        compiler_params=params(4),
        cost_estimate=cost(10**5, MIB // 4),
        name="widen",
    )(ends, right, left)


ARRAYS = 11


def prepare_kernel(
    sea, forcing, weights, excess, mask, planes, left, right, ends, halves
):
    lane = iota((8, 128), 1)
    low = lane < 64
    order = jnp.where(low, 2 * lane, 2 * lane - 127)
    swapped = jnp.where(low, 2 * lane + 1, 2 * lane - 128)

    def split(t, carry):
        rows = pl.ds(pl.multiple_of(8 * t, 8), 8)
        w = [weights[k, rows, :] for k in range(8)]
        total = ((w[0] + w[1]) + (w[2] + w[3])) + ((w[4] + w[5]) + (w[6] + w[7]))
        ocean = mask[rows, :] > 0
        inverse = jnp.where(ocean, 1.0 / ((1.0 + excess[rows, :]) * total), 0.0)
        arrays = [v * inverse for v in w]
        arrays += [inverse, forcing[rows, :], jnp.where(ocean, sea[rows, :], 0.0)]
        for n, array in enumerate(arrays):
            for h in range(2):
                a = lane_gather(array[:, 256 * h : 256 * h + 128], order)
                b = lane_gather(array[:, 256 * h + 128 : 256 * h + 256], swapped)
                halves[4 * n + h, rows, :] = jnp.where(low, a, b)
                halves[4 * n + 2 + h, rows, :] = pltpu.roll(jnp.where(low, b, a), 64, 1)
        return carry

    lax.fori_loop(0, 2 * ROWS // 8, split, 0)

    def pack(t, carry):
        out_rows = pl.ds(pl.multiple_of(8 * t, 8), 8)
        for py in range(2):
            rows = pl.ds(16 * t + py, 8, stride=2)
            packed = [[jnp.zeros((8, 128), F32)] * 2, [jnp.zeros((8, 128), F32)] * 2]
            for n in range(ARRAYS):
                for px in range(2):
                    for h in range(2):
                        value = halves[4 * n + 2 * px + h, rows, :]
                        planes[n, 2 * py + px, out_rows, 128 * h : 128 * h + 128] = value
                        item = 2 * n + px
                        shift = (8 * (item % 16) + (8 if h else 0)) % 128
                        moved = pltpu.roll(value, shift, 1) if shift else value
                        packed[h][item // 16] = jnp.where(lane // 8 == item % 16, moved, packed[h][item // 16])
            for g in range(2):
                left[py, out_rows, 128 * g : 128 * g + 128] = packed[0][g]
                right[py, out_rows, 128 * g : 128 * g + 128] = packed[1][g]
        return carry

    lax.fori_loop(0, ROWS // 8, pack, 0)
    top = iota((8, 256), 0) < 4
    for n in range(ARRAYS):
        for p in range(4):
            ends[n, p] = jnp.where(top, planes[n, p, 0:8], planes[n, p, 56:64])


def prepare(sea, forcing, weights, excess, mask):
    return pl.pallas_call(
        prepare_kernel,
        out_shape=(
            jax.ShapeDtypeStruct((ARRAYS, 4, ROWS, COLS), F32),
            jax.ShapeDtypeStruct((2, ROWS, 256), F32),
            jax.ShapeDtypeStruct((2, ROWS, 256), F32),
            jax.ShapeDtypeStruct((ARRAYS, 4, 8, COLS), F32),
        ),
        scratch_shapes=[pltpu.VMEM((4 * ARRAYS, 2 * ROWS, 128), F32)],
        compiler_params=params(20),
        cost_estimate=cost(10**7, 7 * MIB),
        name="prepare",
    )(sea, forcing, weights, excess, mask)


def place_edges(n, p, right, left, rows, lane):
    item = 2 * n + p % 2
    span = slice(128 * (item // 16), 128 * (item // 16) + 128)
    slot = item % 16
    r, s = right[p // 2, rows, span], left[p // 2, rows, span]
    r = pltpu.roll(r, (128 - 8 * slot) % 128, 1) if slot else r
    s = pltpu.roll(s, (120 - 8 * slot) % 128, 1) if slot != 15 else s
    return jnp.where(lane < 8, r, jnp.where(lane >= 120, s, 0.0))


def widen_operator_kernel(ends, right, left, out):
    lane = iota((8, 128), 1)
    top = iota((8, 128), 0) < 4
    for n in range(ARRAYS):
        for p in range(4):
            out[n, p, :, 0:COLS] = ends[n, p]
            out[n, p, :, COLS:XCOLS] = jnp.where(
                top,
                place_edges(n, p, right, left, slice(0, 8), lane),
                place_edges(n, p, right, left, slice(56, 64), lane),
            )


def widen_operator(ends, right, left):
    return pl.pallas_call(
        widen_operator_kernel,
        out_shape=jax.ShapeDtypeStruct((ARRAYS, 4, 8, XCOLS), F32),
        compiler_params=params(8),
        cost_estimate=cost(10**6, 2 * MIB),
        name="widen_operator",
    )(ends, right, left)


def extend_kernel(planes, right, left, below, above, out):
    lane = iota((ROWS, 128), 1)
    top = iota((8, XCOLS), 0) < 4
    for n in range(ARRAYS):
        for p in range(4):
            out[n, p, 0:ROWS, 0:COLS] = planes[n, p]
            out[n, p, 0:ROWS, COLS:XCOLS] = place_edges(n, p, right, left, slice(0, ROWS), lane)
            out[n, p, ROWS:XROWS, :] = jnp.where(top, below[n, p], above[n, p])


def extend(*arrays):
    return pl.pallas_call(
        extend_kernel,
        out_shape=jax.ShapeDtypeStruct((ARRAYS, 4, XROWS, XCOLS), F32),
        compiler_params=params(20),
        cost_estimate=cost(10**7, 8 * MIB),
        name="extend",
    )(*arrays)


def row_shift(value, step):
    return pltpu.roll(value, (-step) % XROWS, 0) if step else value


def col_shift(value, step):
    return pltpu.roll(value, (-step) % XCOLS, 1) if step else value


def neighbour(step, parity):
    return (step + parity) // 2


def sweep_kernel(operator, stress, right, left, below, above, out, wide, source, field, natural):
    lane = iota((ROWS, 128), 1)
    top = iota((8, XCOLS), 0) < 4
    for c in range(2):
        for p in range(4):
            item = 4 * c + p
            r = pltpu.roll(right[...], (128 - 8 * item) % 128, 1) if item else right[...]
            s = pltpu.roll(left[...], (56 - 8 * item) % 128, 1) if item != 7 else left[...]
            wide[c, p, 0:ROWS, 0:COLS] = stress[c, p]
            wide[c, p, 0:ROWS, COLS:XCOLS] = jnp.where(lane < 64, r, s)
            wide[c, p, ROWS:XROWS, :] = jnp.where(top, below[c, p], above[c, p])
    for p in range(4):
        py, px = p // 2, p % 2
        north = wide[1, 2 * py + 1 - px]
        east = wide[0, 2 * (1 - py) + px]
        zonal = col_shift(north, neighbour(1, px)) - col_shift(north, neighbour(-1, px))
        meridional = row_shift(east, neighbour(1, py)) - row_shift(east, neighbour(-1, py))
        source[p] = (operator[9, p] + zonal - meridional) * operator[8, p]
        field[p] = operator[10, p]
    for colour in COLOURS:
        py, px = colour // 2, colour % 2
        value = source[colour]
        for k, (dy, dx) in enumerate(STEPS):
            plane = 2 * (py ^ (dy & 1)) + (px ^ (dx & 1))
            v = field[plane]
            if dy:
                v = row_shift(v, neighbour(dy, py))
            if dx:
                v = col_shift(v, neighbour(dx, px))
            value = value + operator[k, colour] * v
        field[colour] = value
    lane = iota((ROWS, 128), 1)
    even_lane = lane % 2 == 0
    first = lane // 2
    for py in range(2):
        for h in range(2):
            even = field[2 * py, 0:ROWS, 128 * h : 128 * h + 128]
            odd = field[2 * py + 1, 0:ROWS, 128 * h : 128 * h + 128]
            for b in range(2):
                for t in range(ROWS // 8):
                    index = first[:8] + 64 * b
                    e = lane_gather(even[8 * t : 8 * t + 8], index)
                    o = lane_gather(odd[8 * t : 8 * t + 8], index)
                    natural[2 * h + b, pl.ds(16 * t + py, 8, stride=2), :] = jnp.where(even_lane[:8], e, o)
    for k in range(4):
        out[:, 128 * k : 128 * k + 128] = natural[k]


def sweep(*arrays):
    return pl.pallas_call(
        sweep_kernel,
        out_shape=jax.ShapeDtypeStruct((128, 512), F32),
        scratch_shapes=[
            pltpu.VMEM((2, 4, XROWS, XCOLS), F32),
            pltpu.VMEM((4, XROWS, XCOLS), F32),
            pltpu.VMEM((4, XROWS, XCOLS), F32),
            pltpu.VMEM((4, 128, 128), F32),
        ],
        compiler_params=params(20),
        cost_estimate=cost(10**8, 6 * MIB),
        name="sweep",
    )(*arrays)


AXES = ("zon", "mer")


def exchange(values):
    return lax.all_to_all(values, AXES, split_axis=0, concat_axis=0, tiled=True)


def from_neighbour(values, dz, dm):
    nz, nm = lax.axis_size("zon"), lax.axis_size("mer")
    pairs = [
        (((z + dz) % nz) * nm + m + dm, z * nm + m)
        for z in range(nz)
        for m in range(nm)
        if 0 <= m + dm < nm
    ]
    return lax.ppermute(values, AXES, pairs)


def local(
    sea_level,
    forcing,
    link_weights,
    excess,
    ocean_mask,
    current,
    intersection_block,
    intersection_cols,
    ice_mass,
    coriolis,
    ice_start,
    wind_stress,
):
    blocks = intersection_block[0]
    cols = intersection_cols[0]
    slots = blocks.size
    row, part = blocks >> 2, blocks & 3
    fetch_key = jnp.where(blocks >= 0, part * 128 + row, -1).reshape(slots, 1)
    scatter_key = jnp.where(blocks >= 0, part * 128 + (row & 1) * 64 + (row >> 1), -1).reshape(1, slots)

    sent = send(current, fetch_key, cols, ice_mass[0], coriolis[0], ice_start[:, 0], wind_stress[:, 0])
    received = exchange(sent)
    planes, left_edge, right_edge, ends = prepare(sea_level, forcing, link_weights, excess, ocean_mask)
    right, left = from_neighbour(left_edge, 1, 0), from_neighbour(right_edge, -1, 0)
    rows = widen_operator(ends, right, left)
    operator = extend(planes, right, left, from_neighbour(rows, 0, 1), from_neighbour(rows, 0, -1))
    inverse, hot = invert(cols, scatter_key)
    inverse, operator = lax.optimization_barrier((inverse, operator))
    stress, side, ends = stresses(sent, received, inverse, hot)
    received, side = lax.optimization_barrier((received, side))
    right, left = from_neighbour(side, 1, 0), from_neighbour(side, -1, 0)
    rows = widen(ends, right, left)
    surface = sweep(operator, stress, right, left, from_neighbour(rows, 0, 1), from_neighbour(rows, 0, -1))
    velocity = velocities(sent, received)
    return surface, velocity[:, None]


def solution(mesh):
    return jax.shard_map(
        local,
        mesh=mesh,
        in_specs=(
            P("mer", "zon"),
            P("mer", "zon"),
            P(None, "mer", "zon"),
            P("mer", "zon"),
            P("mer", "zon"),
            P(None, "mer", "zon"),
            P(("zon", "mer"), None, None),
            P(("zon", "mer"), None, None, None),
            P(("zon", "mer"), None, None, None),
            P(("zon", "mer"), None, None, None),
            P(None, ("zon", "mer"), None, None, None),
            P(None, ("zon", "mer"), None, None, None),
        ),
        out_specs=(P("mer", "zon"), P(None, ("zon", "mer"), None, None, None)),
        check_vma=False,
    )
```

```python
import jax
import jax.numpy as jnp
from jax import lax
from jax.experimental import pallas as pl
from jax.experimental.pallas import tpu as pltpu
from jax.sharding import PartitionSpec as P

SWEEPS = 2
ICE_SWEEPS = 3
DRAG = 1.0
LINK = 0.5
STEPS = ((0, 1), (0, -1), (1, 0), (-1, 0), (1, 1), (1, -1), (-1, 1), (-1, -1))
COLOURS = (0,) + (1, 2, 3, 2, 1, 0) * SWEEPS
F32, BF16, I32 = jnp.float32, jnp.bfloat16, jnp.int32
MIB = 1 << 20
ROWS, COLS, XROWS, XCOLS = 64, 256, 72, 384


def params(vmem=48):
    return pltpu.CompilerParams(vmem_limit_bytes=vmem * MIB)


def cost(flops, moved):
    return pl.CostEstimate(flops=flops, bytes_accessed=moved, transcendentals=0)


def iota(shape, dim):
    return lax.broadcasted_iota(I32, shape, dim)


def lane_gather(values, index):
    return jnp.take_along_axis(values, index, axis=1, mode="promise_in_bounds")


def split3(values):
    high = values.astype(BF16)
    rest = values - high.astype(F32)
    middle = rest.astype(BF16)
    low = (rest - middle.astype(F32)).astype(BF16)
    return high, middle, low


def dot(a, b):
    return jnp.dot(a, b, preferred_element_type=F32)


def beside(values, lane):
    before = jnp.where(lane == 0, 0.0, pltpu.roll(values, 1, 1))
    after = jnp.where(lane == 127, 0.0, pltpu.roll(values, 127, 1))
    return LINK * (before + after)


def turn(a, t, east, north):
    return a * east + t * north, a * north - t * east


def sweep_ice(a, t, east, north, base_east, base_north, lane):
    return turn(a, t, base_east + beside(east, lane), base_north + beside(north, lane))


def respond(a, t, current_east, current_north, lane):
    east, north = turn(a, t, current_east, current_north)
    for _ in range(ICE_SWEEPS - 1):
        east, north = sweep_ice(a, t, east, north, current_east, current_north, lane)
    return east, north


GROUP = 16


def send_kernel(current, key, cols, mass_ref, coriolis_ref, start_ref, wind_ref, out, own, table, rows):
    count = cols.shape[0]

    @pl.when(pl.program_id(0) == 0)
    def _():
        for c in range(2):
            for k in range(4):
                parts = split3(current[c, :, 128 * k : 128 * k + 128])
                for part in range(3):
                    table[part, 128 * k : 128 * k + 128, 128 * c : 128 * c + 128] = parts[part]

    hot = jnp.where(key[...] == iota((8 * count, 512), 1), 1.0, 0.0).astype(BF16)
    rows[...] = dot(hot, table[0]) + dot(hot, table[1]) + dot(hot, table[2])
    tall = 8 * GROUP
    lane = iota((tall, 128), 1)

    def body(g, carry):
        group = pl.ds(GROUP * g, GROUP)
        tile = rows[pl.ds(pl.multiple_of(tall * g, tall), tall)]
        index = cols[group].reshape(tall, 128)
        inside = jnp.maximum(index, 0)
        for c in range(2):
            got = jnp.concatenate(
                [lane_gather(tile[8 * i : 8 * i + 8, 128 * c : 128 * c + 128], inside[8 * i : 8 * i + 8]) for i in range(GROUP)],
                axis=0,
            )
            got = jnp.where(index >= 0, DRAG * got, 0.0).reshape(GROUP, 8, 128)
            out[group, 4 + c] = got
            own[group, c] = got
        mass = mass_ref[group].reshape(tall, 128)
        a = mass + DRAG + 2.0 * LINK
        t = coriolis_ref[group].reshape(tall, 128) * mass
        inverse = 1.0 / (a * a + t * t)
        a = a * inverse
        t = t * inverse
        east = start_ref[0, group].reshape(tall, 128)
        north = start_ref[1, group].reshape(tall, 128)
        base_east = mass * east + wind_ref[0, group].reshape(tall, 128)
        base_north = mass * north + wind_ref[1, group].reshape(tall, 128)
        for _ in range(ICE_SWEEPS):
            east, north = sweep_ice(a, t, east, north, base_east, base_north, lane)
        for n, value in enumerate((east, north, a, t)):
            out[group, n] = value.reshape(GROUP, 8, 128)
        return carry

    lax.fori_loop(0, count // GROUP, body, 0)


def chunked(count):
    step = min(count, 64)
    one = pl.BlockSpec((step, 8, 128), lambda i: (i, 0, 0))
    two = pl.BlockSpec((2, step, 8, 128), lambda i: (0, i, 0, 0))
    response = pl.BlockSpec((step, 4, 8, 128), lambda i: (i, 0, 0, 0))
    current = pl.BlockSpec((step, 2, 8, 128), lambda i: (i, 2, 0, 0))
    return step, count // step, one, two, response, current


def send(current, key, cols, mass, coriolis, start, wind):
    count = cols.shape[0]
    step, grid, one, two, _, _ = chunked(count)
    return pl.pallas_call(
        send_kernel,
        grid=(grid,),
        in_specs=[
            pl.BlockSpec((2, 128, 512), lambda i: (0, 0, 0)),
            pl.BlockSpec((8 * step, 1), lambda i: (i, 0)),
            one,
            one,
            one,
            two,
            two,
        ],
        out_specs=(
            pl.BlockSpec((step, 6, 8, 128), lambda i: (i, 0, 0, 0)),
            pl.BlockSpec((step, 2, 8, 128), lambda i: (i, 0, 0, 0)),
        ),
        out_shape=(
            jax.ShapeDtypeStruct((count, 6, 8, 128), F32),
            jax.ShapeDtypeStruct((count, 2, 8, 128), F32),
        ),
        scratch_shapes=[pltpu.VMEM((3, 512, 256), BF16), pltpu.VMEM((8 * step, 256), F32)],
        compiler_params=params(60),
        cost_estimate=cost(10**9, 8 * MIB),
        name="send",
    )(current, key, cols, mass, coriolis, start, wind)


def velocity_kernel(response, current_ref, _, out, done):
    done[...] = jnp.zeros((8, 128), F32)
    tall = 8 * GROUP
    lane = iota((tall, 128), 1)

    def body(g, carry):
        group = pl.ds(GROUP * g, GROUP)
        base_east, base_north, a, t = (response[group, n].reshape(tall, 128) for n in range(4))
        current = [current_ref[group, c].reshape(tall, 128) for c in range(2)]
        east, north = respond(a, t, *current, lane)
        out[0, group] = (base_east + east).reshape(GROUP, 8, 128)
        out[1, group] = (base_north + north).reshape(GROUP, 8, 128)
        return carry

    lax.fori_loop(0, response.shape[0] // GROUP, body, 0)


ORDER = pl.BlockSpec(memory_space=pl.ANY)


def velocities(sent, received, after):
    count = sent.shape[0]
    _, grid, _, two, response, current = chunked(count)
    return pl.pallas_call(
        velocity_kernel,
        grid=(grid,),
        in_specs=[response, current, ORDER],
        out_specs=(two, pl.BlockSpec((8, 128), lambda i: (0, 0))),
        out_shape=(jax.ShapeDtypeStruct((2, count, 8, 128), F32), jax.ShapeDtypeStruct((8, 128), F32)),
        compiler_params=params(60),
        cost_estimate=cost(10**7, 4 * MIB),
        name="velocities",
    )(sent, received, after)


def invert_kernel(cols, key, inverse, hot):
    count = cols.shape[0]
    hot[...] = jnp.where(iota((512, 8 * count), 0) == key[...], 1.0, 0.0).astype(BF16)
    lane = iota((8, 1024), 1)
    weights = jnp.where(lane // 128 == iota((8, 1024), 0), lane % 128 + 1, 0).astype(F32).astype(BF16)
    place = iota((128, 128), 0)

    def body(i, carry):
        index = cols[i]
        target = jnp.where(index >= 0, (index >> 1) + 64 * (index & 1), -1)
        masks = [
            jnp.where(place == jnp.broadcast_to(target[s : s + 1], (128, 128)), 1.0, 0.0).astype(BF16)
            for s in range(8)
        ]
        found = lax.dot_general(
            weights, jnp.concatenate(masks, axis=1), (((1,), (1,)), ((), ())), preferred_element_type=F32
        )
        inverse[i] = found.astype(I32) - 1
        return carry

    lax.fori_loop(0, count, body, 0, unroll=2)


def invert(cols, key):
    count = cols.shape[0]
    return pl.pallas_call(
        invert_kernel,
        out_shape=(jax.ShapeDtypeStruct((count, 8, 128), I32), jax.ShapeDtypeStruct((512, 8 * count), BF16)),
        compiler_params=params(60),
        cost_estimate=cost(10**10, 2 * MIB),
        name="invert",
    )(cols, key)


def stress_kernel(response_in, own_in, inverse_in, hot_in, *refs):
    planes, side, ends, parts, response, current_ref, inverse, hot, arrived, listed = refs[-10:]
    groups = inverse.shape[0] // GROUP

    def transfer(g):
        group = pl.ds(GROUP * g, GROUP)
        return (
            pltpu.make_async_copy(response_in.at[group, pl.ds(0, 4)], response.at[group], arrived.at[0, g]),
            pltpu.make_async_copy(own_in.at[group], current_ref.at[group], arrived.at[1, g]),
        )

    inverse_copy = pltpu.make_async_copy(inverse_in, inverse, listed.at[0])
    hot_copy = pltpu.make_async_copy(hot_in, hot, listed.at[1])
    for g in range(groups):
        for copy in transfer(g):
            copy.start()
        if g == 0:
            inverse_copy.start()
    hot_copy.start()
    inverse_copy.wait()
    tall = 8 * GROUP
    lane = iota((tall, 128), 1)

    def body(g, carry):
        for copy in transfer(g):
            copy.wait()
        group = pl.ds(GROUP * g, GROUP)
        rows = pl.ds(pl.multiple_of(tall * g, tall), tall)
        base_east, base_north, a, t = (response[group, n].reshape(tall, 128) for n in range(4))
        current = [current_ref[group, c].reshape(tall, 128) for c in range(2)]
        east, north = respond(a, t, *current, lane)
        index = inverse[group].reshape(tall, 128)
        inside = jnp.maximum(index, 0)
        for c, drag in enumerate((base_east + east - current[0], base_north + north - current[1])):
            drag = DRAG * drag
            got = jnp.concatenate(
                [lane_gather(drag[8 * i : 8 * i + 8], inside[8 * i : 8 * i + 8]) for i in range(GROUP)], axis=0
            )
            pieces = split3(jnp.where(index >= 0, got, 0.0))
            for part in range(3):
                parts[part, rows, 128 * c : 128 * c + 128] = pieces[part]
        return carry

    lax.fori_loop(0, groups, body, 0)
    hot_copy.wait()
    total = dot(hot[...], parts[0]) + dot(hot[...], parts[1]) + dot(hot[...], parts[2])
    lane = iota((ROWS, 128), 1)
    low = lane < 64
    top = iota((8, 128), 0) < 4
    edge = jnp.zeros((ROWS, 128), F32)
    for c in range(2):
        for py in range(2):
            for h in range(2):
                first = 256 * h + 64 * py
                a = total[first : first + 64, 128 * c : 128 * c + 128]
                b = total[first + 128 : first + 192, 128 * c : 128 * c + 128]
                even = jnp.where(low, a, pltpu.roll(b, 64, 1))
                odd = jnp.where(low, pltpu.roll(a, 64, 1), b)
                for px, value in ((0, even), (1, odd)):
                    plane = 2 * py + px
                    planes[c, plane, :, 128 * h : 128 * h + 128] = value
                    ends[c, plane, :, 128 * h : 128 * h + 128] = jnp.where(top, value[:8], value[56:])
                    item = 4 * c + plane
                    if h == 0:
                        moved = pltpu.roll(value, 8 * item, 1) if item else value
                        edge = jnp.where(lane // 8 == item, moved, edge)
                    else:
                        moved = pltpu.roll(value, (64 + 8 * item + 8) % 128, 1) if item != 7 else value
                        edge = jnp.where(lane // 8 == 8 + item, moved, edge)
    side[...] = edge


def stresses(received, own, inverse, hot, after):
    count = inverse.shape[0]
    inside = pl.BlockSpec(memory_space=pltpu.VMEM)
    shapes = ((2, 4, ROWS, COLS), (ROWS, 128), (2, 4, 8, COLS))
    return pl.pallas_call(
        stress_kernel,
        in_specs=[ORDER] * (4 + len(after)),
        out_specs=(inside,) * 3,
        out_shape=tuple(jax.ShapeDtypeStruct(shape, F32) for shape in shapes),
        scratch_shapes=[
            pltpu.VMEM((3, 8 * count, 256), BF16),
            pltpu.VMEM((count, 4, 8, 128), F32),
            pltpu.VMEM((count, 2, 8, 128), F32),
            pltpu.VMEM((count, 8, 128), I32),
            pltpu.VMEM((512, 8 * count), BF16),
            pltpu.SemaphoreType.DMA((2, count // GROUP)),
            pltpu.SemaphoreType.DMA((2,)),
        ],
        compiler_params=params(60),
        cost_estimate=cost(10**9, 4 * MIB),
        name="stresses",
    )(received, own, inverse, hot, *after)


def widen_kernel(ends, right, left, far_right, far_left, _, out):
    lane = iota((8, 128), 1)
    top = iota((8, 128), 0) < 4
    from_right = jnp.where(top, right[0:8], right[56:64])
    from_left = jnp.where(top, left[0:8], left[56:64])
    for c in range(2):
        for p in range(4):
            item = 4 * c + p
            r = pltpu.roll(from_right, (128 - 8 * item) % 128, 1) if item else from_right
            s = pltpu.roll(from_left, (56 - 8 * item) % 128, 1) if item != 7 else from_left
            out[item, :, 0:COLS] = ends[c, p]
            out[item, :, COLS:XCOLS] = jnp.where(lane < 64, r, s)
    for py in range(2):
        for g in range(2):
            for n, edge in enumerate((far_right, far_left)):
                span = slice(128 * g, 128 * g + 128)
                out[8 + 2 * py + n, :, span] = jnp.where(top, edge[py, 0:8, span], edge[py, 56:64, span])
            out[8 + 2 * py + g, :, COLS:XCOLS] = jnp.zeros((8, 128), F32)


def widen(ends, right, left, far_right, far_left, after):
    inside = pl.BlockSpec(memory_space=pltpu.VMEM)
    return pl.pallas_call(
        widen_kernel,
        in_specs=[inside] * 5 + [ORDER],
        out_shape=jax.ShapeDtypeStruct((12, 8, XCOLS), F32),
        compiler_params=params(4),
        cost_estimate=cost(10**5, MIB // 4),
        name="widen",
    )(ends, right, left, far_right, far_left, after)


ARRAYS = 11


def prepare_kernel(
    sea, forcing, weights, excess, mask, planes, left, right, ends, halves
):
    lane = iota((8, 128), 1)
    low = lane < 64
    order = jnp.where(low, 2 * lane, 2 * lane - 127)
    swapped = jnp.where(low, 2 * lane + 1, 2 * lane - 128)

    def split(t, carry):
        rows = pl.ds(pl.multiple_of(8 * t, 8), 8)
        w = [weights[k, rows, :] for k in range(8)]
        total = ((w[0] + w[1]) + (w[2] + w[3])) + ((w[4] + w[5]) + (w[6] + w[7]))
        ocean = mask[rows, :] > 0
        inverse = jnp.where(ocean, 1.0 / ((1.0 + excess[rows, :]) * total), 0.0)
        arrays = [v * inverse for v in w]
        arrays += [inverse, forcing[rows, :], jnp.where(ocean, sea[rows, :], 0.0)]
        for n, array in enumerate(arrays):
            for h in range(2):
                a = lane_gather(array[:, 256 * h : 256 * h + 128], order)
                b = lane_gather(array[:, 256 * h + 128 : 256 * h + 256], swapped)
                halves[4 * n + h, rows, :] = jnp.where(low, a, b)
                halves[4 * n + 2 + h, rows, :] = pltpu.roll(jnp.where(low, b, a), 64, 1)
        return carry

    lax.fori_loop(0, 2 * ROWS // 8, split, 0)

    def pack(t, carry):
        out_rows = pl.ds(pl.multiple_of(8 * t, 8), 8)
        for py in range(2):
            rows = pl.ds(16 * t + py, 8, stride=2)
            packed = [[jnp.zeros((8, 128), F32)] * 2, [jnp.zeros((8, 128), F32)] * 2]
            for n in range(ARRAYS):
                for px in range(2):
                    for h in range(2):
                        value = halves[4 * n + 2 * px + h, rows, :]
                        planes[n, 2 * py + px, out_rows, 128 * h : 128 * h + 128] = value
                        item = 2 * n + px
                        shift = (8 * (item % 16) + (8 if h else 0)) % 128
                        moved = pltpu.roll(value, shift, 1) if shift else value
                        packed[h][item // 16] = jnp.where(lane // 8 == item % 16, moved, packed[h][item // 16])
            for g in range(2):
                left[py, out_rows, 128 * g : 128 * g + 128] = packed[0][g]
                right[py, out_rows, 128 * g : 128 * g + 128] = packed[1][g]
        return carry

    lax.fori_loop(0, ROWS // 8, pack, 0)
    top = iota((8, 256), 0) < 4
    for n in range(ARRAYS):
        for p in range(4):
            ends[n, p] = jnp.where(top, planes[n, p, 0:8], planes[n, p, 56:64])


def prepare(sea, forcing, weights, excess, mask):
    return pl.pallas_call(
        prepare_kernel,
        out_shape=(
            jax.ShapeDtypeStruct((ARRAYS, 4, ROWS, COLS), F32),
            jax.ShapeDtypeStruct((2, ROWS, 256), F32),
            jax.ShapeDtypeStruct((2, ROWS, 256), F32),
            jax.ShapeDtypeStruct((ARRAYS, 4, 8, COLS), F32),
        ),
        scratch_shapes=[pltpu.VMEM((4 * ARRAYS, 2 * ROWS, 128), F32)],
        compiler_params=params(60),
        cost_estimate=cost(10**7, 7 * MIB),
        name="prepare",
    )(sea, forcing, weights, excess, mask)


def place_edges(n, p, right, left, lane):
    slot = (2 * n + p % 2) % 16
    r = pltpu.roll(right, (128 - 8 * slot) % 128, 1) if slot else right
    s = pltpu.roll(left, (120 - 8 * slot) % 128, 1) if slot != 15 else left
    return jnp.where(lane < 8, r, jnp.where(lane >= 120, s, 0.0))


def packed_at(n, p):
    group = (2 * n + p % 2) // 16
    return slice(128 * group, 128 * group + 128)


def extend_kernel(planes, right, left, _, out):
    lane = iota((ROWS, 128), 1)
    for n in range(ARRAYS):
        for p in range(4):
            span = packed_at(n, p)
            out[n, p, :, 0:COLS] = planes[n, p]
            out[n, p, :, COLS:XCOLS] = place_edges(n, p, right[p // 2, :, span], left[p // 2, :, span], lane)


def extend(planes, right, left, after):
    inside = pl.BlockSpec(memory_space=pltpu.VMEM)
    return pl.pallas_call(
        extend_kernel,
        in_specs=[inside] * 3 + [ORDER],
        out_shape=jax.ShapeDtypeStruct((ARRAYS, 4, ROWS, XCOLS), F32),
        compiler_params=params(20),
        cost_estimate=cost(10**7, 8 * MIB),
        name="extend",
    )(planes, right, left, after)


def row_shift(value, step):
    return pltpu.roll(value, (-step) % XROWS, 0) if step else value


def col_shift(value, step):
    return pltpu.roll(value, (-step) % XCOLS, 1) if step else value


def neighbour(step, parity):
    return (step + parity) // 2


def sweep_kernel(
    operator, far_below, far_above, stress, right, left, below, above, out, wide, source, field, natural, rim
):
    lane = iota((ROWS, 128), 1)
    top = iota((8, XCOLS), 0) < 4
    for c in range(2):
        for p in range(4):
            item = 4 * c + p
            r = pltpu.roll(right[...], (128 - 8 * item) % 128, 1) if item else right[...]
            s = pltpu.roll(left[...], (56 - 8 * item) % 128, 1) if item != 7 else left[...]
            wide[c, p, 0:ROWS, 0:COLS] = stress[c, p]
            wide[c, p, 0:ROWS, COLS:XCOLS] = jnp.where(lane < 64, r, s)
            wide[c, p, ROWS:XROWS, :] = jnp.where(top, below[item], above[item])
    corners = [jnp.where(top, below[8 + n], above[8 + n]) for n in range(4)]
    for n in range(ARRAYS):
        for p in range(4):
            span = packed_at(n, p)
            far_right, far_left = corners[2 * (p // 2)], corners[2 * (p // 2) + 1]
            rim[n, p, :, 0:COLS] = jnp.where(top[:, :COLS], far_below[n, p], far_above[n, p])
            rim[n, p, :, COLS:XCOLS] = place_edges(n, p, far_right[:, span], far_left[:, span], lane[:8])

    def entry(n, p):
        return jnp.concatenate([operator[n, p], rim[n, p]], axis=0)

    for p in range(4):
        py, px = p // 2, p % 2
        north = wide[1, 2 * py + 1 - px]
        east = wide[0, 2 * (1 - py) + px]
        zonal = col_shift(north, neighbour(1, px)) - col_shift(north, neighbour(-1, px))
        meridional = row_shift(east, neighbour(1, py)) - row_shift(east, neighbour(-1, py))
        source[p] = (entry(9, p) + zonal - meridional) * entry(8, p)
        field[p] = entry(10, p)
    for colour in COLOURS:
        py, px = colour // 2, colour % 2
        value = source[colour]
        for k, (dy, dx) in enumerate(STEPS):
            plane = 2 * (py ^ (dy & 1)) + (px ^ (dx & 1))
            v = field[plane]
            if dy:
                v = row_shift(v, neighbour(dy, py))
            if dx:
                v = col_shift(v, neighbour(dx, px))
            value = value + entry(k, colour) * v
        field[colour] = value
    lane = iota((ROWS, 128), 1)
    even_lane = lane % 2 == 0
    first = lane // 2
    for py in range(2):
        for h in range(2):
            even = field[2 * py, 0:ROWS, 128 * h : 128 * h + 128]
            odd = field[2 * py + 1, 0:ROWS, 128 * h : 128 * h + 128]
            for b in range(2):
                for t in range(ROWS // 8):
                    index = first[:8] + 64 * b
                    e = lane_gather(even[8 * t : 8 * t + 8], index)
                    o = lane_gather(odd[8 * t : 8 * t + 8], index)
                    natural[2 * h + b, pl.ds(16 * t + py, 8, stride=2), :] = jnp.where(even_lane[:8], e, o)
    for k in range(4):
        out[:, 128 * k : 128 * k + 128] = natural[k]


def sweep(*arrays):
    return pl.pallas_call(
        sweep_kernel,
        out_shape=jax.ShapeDtypeStruct((128, 512), F32),
        scratch_shapes=[
            pltpu.VMEM((2, 4, XROWS, XCOLS), F32),
            pltpu.VMEM((4, XROWS, XCOLS), F32),
            pltpu.VMEM((4, XROWS, XCOLS), F32),
            pltpu.VMEM((4, 128, 128), F32),
            pltpu.VMEM((ARRAYS, 4, 8, XCOLS), F32),
        ],
        compiler_params=params(20),
        cost_estimate=cost(10**8, 6 * MIB),
        name="sweep",
    )(*arrays)


AXES = ("zon", "mer")


def exchange(values):
    return lax.all_to_all(values, AXES, split_axis=0, concat_axis=0, tiled=True)


def from_neighbour(values, dz, dm):
    nz, nm = lax.axis_size("zon"), lax.axis_size("mer")
    pairs = [
        (((z + dz) % nz) * nm + m + dm, z * nm + m)
        for z in range(nz)
        for m in range(nm)
        if 0 <= m + dm < nm
    ]
    return lax.ppermute(values, AXES, pairs)


def local(
    sea_level,
    forcing,
    link_weights,
    excess,
    ocean_mask,
    current,
    intersection_block,
    intersection_cols,
    ice_mass,
    coriolis,
    ice_start,
    wind_stress,
):
    blocks = intersection_block[0]
    cols = intersection_cols[0]
    slots = blocks.size
    row, part = blocks >> 2, blocks & 3
    fetch_key = jnp.where(blocks >= 0, part * 128 + row, -1).reshape(slots, 1)
    scatter_key = jnp.where(blocks >= 0, part * 128 + (row & 1) * 64 + (row >> 1), -1).reshape(1, slots)

    sent, own = send(current, fetch_key, cols, ice_mass[0], coriolis[0], ice_start[:, 0], wind_stress[:, 0])
    received = exchange(sent)
    planes, left_edge, right_edge, ends = prepare(sea_level, forcing, link_weights, excess, ocean_mask)
    far_right, far_left = from_neighbour(left_edge, 1, 0), from_neighbour(right_edge, -1, 0)
    far_below, far_above = from_neighbour(ends, 0, 1), from_neighbour(ends, 0, -1)
    inverse, hot = invert(cols, scatter_key)
    stress, side, ends = stresses(received, own, inverse, hot, (far_right, far_left, far_below, far_above))
    right, left = from_neighbour(side, 1, 0), from_neighbour(side, -1, 0)
    velocity, done = velocities(sent, received, side)
    rows = widen(ends, right, left, far_right, far_left, done)
    operator = extend(planes, far_right, far_left, rows)
    below, above = from_neighbour(rows, 0, 1), from_neighbour(rows, 0, -1)
    surface = sweep(operator, far_below, far_above, stress, right, left, below, above)
    return surface, velocity[:, None]


def solution(mesh):
    return jax.shard_map(
        local,
        mesh=mesh,
        in_specs=(
            P("mer", "zon"),
            P("mer", "zon"),
            P(None, "mer", "zon"),
            P("mer", "zon"),
            P("mer", "zon"),
            P(None, "mer", "zon"),
            P(("zon", "mer"), None, None),
            P(("zon", "mer"), None, None, None),
            P(("zon", "mer"), None, None, None),
            P(("zon", "mer"), None, None, None),
            P(None, ("zon", "mer"), None, None, None),
            P(None, ("zon", "mer"), None, None, None),
        ),
        out_specs=(P("mer", "zon"), P(None, ("zon", "mer"), None, None, None)),
        check_vma=False,
    )
```

```python
import jax
import jax.numpy as jnp
from jax import lax
from jax.experimental import pallas as pl
from jax.experimental.pallas import tpu as pltpu
from jax.sharding import PartitionSpec as P

SWEEPS = 2
ICE_SWEEPS = 3
DRAG = 1.0
LINK = 0.5
STEPS = ((0, 1), (0, -1), (1, 0), (-1, 0), (1, 1), (1, -1), (-1, 1), (-1, -1))
COLOURS = (0,) + (1, 2, 3, 2, 1, 0) * SWEEPS
F32, BF16, I32 = jnp.float32, jnp.bfloat16, jnp.int32
MIB = 1 << 20
ROWS, COLS, XROWS, XCOLS = 64, 256, 72, 384


def params(vmem=48):
    return pltpu.CompilerParams(vmem_limit_bytes=vmem * MIB)


def cost(flops, moved):
    return pl.CostEstimate(flops=flops, bytes_accessed=moved, transcendentals=0)


def iota(shape, dim):
    return lax.broadcasted_iota(I32, shape, dim)


def lane_gather(values, index):
    return jnp.take_along_axis(values, index, axis=1, mode="promise_in_bounds")


def split3(values):
    high = values.astype(BF16)
    rest = values - high.astype(F32)
    middle = rest.astype(BF16)
    low = (rest - middle.astype(F32)).astype(BF16)
    return high, middle, low


def dot(a, b):
    return jnp.dot(a, b, preferred_element_type=F32)


def beside(values, lane):
    before = jnp.where(lane == 0, 0.0, pltpu.roll(values, 1, 1))
    after = jnp.where(lane == 127, 0.0, pltpu.roll(values, 127, 1))
    return LINK * (before + after)


def turn(a, t, east, north):
    return a * east + t * north, a * north - t * east


def sweep_ice(a, t, east, north, base_east, base_north, lane):
    return turn(a, t, base_east + beside(east, lane), base_north + beside(north, lane))


def respond(a, t, current_east, current_north, lane):
    east, north = turn(a, t, current_east, current_north)
    for _ in range(ICE_SWEEPS - 1):
        east, north = sweep_ice(a, t, east, north, current_east, current_north, lane)
    return east, north


PIECE = 32


def send_kernel(current_in, blocks, *refs):
    ice_in, sent, (current, table, rows, hot), ice, out, (first, arrived, gone) = (
        refs[:5],
        refs[5],
        refs[6:10],
        refs[10:15],
        refs[15],
        refs[16:],
    )
    count = out.shape[0]
    piece = min(count, PIECE)
    current_copy = pltpu.make_async_copy(current_in, current, first.at[0])
    current_copy.start()

    def arrive(p):
        span = pl.ds(piece * p, piece)
        return [
            pltpu.make_async_copy(source.at[span], target.at[span], arrived.at[n, p])
            if n < 3
            else pltpu.make_async_copy(source.at[:, span], target.at[:, span], arrived.at[n, p])
            for n, (source, target) in enumerate(zip(ice_in, ice))
        ]

    def leave(p):
        span = pl.ds(piece * p, piece)
        return pltpu.make_async_copy(out.at[span], sent.at[span], gone.at[p])

    for p in range(count // piece):
        for copy in arrive(p):
            copy.start()

    key = jnp.where(blocks[...] >= 0, (blocks[...] & 3) * 128 + (blocks[...] >> 2), -1)
    key = jnp.transpose(jnp.concatenate([key, jnp.zeros((120, 128), I32)], axis=0))
    place = iota((128, 512), 1)
    for s in range(8):
        hot[128 * s : 128 * s + 128] = jnp.where(key[:, s : s + 1] == place, 1.0, 0.0).astype(BF16)
    current_copy.wait()
    for c in range(2):
        for k in range(4):
            parts = split3(current[c, :, 128 * k : 128 * k + 128])
            for part in range(3):
                table[part, 128 * k : 128 * k + 128, 128 * c : 128 * c + 128] = parts[part]
    for q in range(4):
        span = slice(256 * q, 256 * q + 256)
        got = dot(hot[span], table[0]) + dot(hot[span], table[1]) + dot(hot[span], table[2])
        rows[0, span] = got[:, :128]
        rows[1, span] = got[:, 128:]

    tall = 8 * piece
    lane = iota((tall, 128), 1)
    cols, mass_ref, coriolis_ref, start_ref, wind_ref = ice

    def body(g):
        group = pl.ds(piece * g, piece)
        index = cols[group].reshape(tall, 128)
        inside = jnp.maximum(index, 0)
        for c in range(2):
            got = jnp.concatenate(
                [
                    lane_gather(rows[c, pl.ds(piece * g + i, 8, stride=128), :], inside[8 * i : 8 * i + 8])
                    for i in range(piece)
                ],
                axis=0,
            )
            out[group, 4 + c] = jnp.where(index >= 0, DRAG * got, 0.0).reshape(piece, 8, 128)
        mass = mass_ref[group].reshape(tall, 128)
        a = mass + DRAG + 2.0 * LINK
        t = coriolis_ref[group].reshape(tall, 128) * mass
        inverse = 1.0 / (a * a + t * t)
        a = a * inverse
        t = t * inverse
        east = start_ref[0, group].reshape(tall, 128)
        north = start_ref[1, group].reshape(tall, 128)
        base_east = mass * east + wind_ref[0, group].reshape(tall, 128)
        base_north = mass * north + wind_ref[1, group].reshape(tall, 128)
        for _ in range(ICE_SWEEPS):
            east, north = sweep_ice(a, t, east, north, base_east, base_north, lane)
        for n, value in enumerate((east, north, a, t)):
            out[group, n] = value.reshape(piece, 8, 128)

    def move(p, carry):
        for copy in arrive(p):
            copy.wait()
        body(p)
        leave(p).start()
        return carry

    lax.fori_loop(0, count // piece, move, 0)
    for p in range(count // piece):
        leave(p).wait()


ORDER = pl.BlockSpec(memory_space=pl.ANY)


def chunked(count):
    step = min(count, 64)
    one = pl.BlockSpec((step, 8, 128), lambda i: (i, 0, 0))
    two = pl.BlockSpec((2, step, 8, 128), lambda i: (0, i, 0, 0))
    response = pl.BlockSpec((step, 4, 8, 128), lambda i: (i, 0, 0, 0))
    current = pl.BlockSpec((step, 2, 8, 128), lambda i: (i, 2, 0, 0))
    return step, count // step, one, two, response, current


def send(current, blocks, cols, mass, coriolis, start, wind):
    count = cols.shape[0]
    pieces = count // min(count, PIECE)
    one, two = (count, 8, 128), (2, count, 8, 128)
    return pl.pallas_call(
        send_kernel,
        in_specs=[ORDER, pl.BlockSpec(memory_space=pltpu.VMEM)] + [ORDER] * 5,
        out_specs=ORDER,
        out_shape=jax.ShapeDtypeStruct((count, 6, 8, 128), F32),
        scratch_shapes=[
            pltpu.VMEM((2, 128, 512), F32),
            pltpu.VMEM((3, 512, 256), BF16),
            pltpu.VMEM((2, 1024, 128), F32),
            pltpu.VMEM((1024, 512), BF16),
            pltpu.VMEM(one, I32),
            pltpu.VMEM(one, F32),
            pltpu.VMEM(one, F32),
            pltpu.VMEM(two, F32),
            pltpu.VMEM(two, F32),
            pltpu.VMEM((count, 6, 8, 128), F32),
            pltpu.SemaphoreType.DMA((1,)),
            pltpu.SemaphoreType.DMA((5, pieces)),
            pltpu.SemaphoreType.DMA((pieces,)),
        ],
        compiler_params=params(60),
        cost_estimate=cost(10**9, 8 * MIB),
        name="send",
    )(current, blocks, cols, mass, coriolis, start, wind)


def velocity_kernel(response, current_ref, _, out, done):
    done[...] = jnp.zeros((8, 128), F32)
    piece = min(response.shape[0], PIECE)
    tall = 8 * piece
    lane = iota((tall, 128), 1)

    def body(g, carry):
        group = pl.ds(piece * g, piece)
        base_east, base_north, a, t = (response[group, n].reshape(tall, 128) for n in range(4))
        current = [current_ref[group, c].reshape(tall, 128) for c in range(2)]
        east, north = respond(a, t, *current, lane)
        out[0, group] = (base_east + east).reshape(piece, 8, 128)
        out[1, group] = (base_north + north).reshape(piece, 8, 128)
        return carry

    lax.fori_loop(0, response.shape[0] // piece, body, 0)


def velocities(sent, received, after):
    count = sent.shape[0]
    _, grid, _, two, response, current = chunked(count)
    return pl.pallas_call(
        velocity_kernel,
        grid=(grid,),
        in_specs=[response, current, ORDER],
        out_specs=(two, pl.BlockSpec((8, 128), lambda i: (0, 0))),
        out_shape=(jax.ShapeDtypeStruct((2, count, 8, 128), F32), jax.ShapeDtypeStruct((8, 128), F32)),
        compiler_params=params(50),
        cost_estimate=cost(10**7, 4 * MIB),
        name="velocities",
    )(sent, received, after)


def invert_kernel(cols, key, inverse, hot):
    count = cols.shape[0]
    hot[...] = jnp.where(iota((512, 8 * count), 0) == key[...], 1.0, 0.0).astype(BF16)
    lane = iota((8, 1024), 1)
    weights = jnp.where(lane // 128 == iota((8, 1024), 0), lane % 128 + 1, 0).astype(F32).astype(BF16)
    place = iota((128, 128), 0).astype(F32).astype(BF16)
    one, zero = jnp.ones((128, 128), BF16), jnp.zeros((128, 128), BF16)

    def body(i, carry):
        index = cols[i]
        target = jnp.where(index >= 0, (index >> 1) + 64 * (index & 1), -1).astype(F32)
        masks = []
        for s in range(8):
            row = jnp.broadcast_to(target[s : s + 1], (16, 128)).astype(BF16)
            masks.append(jnp.where(place == jnp.concatenate([row] * 8, axis=0), one, zero))
        found = lax.dot_general(
            weights, jnp.concatenate(masks, axis=1), (((1,), (1,)), ((), ())), preferred_element_type=F32
        )
        inverse[i] = found.astype(I32) - 1
        return carry

    lax.fori_loop(0, count, body, 0, unroll=8)


def invert(cols, key):
    count = cols.shape[0]
    return pl.pallas_call(
        invert_kernel,
        out_shape=(jax.ShapeDtypeStruct((count, 8, 128), I32), jax.ShapeDtypeStruct((512, 8 * count), BF16)),
        compiler_params=params(60),
        cost_estimate=cost(10**10, 2 * MIB),
        name="invert",
    )(cols, key)


def stress_kernel(response_in, sent_in, inverse_in, hot_in, *refs):
    planes, side, ends, parts, response, current_ref, inverse, hot, arrived, listed = refs[-10:]
    count = inverse.shape[0]
    piece = min(count, PIECE)

    def transfer(p):
        span = pl.ds(piece * p, piece)
        return (
            pltpu.make_async_copy(response_in.at[span, pl.ds(0, 4)], response.at[span], arrived.at[0, p]),
            pltpu.make_async_copy(sent_in.at[span, pl.ds(4, 2)], current_ref.at[span], arrived.at[1, p]),
        )

    inverse_copy = pltpu.make_async_copy(inverse_in, inverse, listed.at[0])
    hot_copy = pltpu.make_async_copy(hot_in, hot, listed.at[1])
    for p in range(count // piece):
        for copy in transfer(p):
            copy.start()
        if p == 0:
            inverse_copy.start()
    hot_copy.start()
    inverse_copy.wait()
    tall = 8 * piece
    lane = iota((tall, 128), 1)

    def body(g):
        group = pl.ds(piece * g, piece)
        rows = pl.ds(pl.multiple_of(tall * g, tall), tall)
        base_east, base_north, a, t = (response[group, n].reshape(tall, 128) for n in range(4))
        current = [current_ref[group, c].reshape(tall, 128) for c in range(2)]
        east, north = respond(a, t, *current, lane)
        index = inverse[group].reshape(tall, 128)
        inside = jnp.maximum(index, 0)
        for c, drag in enumerate((base_east + east - current[0], base_north + north - current[1])):
            drag = DRAG * drag
            got = jnp.concatenate(
                [lane_gather(drag[8 * i : 8 * i + 8], inside[8 * i : 8 * i + 8]) for i in range(piece)], axis=0
            )
            pieces = split3(jnp.where(index >= 0, got, 0.0))
            for part in range(3):
                parts[part, rows, 128 * c : 128 * c + 128] = pieces[part]

    def move(p, carry):
        for copy in transfer(p):
            copy.wait()
        body(p)
        return carry

    lax.fori_loop(0, count // piece, move, 0)
    hot_copy.wait()
    total = dot(hot[...], parts[0]) + dot(hot[...], parts[1]) + dot(hot[...], parts[2])
    lane = iota((ROWS, 128), 1)
    low = lane < 64
    top = iota((8, 128), 0) < 4
    edge = jnp.zeros((ROWS, 128), F32)
    for c in range(2):
        for py in range(2):
            for h in range(2):
                first = 256 * h + 64 * py
                a = total[first : first + 64, 128 * c : 128 * c + 128]
                b = total[first + 128 : first + 192, 128 * c : 128 * c + 128]
                even = jnp.where(low, a, pltpu.roll(b, 64, 1))
                odd = jnp.where(low, pltpu.roll(a, 64, 1), b)
                for px, value in ((0, even), (1, odd)):
                    plane = 2 * py + px
                    planes[c, plane, :, 128 * h : 128 * h + 128] = value
                    ends[c, plane, :, 128 * h : 128 * h + 128] = jnp.where(top, value[:8], value[56:])
                    item = 4 * c + plane
                    if h == 0:
                        moved = pltpu.roll(value, 8 * item, 1) if item else value
                        edge = jnp.where(lane // 8 == item, moved, edge)
                    else:
                        moved = pltpu.roll(value, (64 + 8 * item + 8) % 128, 1) if item != 7 else value
                        edge = jnp.where(lane // 8 == 8 + item, moved, edge)
    side[...] = edge


def stresses(received, sent, inverse, hot, after):
    count = inverse.shape[0]
    inside = pl.BlockSpec(memory_space=pltpu.VMEM)
    shapes = ((2, 4, ROWS, COLS), (ROWS, 128), (2, 4, 8, COLS))
    return pl.pallas_call(
        stress_kernel,
        in_specs=[ORDER] * (4 + len(after)),
        out_specs=(inside,) * 3,
        out_shape=tuple(jax.ShapeDtypeStruct(shape, F32) for shape in shapes),
        scratch_shapes=[
            pltpu.VMEM((3, 8 * count, 256), BF16),
            pltpu.VMEM((count, 4, 8, 128), F32),
            pltpu.VMEM((count, 2, 8, 128), F32),
            pltpu.VMEM((count, 8, 128), I32),
            pltpu.VMEM((512, 8 * count), BF16),
            pltpu.SemaphoreType.DMA((2, count // min(count, PIECE))),
            pltpu.SemaphoreType.DMA((2,)),
        ],
        compiler_params=params(60),
        cost_estimate=cost(10**9, 4 * MIB),
        name="stresses",
    )(received, sent, inverse, hot, *after)


def widen_kernel(ends, right, left, far_right, far_left, _, out):
    lane = iota((8, 128), 1)
    top = iota((8, 128), 0) < 4
    from_right = jnp.where(top, right[0:8], right[56:64])
    from_left = jnp.where(top, left[0:8], left[56:64])
    for c in range(2):
        for p in range(4):
            item = 4 * c + p
            r = pltpu.roll(from_right, (128 - 8 * item) % 128, 1) if item else from_right
            s = pltpu.roll(from_left, (56 - 8 * item) % 128, 1) if item != 7 else from_left
            out[item, :, 0:COLS] = ends[c, p]
            out[item, :, COLS:XCOLS] = jnp.where(lane < 64, r, s)
    for py in range(2):
        for g in range(2):
            for n, edge in enumerate((far_right, far_left)):
                span = slice(128 * g, 128 * g + 128)
                out[8 + 2 * py + n, :, span] = jnp.where(top, edge[py, 0:8, span], edge[py, 56:64, span])
            out[8 + 2 * py + g, :, COLS:XCOLS] = jnp.zeros((8, 128), F32)


def widen(ends, right, left, far_right, far_left, after):
    inside = pl.BlockSpec(memory_space=pltpu.VMEM)
    return pl.pallas_call(
        widen_kernel,
        in_specs=[inside] * 5 + [ORDER],
        out_shape=jax.ShapeDtypeStruct((12, 8, XCOLS), F32),
        compiler_params=params(4),
        cost_estimate=cost(10**5, MIB // 4),
        name="widen",
    )(ends, right, left, far_right, far_left, after)


ARRAYS = 11


def prepare_kernel(
    sea, forcing, weights, excess, mask, planes, left, right, ends, halves
):
    lane = iota((8, 128), 1)
    low = lane < 64
    order = jnp.where(low, 2 * lane, 2 * lane - 127)
    swapped = jnp.where(low, 2 * lane + 1, 2 * lane - 128)

    def split(t, carry):
        rows = pl.ds(pl.multiple_of(8 * t, 8), 8)
        w = [weights[k, rows, :] for k in range(8)]
        total = ((w[0] + w[1]) + (w[2] + w[3])) + ((w[4] + w[5]) + (w[6] + w[7]))
        ocean = mask[rows, :] > 0
        inverse = jnp.where(ocean, 1.0 / ((1.0 + excess[rows, :]) * total), 0.0)
        arrays = [v * inverse for v in w]
        arrays += [inverse, forcing[rows, :], jnp.where(ocean, sea[rows, :], 0.0)]
        for n, array in enumerate(arrays):
            for h in range(2):
                a = lane_gather(array[:, 256 * h : 256 * h + 128], order)
                b = lane_gather(array[:, 256 * h + 128 : 256 * h + 256], swapped)
                halves[4 * n + h, rows, :] = jnp.where(low, a, b)
                halves[4 * n + 2 + h, rows, :] = pltpu.roll(jnp.where(low, b, a), 64, 1)
        return carry

    lax.fori_loop(0, 2 * ROWS // 8, split, 0)

    def pack(t, carry):
        out_rows = pl.ds(pl.multiple_of(8 * t, 8), 8)
        for py in range(2):
            rows = pl.ds(16 * t + py, 8, stride=2)
            packed = [[jnp.zeros((8, 128), F32)] * 2, [jnp.zeros((8, 128), F32)] * 2]
            for n in range(ARRAYS):
                for px in range(2):
                    for h in range(2):
                        value = halves[4 * n + 2 * px + h, rows, :]
                        planes[n, 2 * py + px, out_rows, 128 * h : 128 * h + 128] = value
                        item = 2 * n + px
                        shift = (8 * (item % 16) + (8 if h else 0)) % 128
                        moved = pltpu.roll(value, shift, 1) if shift else value
                        packed[h][item // 16] = jnp.where(lane // 8 == item % 16, moved, packed[h][item // 16])
            for g in range(2):
                left[py, out_rows, 128 * g : 128 * g + 128] = packed[0][g]
                right[py, out_rows, 128 * g : 128 * g + 128] = packed[1][g]
        return carry

    lax.fori_loop(0, ROWS // 8, pack, 0)
    top = iota((8, 256), 0) < 4
    for n in range(ARRAYS):
        for p in range(4):
            ends[n, p] = jnp.where(top, planes[n, p, 0:8], planes[n, p, 56:64])


def prepare(sea, forcing, weights, excess, mask):
    return pl.pallas_call(
        prepare_kernel,
        out_shape=(
            jax.ShapeDtypeStruct((ARRAYS, 4, ROWS, COLS), F32),
            jax.ShapeDtypeStruct((2, ROWS, 256), F32),
            jax.ShapeDtypeStruct((2, ROWS, 256), F32),
            jax.ShapeDtypeStruct((ARRAYS, 4, 8, COLS), F32),
        ),
        scratch_shapes=[pltpu.VMEM((4 * ARRAYS, 2 * ROWS, 128), F32)],
        compiler_params=params(60),
        cost_estimate=cost(10**7, 7 * MIB),
        name="prepare",
    )(sea, forcing, weights, excess, mask)


def place_edges(n, p, right, left, lane):
    slot = (2 * n + p % 2) % 16
    r = pltpu.roll(right, (128 - 8 * slot) % 128, 1) if slot else right
    s = pltpu.roll(left, (120 - 8 * slot) % 128, 1) if slot != 15 else left
    return jnp.where(lane < 8, r, jnp.where(lane >= 120, s, 0.0))


def packed_at(n, p):
    group = (2 * n + p % 2) // 16
    return slice(128 * group, 128 * group + 128)


def extend_kernel(planes, right, left, _, out):
    lane = iota((ROWS, 128), 1)
    for n in range(ARRAYS):
        for p in range(4):
            span = packed_at(n, p)
            out[n, p, :, 0:COLS] = planes[n, p]
            out[n, p, :, COLS:XCOLS] = place_edges(n, p, right[p // 2, :, span], left[p // 2, :, span], lane)


def extend(planes, right, left, after):
    inside = pl.BlockSpec(memory_space=pltpu.VMEM)
    return pl.pallas_call(
        extend_kernel,
        in_specs=[inside] * 3 + [ORDER],
        out_shape=jax.ShapeDtypeStruct((ARRAYS, 4, ROWS, XCOLS), F32),
        compiler_params=params(20),
        cost_estimate=cost(10**7, 8 * MIB),
        name="extend",
    )(planes, right, left, after)


def row_shift(value, step):
    return pltpu.roll(value, (-step) % XROWS, 0) if step else value


def col_shift(value, step):
    return pltpu.roll(value, (-step) % XCOLS, 1) if step else value


def neighbour(step, parity):
    return (step + parity) // 2


def sweep_kernel(
    operator, far_below, far_above, stress, right, left, below, above, out, wide, source, field, natural, rim
):
    lane = iota((ROWS, 128), 1)
    top = iota((8, XCOLS), 0) < 4
    for c in range(2):
        for p in range(4):
            item = 4 * c + p
            r = pltpu.roll(right[...], (128 - 8 * item) % 128, 1) if item else right[...]
            s = pltpu.roll(left[...], (56 - 8 * item) % 128, 1) if item != 7 else left[...]
            wide[c, p, 0:ROWS, 0:COLS] = stress[c, p]
            wide[c, p, 0:ROWS, COLS:XCOLS] = jnp.where(lane < 64, r, s)
            wide[c, p, ROWS:XROWS, :] = jnp.where(top, below[item], above[item])
    corners = [jnp.where(top, below[8 + n], above[8 + n]) for n in range(4)]
    for n in range(ARRAYS):
        for p in range(4):
            span = packed_at(n, p)
            far_right, far_left = corners[2 * (p // 2)], corners[2 * (p // 2) + 1]
            rim[n, p, :, 0:COLS] = jnp.where(top[:, :COLS], far_below[n, p], far_above[n, p])
            rim[n, p, :, COLS:XCOLS] = place_edges(n, p, far_right[:, span], far_left[:, span], lane[:8])

    def entry(n, p):
        return jnp.concatenate([operator[n, p], rim[n, p]], axis=0)

    for p in range(4):
        py, px = p // 2, p % 2
        north = wide[1, 2 * py + 1 - px]
        east = wide[0, 2 * (1 - py) + px]
        zonal = col_shift(north, neighbour(1, px)) - col_shift(north, neighbour(-1, px))
        meridional = row_shift(east, neighbour(1, py)) - row_shift(east, neighbour(-1, py))
        source[p] = (entry(9, p) + zonal - meridional) * entry(8, p)
        field[p] = entry(10, p)
    for colour in COLOURS:
        py, px = colour // 2, colour % 2
        value = source[colour]
        for k, (dy, dx) in enumerate(STEPS):
            plane = 2 * (py ^ (dy & 1)) + (px ^ (dx & 1))
            v = field[plane]
            if dy:
                v = row_shift(v, neighbour(dy, py))
            if dx:
                v = col_shift(v, neighbour(dx, px))
            value = value + entry(k, colour) * v
        field[colour] = value
    lane = iota((ROWS, 128), 1)
    even_lane = lane % 2 == 0
    first = lane // 2
    for py in range(2):
        for h in range(2):
            even = field[2 * py, 0:ROWS, 128 * h : 128 * h + 128]
            odd = field[2 * py + 1, 0:ROWS, 128 * h : 128 * h + 128]
            for b in range(2):
                for t in range(ROWS // 8):
                    index = first[:8] + 64 * b
                    e = lane_gather(even[8 * t : 8 * t + 8], index)
                    o = lane_gather(odd[8 * t : 8 * t + 8], index)
                    natural[2 * h + b, pl.ds(16 * t + py, 8, stride=2), :] = jnp.where(even_lane[:8], e, o)
    for k in range(4):
        out[:, 128 * k : 128 * k + 128] = natural[k]


def sweep(*arrays):
    return pl.pallas_call(
        sweep_kernel,
        out_shape=jax.ShapeDtypeStruct((128, 512), F32),
        scratch_shapes=[
            pltpu.VMEM((2, 4, XROWS, XCOLS), F32),
            pltpu.VMEM((4, XROWS, XCOLS), F32),
            pltpu.VMEM((4, XROWS, XCOLS), F32),
            pltpu.VMEM((4, 128, 128), F32),
            pltpu.VMEM((ARRAYS, 4, 8, XCOLS), F32),
        ],
        compiler_params=params(20),
        cost_estimate=cost(10**8, 6 * MIB),
        name="sweep",
    )(*arrays)


AXES = ("zon", "mer")


def exchange(values):
    return lax.all_to_all(values, AXES, split_axis=0, concat_axis=0, tiled=True)


def from_neighbour(values, dz, dm):
    nz, nm = lax.axis_size("zon"), lax.axis_size("mer")
    pairs = [
        (((z + dz) % nz) * nm + m + dm, z * nm + m)
        for z in range(nz)
        for m in range(nm)
        if 0 <= m + dm < nm
    ]
    return lax.ppermute(values, AXES, pairs)


def local(
    sea_level,
    forcing,
    link_weights,
    excess,
    ocean_mask,
    current,
    intersection_block,
    intersection_cols,
    ice_mass,
    coriolis,
    ice_start,
    wind_stress,
):
    blocks = intersection_block[0]
    cols = intersection_cols[0]
    slots = blocks.size
    row, part = blocks >> 2, blocks & 3
    scatter_key = jnp.where(blocks >= 0, part * 128 + (row & 1) * 64 + (row >> 1), -1).reshape(1, slots)
    by_slot = jnp.pad(blocks.T, ((0, 0), (0, 128 - blocks.shape[0])), constant_values=-1)

    sent = send(current, by_slot, cols, ice_mass[0], coriolis[0], ice_start[:, 0], wind_stress[:, 0])
    received = exchange(sent)
    planes, left_edge, right_edge, ends = prepare(sea_level, forcing, link_weights, excess, ocean_mask)
    far_right, far_left = from_neighbour(left_edge, 1, 0), from_neighbour(right_edge, -1, 0)
    far_below, far_above = from_neighbour(ends, 0, 1), from_neighbour(ends, 0, -1)
    inverse, hot = invert(cols, scatter_key)
    stress, side, ends = stresses(received, sent, inverse, hot, (far_right, far_left, far_below, far_above))
    right, left = from_neighbour(side, 1, 0), from_neighbour(side, -1, 0)
    velocity, done = velocities(sent, received, side)
    rows = widen(ends, right, left, far_right, far_left, done)
    operator = extend(planes, far_right, far_left, rows)
    below, above = from_neighbour(rows, 0, 1), from_neighbour(rows, 0, -1)
    surface = sweep(operator, far_below, far_above, stress, right, left, below, above)
    return surface, velocity[:, None]


def solution(mesh):
    return jax.shard_map(
        local,
        mesh=mesh,
        in_specs=(
            P("mer", "zon"),
            P("mer", "zon"),
            P(None, "mer", "zon"),
            P("mer", "zon"),
            P("mer", "zon"),
            P(None, "mer", "zon"),
            P(("zon", "mer"), None, None),
            P(("zon", "mer"), None, None, None),
            P(("zon", "mer"), None, None, None),
            P(("zon", "mer"), None, None, None),
            P(None, ("zon", "mer"), None, None, None),
            P(None, ("zon", "mer"), None, None, None),
        ),
        out_specs=(P("mer", "zon"), P(None, ("zon", "mer"), None, None, None)),
        check_vma=False,
    )
```

```python
import jax
import jax.numpy as jnp
from jax import lax
from jax.experimental import pallas as pl
from jax.experimental.pallas import tpu as pltpu
from jax.sharding import PartitionSpec as P

SWEEPS = 2
ICE_SWEEPS = 3
DRAG = 1.0
LINK = 0.5
STEPS = ((0, 1), (0, -1), (1, 0), (-1, 0), (1, 1), (1, -1), (-1, 1), (-1, -1))
COLOURS = (0,) + (1, 2, 3, 2, 1, 0) * SWEEPS
F32, BF16, I32 = jnp.float32, jnp.bfloat16, jnp.int32
MIB = 1 << 20
ROWS, COLS, XROWS, XCOLS = 64, 256, 72, 384


def params(vmem=48):
    return pltpu.CompilerParams(vmem_limit_bytes=vmem * MIB)


def cost(flops, moved):
    return pl.CostEstimate(flops=flops, bytes_accessed=moved, transcendentals=0)


def iota(shape, dim):
    return lax.broadcasted_iota(I32, shape, dim)


def lane_gather(values, index):
    return jnp.take_along_axis(values, index, axis=1, mode="promise_in_bounds")


def split3(values):
    high = values.astype(BF16)
    rest = values - high.astype(F32)
    middle = rest.astype(BF16)
    low = (rest - middle.astype(F32)).astype(BF16)
    return high, middle, low


def dot(a, b):
    return jnp.dot(a, b, preferred_element_type=F32)


def beside(values, lane):
    before = jnp.where(lane == 0, 0.0, pltpu.roll(values, 1, 1))
    after = jnp.where(lane == 127, 0.0, pltpu.roll(values, 127, 1))
    return LINK * (before + after)


def turn(a, t, east, north):
    return a * east + t * north, a * north - t * east


def sweep_ice(a, t, east, north, base_east, base_north, lane):
    return turn(a, t, base_east + beside(east, lane), base_north + beside(north, lane))


def respond(a, t, current_east, current_north, lane):
    east, north = turn(a, t, current_east, current_north)
    for _ in range(ICE_SWEEPS - 1):
        east, north = sweep_ice(a, t, east, north, current_east, current_north, lane)
    return east, north


PIECE = 32


def send_kernel(current_in, blocks, *refs):
    ice_in, sent, (current, table, rows, hot), ice, out, (first, arrived, gone) = (
        refs[:5],
        refs[5],
        refs[6:10],
        refs[10:15],
        refs[15],
        refs[16:],
    )
    count = out.shape[0]
    piece = min(count, PIECE)
    current_copy = pltpu.make_async_copy(current_in, current, first.at[0])
    current_copy.start()

    def arrive(p):
        span = pl.ds(piece * p, piece)
        return [
            pltpu.make_async_copy(source.at[span], target.at[span], arrived.at[n, p])
            if n < 3
            else pltpu.make_async_copy(source.at[:, span], target.at[:, span], arrived.at[n, p])
            for n, (source, target) in enumerate(zip(ice_in, ice))
        ]

    def leave(p):
        span = pl.ds(piece * p, piece)
        return pltpu.make_async_copy(out.at[span], sent.at[span], gone.at[p])

    for p in range(count // piece):
        for copy in arrive(p):
            copy.start()

    key = jnp.where(blocks[...] >= 0, (blocks[...] & 3) * 128 + (blocks[...] >> 2), -1)
    key = jnp.transpose(jnp.concatenate([key, jnp.zeros((120, 128), I32)], axis=0))
    place = iota((128, 512), 1)
    for s in range(8):
        hot[128 * s : 128 * s + 128] = jnp.where(key[:, s : s + 1] == place, 1.0, 0.0).astype(BF16)
    current_copy.wait()
    for c in range(2):
        for k in range(4):
            parts = split3(current[c, :, 128 * k : 128 * k + 128])
            for part in range(3):
                table[part, 128 * k : 128 * k + 128, 128 * c : 128 * c + 128] = parts[part]
    for q in range(4):
        span = slice(256 * q, 256 * q + 256)
        got = dot(hot[span], table[0]) + dot(hot[span], table[1]) + dot(hot[span], table[2])
        rows[0, span] = got[:, :128]
        rows[1, span] = got[:, 128:]

    tall = 8 * piece
    lane = iota((tall, 128), 1)
    cols, mass_ref, coriolis_ref, start_ref, wind_ref = ice

    def body(g):
        group = pl.ds(piece * g, piece)
        index = cols[group].reshape(tall, 128)
        inside = jnp.maximum(index, 0)
        for c in range(2):
            got = jnp.concatenate(
                [
                    lane_gather(rows[c, pl.ds(piece * g + i, 8, stride=128), :], inside[8 * i : 8 * i + 8])
                    for i in range(piece)
                ],
                axis=0,
            )
            out[group, 4 + c] = jnp.where(index >= 0, DRAG * got, 0.0).reshape(piece, 8, 128)
        mass = mass_ref[group].reshape(tall, 128)
        a = mass + DRAG + 2.0 * LINK
        t = coriolis_ref[group].reshape(tall, 128) * mass
        inverse = 1.0 / (a * a + t * t)
        a = a * inverse
        t = t * inverse
        east = start_ref[0, group].reshape(tall, 128)
        north = start_ref[1, group].reshape(tall, 128)
        base_east = mass * east + wind_ref[0, group].reshape(tall, 128)
        base_north = mass * north + wind_ref[1, group].reshape(tall, 128)
        for _ in range(ICE_SWEEPS):
            east, north = sweep_ice(a, t, east, north, base_east, base_north, lane)
        for n, value in enumerate((east, north, a, t)):
            out[group, n] = value.reshape(piece, 8, 128)

    def move(p, carry):
        for copy in arrive(p):
            copy.wait()
        body(p)
        leave(p).start()
        return carry

    lax.fori_loop(0, count // piece, move, 0)
    for p in range(count // piece):
        leave(p).wait()


ORDER = pl.BlockSpec(memory_space=pl.ANY)


def chunked(count):
    step = min(count, 64)
    one = pl.BlockSpec((step, 8, 128), lambda i: (i, 0, 0))
    two = pl.BlockSpec((2, step, 8, 128), lambda i: (0, i, 0, 0))
    response = pl.BlockSpec((step, 4, 8, 128), lambda i: (i, 0, 0, 0))
    current = pl.BlockSpec((step, 2, 8, 128), lambda i: (i, 2, 0, 0))
    return step, count // step, one, two, response, current


def send(current, blocks, cols, mass, coriolis, start, wind):
    count = cols.shape[0]
    pieces = count // min(count, PIECE)
    one, two = (count, 8, 128), (2, count, 8, 128)
    return pl.pallas_call(
        send_kernel,
        in_specs=[ORDER, pl.BlockSpec(memory_space=pltpu.VMEM)] + [ORDER] * 5,
        out_specs=ORDER,
        out_shape=jax.ShapeDtypeStruct((count, 6, 8, 128), F32),
        scratch_shapes=[
            pltpu.VMEM((2, 128, 512), F32),
            pltpu.VMEM((3, 512, 256), BF16),
            pltpu.VMEM((2, 1024, 128), F32),
            pltpu.VMEM((1024, 512), BF16),
            pltpu.VMEM(one, I32),
            pltpu.VMEM(one, F32),
            pltpu.VMEM(one, F32),
            pltpu.VMEM(two, F32),
            pltpu.VMEM(two, F32),
            pltpu.VMEM((count, 6, 8, 128), F32),
            pltpu.SemaphoreType.DMA((1,)),
            pltpu.SemaphoreType.DMA((5, pieces)),
            pltpu.SemaphoreType.DMA((pieces,)),
        ],
        compiler_params=params(60),
        cost_estimate=cost(10**9, 8 * MIB),
        name="send",
    )(current, blocks, cols, mass, coriolis, start, wind)


def velocity_kernel(response, current_ref, _, out, done):
    done[...] = jnp.zeros((8, 128), F32)
    piece = min(response.shape[0], PIECE)
    tall = 8 * piece
    lane = iota((tall, 128), 1)

    def body(g, carry):
        group = pl.ds(piece * g, piece)
        base_east, base_north, a, t = (response[group, n].reshape(tall, 128) for n in range(4))
        current = [current_ref[group, c].reshape(tall, 128) for c in range(2)]
        east, north = respond(a, t, *current, lane)
        out[0, group] = (base_east + east).reshape(piece, 8, 128)
        out[1, group] = (base_north + north).reshape(piece, 8, 128)
        return carry

    lax.fori_loop(0, response.shape[0] // piece, body, 0)


def velocities(sent, received, after):
    count = sent.shape[0]
    _, grid, _, two, response, current = chunked(count)
    return pl.pallas_call(
        velocity_kernel,
        grid=(grid,),
        in_specs=[response, current, ORDER],
        out_specs=(two, pl.BlockSpec((8, 128), lambda i: (0, 0))),
        out_shape=(jax.ShapeDtypeStruct((2, count, 8, 128), F32), jax.ShapeDtypeStruct((8, 128), F32)),
        compiler_params=params(50),
        cost_estimate=cost(10**7, 4 * MIB),
        name="velocities",
    )(sent, received, after)


def invert_kernel(cols, key, inverse, hot):
    count = cols.shape[0]
    hot[...] = jnp.where(iota((512, 8 * count), 0) == key[...], 1.0, 0.0).astype(BF16)
    lane = iota((8, 1024), 1)
    weights = jnp.where(lane // 128 == iota((8, 1024), 0), lane % 128 + 1, 0).astype(F32).astype(BF16)
    place = iota((128, 128), 0).astype(F32).astype(BF16)
    one, zero = jnp.ones((128, 128), BF16), jnp.zeros((128, 128), BF16)

    def body(i, carry):
        index = cols[i]
        target = jnp.where(index >= 0, (index >> 1) + 64 * (index & 1), -1).astype(F32)
        masks = []
        for s in range(8):
            row = jnp.broadcast_to(target[s : s + 1], (16, 128)).astype(BF16)
            masks.append(jnp.where(place == jnp.concatenate([row] * 8, axis=0), one, zero))
        found = lax.dot_general(
            weights, jnp.concatenate(masks, axis=1), (((1,), (1,)), ((), ())), preferred_element_type=F32
        )
        inverse[i] = found.astype(I32) - 1
        return carry

    lax.fori_loop(0, count, body, 0, unroll=8)


def invert(cols, key):
    count = cols.shape[0]
    return pl.pallas_call(
        invert_kernel,
        out_shape=(jax.ShapeDtypeStruct((count, 8, 128), I32), jax.ShapeDtypeStruct((512, 8 * count), BF16)),
        compiler_params=params(60),
        cost_estimate=cost(10**10, 2 * MIB),
        name="invert",
    )(cols, key)


def stress_kernel(response_in, sent_in, inverse_in, hot_in, *refs):
    planes, side, ends, parts, response, current_ref, inverse, hot, arrived, listed = refs[-10:]
    count = inverse.shape[0]
    piece = min(count, PIECE)

    def transfer(p):
        span = pl.ds(piece * p, piece)
        return (
            pltpu.make_async_copy(response_in.at[span, pl.ds(0, 4)], response.at[span], arrived.at[0, p]),
            pltpu.make_async_copy(sent_in.at[span, pl.ds(4, 2)], current_ref.at[span], arrived.at[1, p]),
        )

    inverse_copy = pltpu.make_async_copy(inverse_in, inverse, listed.at[0])
    hot_copy = pltpu.make_async_copy(hot_in, hot, listed.at[1])
    for p in range(count // piece):
        for copy in transfer(p):
            copy.start()
        if p == 0:
            inverse_copy.start()
    hot_copy.start()
    inverse_copy.wait()
    tall = 8 * piece
    lane = iota((tall, 128), 1)

    def body(g):
        group = pl.ds(piece * g, piece)
        rows = pl.ds(pl.multiple_of(tall * g, tall), tall)
        base_east, base_north, a, t = (response[group, n].reshape(tall, 128) for n in range(4))
        current = [current_ref[group, c].reshape(tall, 128) for c in range(2)]
        east, north = respond(a, t, *current, lane)
        index = inverse[group].reshape(tall, 128)
        inside = jnp.maximum(index, 0)
        for c, drag in enumerate((base_east + east - current[0], base_north + north - current[1])):
            drag = DRAG * drag
            got = jnp.concatenate(
                [lane_gather(drag[8 * i : 8 * i + 8], inside[8 * i : 8 * i + 8]) for i in range(piece)], axis=0
            )
            pieces = split3(jnp.where(index >= 0, got, 0.0))
            for part in range(3):
                parts[part, rows, 128 * c : 128 * c + 128] = pieces[part]

    def move(p, carry):
        for copy in transfer(p):
            copy.wait()
        body(p)
        return carry

    lax.fori_loop(0, count // piece, move, 0)
    hot_copy.wait()
    total = dot(hot[...], parts[0]) + dot(hot[...], parts[1]) + dot(hot[...], parts[2])
    lane = iota((ROWS, 128), 1)
    low = lane < 64
    top = iota((8, 128), 0) < 4
    edge = jnp.zeros((ROWS, 128), F32)
    for c in range(2):
        for py in range(2):
            for h in range(2):
                first = 256 * h + 64 * py
                a = total[first : first + 64, 128 * c : 128 * c + 128]
                b = total[first + 128 : first + 192, 128 * c : 128 * c + 128]
                even = jnp.where(low, a, pltpu.roll(b, 64, 1))
                odd = jnp.where(low, pltpu.roll(a, 64, 1), b)
                for px, value in ((0, even), (1, odd)):
                    plane = 2 * py + px
                    planes[c, plane, :, 128 * h : 128 * h + 128] = value
                    ends[c, plane, :, 128 * h : 128 * h + 128] = jnp.where(top, value[:8], value[56:])
                    item = 4 * c + plane
                    if h == 0:
                        moved = pltpu.roll(value, 8 * item, 1) if item else value
                        edge = jnp.where(lane // 8 == item, moved, edge)
                    else:
                        moved = pltpu.roll(value, (64 + 8 * item + 8) % 128, 1) if item != 7 else value
                        edge = jnp.where(lane // 8 == 8 + item, moved, edge)
    side[...] = edge


def stresses(received, sent, inverse, hot, after):
    count = inverse.shape[0]
    inside = pl.BlockSpec(memory_space=pltpu.VMEM)
    shapes = ((2, 4, ROWS, COLS), (ROWS, 128), (2, 4, 8, COLS))
    return pl.pallas_call(
        stress_kernel,
        in_specs=[ORDER] * (4 + len(after)),
        out_specs=(inside,) * 3,
        out_shape=tuple(jax.ShapeDtypeStruct(shape, F32) for shape in shapes),
        scratch_shapes=[
            pltpu.VMEM((3, 8 * count, 256), BF16),
            pltpu.VMEM((count, 4, 8, 128), F32),
            pltpu.VMEM((count, 2, 8, 128), F32),
            pltpu.VMEM((count, 8, 128), I32),
            pltpu.VMEM((512, 8 * count), BF16),
            pltpu.SemaphoreType.DMA((2, count // min(count, PIECE))),
            pltpu.SemaphoreType.DMA((2,)),
        ],
        compiler_params=params(60),
        cost_estimate=cost(10**9, 4 * MIB),
        name="stresses",
    )(received, sent, inverse, hot, *after)


def widen_kernel(ends, right, left, far_right, far_left, _, out):
    lane = iota((8, 128), 1)
    top = iota((8, 128), 0) < 4
    from_right = jnp.where(top, right[0:8], right[56:64])
    from_left = jnp.where(top, left[0:8], left[56:64])
    for c in range(2):
        for p in range(4):
            item = 4 * c + p
            r = pltpu.roll(from_right, (128 - 8 * item) % 128, 1) if item else from_right
            s = pltpu.roll(from_left, (56 - 8 * item) % 128, 1) if item != 7 else from_left
            out[item, :, 0:COLS] = ends[c, p]
            out[item, :, COLS:XCOLS] = jnp.where(lane < 64, r, s)
    for py in range(2):
        for g in range(2):
            for n, edge in enumerate((far_right, far_left)):
                span = slice(128 * g, 128 * g + 128)
                out[8 + 2 * py + n, :, span] = jnp.where(top, edge[py, 0:8, span], edge[py, 56:64, span])
            out[8 + 2 * py + g, :, COLS:XCOLS] = jnp.zeros((8, 128), F32)


def widen(ends, right, left, far_right, far_left, after):
    inside = pl.BlockSpec(memory_space=pltpu.VMEM)
    return pl.pallas_call(
        widen_kernel,
        in_specs=[inside] * 5 + [ORDER],
        out_shape=jax.ShapeDtypeStruct((12, 8, XCOLS), F32),
        compiler_params=params(4),
        cost_estimate=cost(10**5, MIB // 4),
        name="widen",
    )(ends, right, left, far_right, far_left, after)


ARRAYS = 11


def prepare_kernel(
    sea, forcing, weights, excess, mask, planes, left, right, ends, halves
):
    lane = iota((8, 128), 1)
    low = lane < 64
    order = jnp.where(low, 2 * lane, 2 * lane - 127)
    swapped = jnp.where(low, 2 * lane + 1, 2 * lane - 128)

    def split(t, carry):
        rows = pl.ds(pl.multiple_of(8 * t, 8), 8)
        w = [weights[k, rows, :] for k in range(8)]
        total = ((w[0] + w[1]) + (w[2] + w[3])) + ((w[4] + w[5]) + (w[6] + w[7]))
        ocean = mask[rows, :] > 0
        inverse = jnp.where(ocean, 1.0 / ((1.0 + excess[rows, :]) * total), 0.0)
        arrays = [v * inverse for v in w]
        arrays += [inverse, forcing[rows, :], jnp.where(ocean, sea[rows, :], 0.0)]
        for n, array in enumerate(arrays):
            for h in range(2):
                a = lane_gather(array[:, 256 * h : 256 * h + 128], order)
                b = lane_gather(array[:, 256 * h + 128 : 256 * h + 256], swapped)
                halves[4 * n + h, rows, :] = jnp.where(low, a, b)
                halves[4 * n + 2 + h, rows, :] = pltpu.roll(jnp.where(low, b, a), 64, 1)
        return carry

    lax.fori_loop(0, 2 * ROWS // 8, split, 0)

    def pack(t, carry):
        out_rows = pl.ds(pl.multiple_of(8 * t, 8), 8)
        for py in range(2):
            rows = pl.ds(16 * t + py, 8, stride=2)
            packed = [[jnp.zeros((8, 128), F32)] * 2, [jnp.zeros((8, 128), F32)] * 2]
            for n in range(ARRAYS):
                for px in range(2):
                    for h in range(2):
                        value = halves[4 * n + 2 * px + h, rows, :]
                        planes[n, 2 * py + px, out_rows, 128 * h : 128 * h + 128] = value
                        item = 2 * n + px
                        shift = (8 * (item % 16) + (8 if h else 0)) % 128
                        moved = pltpu.roll(value, shift, 1) if shift else value
                        packed[h][item // 16] = jnp.where(lane // 8 == item % 16, moved, packed[h][item // 16])
            for g in range(2):
                left[py, out_rows, 128 * g : 128 * g + 128] = packed[0][g]
                right[py, out_rows, 128 * g : 128 * g + 128] = packed[1][g]
        return carry

    lax.fori_loop(0, ROWS // 8, pack, 0)
    top = iota((8, 256), 0) < 4
    for n in range(ARRAYS):
        for p in range(4):
            ends[n, p] = jnp.where(top, planes[n, p, 0:8], planes[n, p, 56:64])


def prepare(sea, forcing, weights, excess, mask):
    return pl.pallas_call(
        prepare_kernel,
        out_shape=(
            jax.ShapeDtypeStruct((ARRAYS, 4, ROWS, COLS), F32),
            jax.ShapeDtypeStruct((2, ROWS, 256), F32),
            jax.ShapeDtypeStruct((2, ROWS, 256), F32),
            jax.ShapeDtypeStruct((ARRAYS, 4, 8, COLS), F32),
        ),
        scratch_shapes=[pltpu.VMEM((4 * ARRAYS, 2 * ROWS, 128), F32)],
        compiler_params=params(60),
        cost_estimate=cost(10**7, 7 * MIB),
        name="prepare",
    )(sea, forcing, weights, excess, mask)


def place_edges(n, p, right, left, lane):
    slot = (2 * n + p % 2) % 16
    r = pltpu.roll(right, (128 - 8 * slot) % 128, 1) if slot else right
    s = pltpu.roll(left, (120 - 8 * slot) % 128, 1) if slot != 15 else left
    return jnp.where(lane < 8, r, jnp.where(lane >= 120, s, 0.0))


def packed_at(n, p):
    group = (2 * n + p % 2) // 16
    return slice(128 * group, 128 * group + 128)


def extend_kernel(planes, right, left, _, out):
    lane = iota((ROWS, 128), 1)
    for n in range(ARRAYS):
        for p in range(4):
            span = packed_at(n, p)
            out[n, p, :, 0:COLS] = planes[n, p]
            out[n, p, :, COLS:XCOLS] = place_edges(n, p, right[p // 2, :, span], left[p // 2, :, span], lane)


def extend(planes, right, left, after):
    inside = pl.BlockSpec(memory_space=pltpu.VMEM)
    return pl.pallas_call(
        extend_kernel,
        in_specs=[inside] * 3 + [ORDER],
        out_shape=jax.ShapeDtypeStruct((ARRAYS, 4, ROWS, XCOLS), F32),
        compiler_params=params(20),
        cost_estimate=cost(10**7, 8 * MIB),
        name="extend",
    )(planes, right, left, after)


def row_shift(value, step):
    return pltpu.roll(value, (-step) % XROWS, 0) if step else value


def col_shift(value, step):
    return pltpu.roll(value, (-step) % XCOLS, 1) if step else value


def neighbour(step, parity):
    return (step + parity) // 2


def sweep_kernel(
    operator, far_below, far_above, stress, right, left, below, above, out, wide, source, field, natural, rim
):
    lane = iota((ROWS, 128), 1)
    top = iota((8, XCOLS), 0) < 4
    for c in range(2):
        for p in range(4):
            item = 4 * c + p
            r = pltpu.roll(right[...], (128 - 8 * item) % 128, 1) if item else right[...]
            s = pltpu.roll(left[...], (56 - 8 * item) % 128, 1) if item != 7 else left[...]
            wide[c, p, 0:ROWS, 0:COLS] = stress[c, p]
            wide[c, p, 0:ROWS, COLS:XCOLS] = jnp.where(lane < 64, r, s)
            wide[c, p, ROWS:XROWS, :] = jnp.where(top, below[item], above[item])
    corners = [jnp.where(top, below[8 + n], above[8 + n]) for n in range(4)]
    for n in range(ARRAYS):
        for p in range(4):
            span = packed_at(n, p)
            far_right, far_left = corners[2 * (p // 2)], corners[2 * (p // 2) + 1]
            rim[n, p, :, 0:COLS] = jnp.where(top[:, :COLS], far_below[n, p], far_above[n, p])
            rim[n, p, :, COLS:XCOLS] = place_edges(n, p, far_right[:, span], far_left[:, span], lane[:8])

    def entry(n, p):
        return jnp.concatenate([operator[n, p], rim[n, p]], axis=0)

    for p in range(4):
        py, px = p // 2, p % 2
        north = wide[1, 2 * py + 1 - px]
        east = wide[0, 2 * (1 - py) + px]
        zonal = col_shift(north, neighbour(1, px)) - col_shift(north, neighbour(-1, px))
        meridional = row_shift(east, neighbour(1, py)) - row_shift(east, neighbour(-1, py))
        source[p] = (entry(9, p) + zonal - meridional) * entry(8, p)
        field[p] = entry(10, p)
    for colour in COLOURS:
        py, px = colour // 2, colour % 2
        value = source[colour]
        for k, (dy, dx) in enumerate(STEPS):
            plane = 2 * (py ^ (dy & 1)) + (px ^ (dx & 1))
            v = field[plane]
            if dy:
                v = row_shift(v, neighbour(dy, py))
            if dx:
                v = col_shift(v, neighbour(dx, px))
            value = value + entry(k, colour) * v
        field[colour] = value
    lane = iota((ROWS, 128), 1)
    even_lane = lane % 2 == 0
    first = lane // 2
    for py in range(2):
        for h in range(2):
            even = field[2 * py, 0:ROWS, 128 * h : 128 * h + 128]
            odd = field[2 * py + 1, 0:ROWS, 128 * h : 128 * h + 128]
            for b in range(2):
                for t in range(ROWS // 8):
                    index = first[:8] + 64 * b
                    e = lane_gather(even[8 * t : 8 * t + 8], index)
                    o = lane_gather(odd[8 * t : 8 * t + 8], index)
                    natural[2 * h + b, pl.ds(16 * t + py, 8, stride=2), :] = jnp.where(even_lane[:8], e, o)
    for k in range(4):
        out[:, 128 * k : 128 * k + 128] = natural[k]


def sweep(*arrays):
    return pl.pallas_call(
        sweep_kernel,
        out_shape=jax.ShapeDtypeStruct((128, 512), F32),
        scratch_shapes=[
            pltpu.VMEM((2, 4, XROWS, XCOLS), F32),
            pltpu.VMEM((4, XROWS, XCOLS), F32),
            pltpu.VMEM((4, XROWS, XCOLS), F32),
            pltpu.VMEM((4, 128, 128), F32),
            pltpu.VMEM((ARRAYS, 4, 8, XCOLS), F32),
        ],
        compiler_params=params(20),
        cost_estimate=cost(10**8, 6 * MIB),
        name="sweep",
    )(*arrays)


AXES = ("zon", "mer")


def exchange(values):
    return lax.all_to_all(values, AXES, split_axis=0, concat_axis=0, tiled=True)


def from_neighbour(values, dz, dm):
    nz, nm = lax.axis_size("zon"), lax.axis_size("mer")
    pairs = [
        (((z + dz) % nz) * nm + m + dm, z * nm + m)
        for z in range(nz)
        for m in range(nm)
        if 0 <= m + dm < nm
    ]
    return lax.ppermute(values, AXES, pairs)


def local(
    sea_level,
    forcing,
    link_weights,
    excess,
    ocean_mask,
    current,
    intersection_block,
    intersection_cols,
    ice_mass,
    coriolis,
    ice_start,
    wind_stress,
):
    blocks = intersection_block[0]
    cols = intersection_cols[0]
    slots = blocks.size
    row, part = blocks >> 2, blocks & 3
    scatter_key = jnp.where(blocks >= 0, part * 128 + (row & 1) * 64 + (row >> 1), -1).reshape(1, slots)
    by_slot = jnp.pad(blocks.T, ((0, 0), (0, 128 - blocks.shape[0])), constant_values=-1)

    sent = send(current, by_slot, cols, ice_mass[0], coriolis[0], ice_start[:, 0], wind_stress[:, 0])
    received = exchange(sent)
    planes, left_edge, right_edge, ends = prepare(sea_level, forcing, link_weights, excess, ocean_mask)
    far_right, far_left = from_neighbour(left_edge, 1, 0), from_neighbour(right_edge, -1, 0)
    far_below, far_above = from_neighbour(ends, 0, 1), from_neighbour(ends, 0, -1)
    inverse, hot = invert(cols, scatter_key)
    stress, side, ends = stresses(received, sent, inverse, hot, (left_edge,))
    right, left = from_neighbour(side, 1, 0), from_neighbour(side, -1, 0)
    velocity, done = velocities(sent, received, side)
    rows = widen(ends, right, left, far_right, far_left, done)
    operator = extend(planes, far_right, far_left, rows)
    below, above = from_neighbour(rows, 0, 1), from_neighbour(rows, 0, -1)
    surface = sweep(operator, far_below, far_above, stress, right, left, below, above)
    return surface, velocity[:, None]


def solution(mesh):
    return jax.shard_map(
        local,
        mesh=mesh,
        in_specs=(
            P("mer", "zon"),
            P("mer", "zon"),
            P(None, "mer", "zon"),
            P("mer", "zon"),
            P("mer", "zon"),
            P(None, "mer", "zon"),
            P(("zon", "mer"), None, None),
            P(("zon", "mer"), None, None, None),
            P(("zon", "mer"), None, None, None),
            P(("zon", "mer"), None, None, None),
            P(None, ("zon", "mer"), None, None, None),
            P(None, ("zon", "mer"), None, None, None),
        ),
        out_specs=(P("mer", "zon"), P(None, ("zon", "mer"), None, None, None)),
        check_vma=False,
    )
```

```python
import jax
import jax.numpy as jnp
from jax import lax
from jax.experimental import pallas as pl
from jax.experimental.pallas import tpu as pltpu
from jax.sharding import PartitionSpec as P

SWEEPS = 2
ICE_SWEEPS = 3
DRAG = 1.0
LINK = 0.5
STEPS = ((0, 1), (0, -1), (1, 0), (-1, 0), (1, 1), (1, -1), (-1, 1), (-1, -1))
COLOURS = (0,) + (1, 2, 3, 2, 1, 0) * SWEEPS
F32, BF16, I32 = jnp.float32, jnp.bfloat16, jnp.int32
MIB = 1 << 20
ROWS, COLS, XROWS, XCOLS = 64, 256, 72, 384


def params(vmem=48):
    return pltpu.CompilerParams(vmem_limit_bytes=vmem * MIB)


def cost(flops, moved):
    return pl.CostEstimate(flops=flops, bytes_accessed=moved, transcendentals=0)


def iota(shape, dim):
    return lax.broadcasted_iota(I32, shape, dim)


def lane_gather(values, index):
    return jnp.take_along_axis(values, index, axis=1, mode="promise_in_bounds")


def split3(values):
    high = values.astype(BF16)
    rest = values - high.astype(F32)
    middle = rest.astype(BF16)
    low = (rest - middle.astype(F32)).astype(BF16)
    return high, middle, low


def half_turn(tile):
    return pltpu.roll(tile, 4, 0)


def pack_rows(even_rows, odd_rows, top):
    return (
        jnp.where(top, even_rows, half_turn(odd_rows)),
        jnp.where(top, half_turn(even_rows), odd_rows),
    )


def unpack_rows(py, below, above, top):
    if py:
        return jnp.where(top, half_turn(below), above)
    return jnp.where(top, below, half_turn(above))


def dot(a, b):
    return jnp.dot(a, b, preferred_element_type=F32)


def beside(values, lane):
    before = jnp.where(lane == 0, 0.0, pltpu.roll(values, 1, 1))
    after = jnp.where(lane == 127, 0.0, pltpu.roll(values, 127, 1))
    return LINK * (before + after)


def turn(a, t, east, north):
    return a * east + t * north, a * north - t * east


def sweep_ice(a, t, east, north, base_east, base_north, lane):
    return turn(a, t, base_east + beside(east, lane), base_north + beside(north, lane))


def respond(a, t, current_east, current_north, lane):
    east, north = turn(a, t, current_east, current_north)
    for _ in range(ICE_SWEEPS - 1):
        east, north = sweep_ice(a, t, east, north, current_east, current_north, lane)
    return east, north


PIECE = 32


def send_kernel(current_in, blocks, *refs):
    ice_in, sent, (current, table, rows, hot), ice, out, (first, arrived, gone) = (
        refs[:5],
        refs[5],
        refs[6:10],
        refs[10:15],
        refs[15],
        refs[16:],
    )
    count = out.shape[0]
    piece = min(count, PIECE)
    current_copy = pltpu.make_async_copy(current_in, current, first.at[0])
    current_copy.start()

    def arrive(p):
        span = pl.ds(piece * p, piece)
        return [
            pltpu.make_async_copy(source.at[span], target.at[span], arrived.at[n, p])
            if n < 3
            else pltpu.make_async_copy(source.at[:, span], target.at[:, span], arrived.at[n, p])
            for n, (source, target) in enumerate(zip(ice_in, ice))
        ]

    def leave(p):
        span = pl.ds(piece * p, piece)
        return pltpu.make_async_copy(out.at[span], sent.at[span], gone.at[p])

    for p in range(count // piece):
        for copy in arrive(p):
            copy.start()

    key = jnp.where(blocks[...] >= 0, (blocks[...] & 3) * 128 + (blocks[...] >> 2), -1)
    key = jnp.transpose(jnp.concatenate([key, jnp.zeros((120, 128), I32)], axis=0))
    place = iota((128, 512), 1)
    for s in range(8):
        hot[128 * s : 128 * s + 128] = jnp.where(key[:, s : s + 1] == place, 1.0, 0.0).astype(BF16)
    current_copy.wait()
    for c in range(2):
        for k in range(4):
            parts = split3(current[c, :, 128 * k : 128 * k + 128])
            for part in range(3):
                table[part, 128 * k : 128 * k + 128, 128 * c : 128 * c + 128] = parts[part]
    for q in range(4):
        span = slice(256 * q, 256 * q + 256)
        got = dot(hot[span], table[0]) + dot(hot[span], table[1]) + dot(hot[span], table[2])
        rows[0, span] = got[:, :128]
        rows[1, span] = got[:, 128:]

    tall = 8 * piece
    lane = iota((tall, 128), 1)
    cols, mass_ref, coriolis_ref, start_ref, wind_ref = ice

    def body(g):
        group = pl.ds(piece * g, piece)
        index = cols[group].reshape(tall, 128)
        inside = jnp.maximum(index, 0)
        for c in range(2):
            got = jnp.concatenate(
                [
                    lane_gather(rows[c, pl.ds(piece * g + i, 8, stride=128), :], inside[8 * i : 8 * i + 8])
                    for i in range(piece)
                ],
                axis=0,
            )
            out[group, 4 + c] = jnp.where(index >= 0, DRAG * got, 0.0).reshape(piece, 8, 128)
        mass = mass_ref[group].reshape(tall, 128)
        a = mass + DRAG + 2.0 * LINK
        t = coriolis_ref[group].reshape(tall, 128) * mass
        inverse = 1.0 / (a * a + t * t)
        a = a * inverse
        t = t * inverse
        east = start_ref[0, group].reshape(tall, 128)
        north = start_ref[1, group].reshape(tall, 128)
        base_east = mass * east + wind_ref[0, group].reshape(tall, 128)
        base_north = mass * north + wind_ref[1, group].reshape(tall, 128)
        for _ in range(ICE_SWEEPS):
            east, north = sweep_ice(a, t, east, north, base_east, base_north, lane)
        for n, value in enumerate((east, north, a, t)):
            out[group, n] = value.reshape(piece, 8, 128)

    def move(p, carry):
        for copy in arrive(p):
            copy.wait()
        body(p)
        leave(p).start()
        return carry

    lax.fori_loop(0, count // piece, move, 0)
    for p in range(count // piece):
        leave(p).wait()


ORDER = pl.BlockSpec(memory_space=pl.ANY)


def chunked(count):
    step = min(count, 64)
    one = pl.BlockSpec((step, 8, 128), lambda i: (i, 0, 0))
    two = pl.BlockSpec((2, step, 8, 128), lambda i: (0, i, 0, 0))
    response = pl.BlockSpec((step, 4, 8, 128), lambda i: (i, 0, 0, 0))
    current = pl.BlockSpec((step, 2, 8, 128), lambda i: (i, 2, 0, 0))
    return step, count // step, one, two, response, current


def send(current, blocks, cols, mass, coriolis, start, wind):
    count = cols.shape[0]
    pieces = count // min(count, PIECE)
    one, two = (count, 8, 128), (2, count, 8, 128)
    return pl.pallas_call(
        send_kernel,
        in_specs=[ORDER, pl.BlockSpec(memory_space=pltpu.VMEM)] + [ORDER] * 5,
        out_specs=ORDER,
        out_shape=jax.ShapeDtypeStruct((count, 6, 8, 128), F32),
        scratch_shapes=[
            pltpu.VMEM((2, 128, 512), F32),
            pltpu.VMEM((3, 512, 256), BF16),
            pltpu.VMEM((2, 1024, 128), F32),
            pltpu.VMEM((1024, 512), BF16),
            pltpu.VMEM(one, I32),
            pltpu.VMEM(one, F32),
            pltpu.VMEM(one, F32),
            pltpu.VMEM(two, F32),
            pltpu.VMEM(two, F32),
            pltpu.VMEM((count, 6, 8, 128), F32),
            pltpu.SemaphoreType.DMA((1,)),
            pltpu.SemaphoreType.DMA((5, pieces)),
            pltpu.SemaphoreType.DMA((pieces,)),
        ],
        compiler_params=params(60),
        cost_estimate=cost(10**9, 8 * MIB),
        name="send",
    )(current, blocks, cols, mass, coriolis, start, wind)


def velocity_kernel(response, current_ref, _, out, done):
    done[...] = jnp.zeros((8, 128), F32)
    piece = min(response.shape[0], PIECE)
    tall = 8 * piece
    lane = iota((tall, 128), 1)

    def body(g, carry):
        group = pl.ds(piece * g, piece)
        base_east, base_north, a, t = (response[group, n].reshape(tall, 128) for n in range(4))
        current = [current_ref[group, c].reshape(tall, 128) for c in range(2)]
        east, north = respond(a, t, *current, lane)
        out[0, group] = (base_east + east).reshape(piece, 8, 128)
        out[1, group] = (base_north + north).reshape(piece, 8, 128)
        return carry

    lax.fori_loop(0, response.shape[0] // piece, body, 0)


def velocities(sent, received, after):
    count = sent.shape[0]
    _, grid, _, two, response, current = chunked(count)
    return pl.pallas_call(
        velocity_kernel,
        grid=(grid,),
        in_specs=[response, current, ORDER],
        out_specs=(two, pl.BlockSpec((8, 128), lambda i: (0, 0))),
        out_shape=(jax.ShapeDtypeStruct((2, count, 8, 128), F32), jax.ShapeDtypeStruct((8, 128), F32)),
        compiler_params=params(50),
        cost_estimate=cost(10**7, 4 * MIB),
        name="velocities",
    )(sent, received, after)


def invert_kernel(cols, key, inverse, hot):
    count = cols.shape[0]
    hot[...] = jnp.where(iota((512, 8 * count), 0) == key[...], 1.0, 0.0).astype(BF16)
    lane = iota((8, 1024), 1)
    weights = jnp.where(lane // 128 == iota((8, 1024), 0), lane % 128 + 1, 0).astype(F32).astype(BF16)
    place = iota((128, 128), 0).astype(F32).astype(BF16)
    one, zero = jnp.ones((128, 128), BF16), jnp.zeros((128, 128), BF16)

    def body(i, carry):
        index = cols[i]
        target = jnp.where(index >= 0, (index >> 1) + 64 * (index & 1), -1).astype(F32)
        masks = []
        for s in range(8):
            row = jnp.broadcast_to(target[s : s + 1], (16, 128)).astype(BF16)
            masks.append(jnp.where(place == jnp.concatenate([row] * 8, axis=0), one, zero))
        found = lax.dot_general(
            weights, jnp.concatenate(masks, axis=1), (((1,), (1,)), ((), ())), preferred_element_type=F32
        )
        inverse[i] = found.astype(I32) - 1
        return carry

    lax.fori_loop(0, count, body, 0, unroll=8)


def invert(cols, key):
    count = cols.shape[0]
    return pl.pallas_call(
        invert_kernel,
        out_shape=(jax.ShapeDtypeStruct((count, 8, 128), I32), jax.ShapeDtypeStruct((512, 8 * count), BF16)),
        compiler_params=params(60),
        cost_estimate=cost(10**10, 2 * MIB),
        name="invert",
    )(cols, key)


def stress_kernel(response_in, sent_in, inverse_in, hot_in, *refs):
    planes, side, ends, parts, response, current_ref, inverse, hot, arrived, listed = refs[-10:]
    count = inverse.shape[0]
    piece = min(count, PIECE)

    def transfer(p):
        span = pl.ds(piece * p, piece)
        return (
            pltpu.make_async_copy(response_in.at[span, pl.ds(0, 4)], response.at[span], arrived.at[0, p]),
            pltpu.make_async_copy(sent_in.at[span, pl.ds(4, 2)], current_ref.at[span], arrived.at[1, p]),
        )

    inverse_copy = pltpu.make_async_copy(inverse_in, inverse, listed.at[0])
    hot_copy = pltpu.make_async_copy(hot_in, hot, listed.at[1])
    for p in range(count // piece):
        for copy in transfer(p):
            copy.start()
        if p == 0:
            inverse_copy.start()
    hot_copy.start()
    inverse_copy.wait()
    tall = 8 * piece
    lane = iota((tall, 128), 1)

    def body(g):
        group = pl.ds(piece * g, piece)
        rows = pl.ds(pl.multiple_of(tall * g, tall), tall)
        base_east, base_north, a, t = (response[group, n].reshape(tall, 128) for n in range(4))
        current = [current_ref[group, c].reshape(tall, 128) for c in range(2)]
        east, north = respond(a, t, *current, lane)
        index = inverse[group].reshape(tall, 128)
        inside = jnp.maximum(index, 0)
        for c, drag in enumerate((base_east + east - current[0], base_north + north - current[1])):
            drag = DRAG * drag
            got = jnp.concatenate(
                [lane_gather(drag[8 * i : 8 * i + 8], inside[8 * i : 8 * i + 8]) for i in range(piece)], axis=0
            )
            pieces = split3(jnp.where(index >= 0, got, 0.0))
            for part in range(3):
                parts[part, rows, 128 * c : 128 * c + 128] = pieces[part]

    def move(p, carry):
        for copy in transfer(p):
            copy.wait()
        body(p)
        return carry

    lax.fori_loop(0, count // piece, move, 0)
    hot_copy.wait()
    total = dot(hot[...], parts[0]) + dot(hot[...], parts[1]) + dot(hot[...], parts[2])
    lane = iota((ROWS, 128), 1)
    low = lane < 64
    top = iota((8, 128), 0) < 4
    edge = jnp.zeros((ROWS, 128), F32)
    for c in range(2):
        for py in range(2):
            for h in range(2):
                first = 256 * h + 64 * py
                a = total[first : first + 64, 128 * c : 128 * c + 128]
                b = total[first + 128 : first + 192, 128 * c : 128 * c + 128]
                even = jnp.where(low, a, pltpu.roll(b, 64, 1))
                odd = jnp.where(low, pltpu.roll(a, 64, 1), b)
                for px, value in ((0, even), (1, odd)):
                    plane = 2 * py + px
                    planes[c, plane, :, 128 * h : 128 * h + 128] = value
                    ends[c, plane, :, 128 * h : 128 * h + 128] = jnp.where(top, value[:8], value[56:])
                    item = 4 * c + plane
                    if h == 0:
                        moved = pltpu.roll(value, 8 * item, 1) if item else value
                        edge = jnp.where(lane // 8 == item, moved, edge)
                    else:
                        moved = pltpu.roll(value, (64 + 8 * item + 8) % 128, 1) if item != 7 else value
                        edge = jnp.where(lane // 8 == 8 + item, moved, edge)
    side[...] = edge


def stresses(received, sent, inverse, hot, after):
    count = inverse.shape[0]
    inside = pl.BlockSpec(memory_space=pltpu.VMEM)
    shapes = ((2, 4, ROWS, COLS), (ROWS, 128), (2, 4, 8, COLS))
    return pl.pallas_call(
        stress_kernel,
        in_specs=[ORDER] * (4 + len(after)),
        out_specs=(inside,) * 3,
        out_shape=tuple(jax.ShapeDtypeStruct(shape, F32) for shape in shapes),
        scratch_shapes=[
            pltpu.VMEM((3, 8 * count, 256), BF16),
            pltpu.VMEM((count, 4, 8, 128), F32),
            pltpu.VMEM((count, 2, 8, 128), F32),
            pltpu.VMEM((count, 8, 128), I32),
            pltpu.VMEM((512, 8 * count), BF16),
            pltpu.SemaphoreType.DMA((2, count // min(count, PIECE))),
            pltpu.SemaphoreType.DMA((2,)),
        ],
        compiler_params=params(60),
        cost_estimate=cost(10**9, 4 * MIB),
        name="stresses",
    )(received, sent, inverse, hot, *after)


def widen_kernel(ends, right, left, far_right, far_left, _, up, down):
    lane = iota((8, 128), 1)
    top = iota((8, 128), 0) < 4
    wide_top = iota((8, COLS), 0) < 4
    from_right = jnp.where(top, right[0:8], right[56:64])
    from_left = jnp.where(top, left[0:8], left[56:64])

    def edges(item):
        r = pltpu.roll(from_right, (128 - 8 * item) % 128, 1) if item else from_right
        s = pltpu.roll(from_left, (56 - 8 * item) % 128, 1) if item != 7 else from_left
        return jnp.where(lane < 64, r, s)

    for c in range(2):
        for px in range(2):
            up[2 * c + px, :, 0:COLS], down[2 * c + px, :, 0:COLS] = pack_rows(ends[c, px], ends[c, 2 + px], wide_top)
            up[2 * c + px, :, COLS:XCOLS], down[2 * c + px, :, COLS:XCOLS] = pack_rows(
                edges(4 * c + px), edges(4 * c + 2 + px), top
            )
    for n, edge in enumerate((far_right, far_left)):
        even, odd = (jnp.where(wide_top, edge[py, 0:8], edge[py, 56:64]) for py in range(2))
        up[4 + n, :, 0:COLS], down[4 + n, :, 0:COLS] = pack_rows(even, odd, wide_top)
        up[4 + n, :, COLS:XCOLS] = jnp.zeros((8, 128), F32)
        down[4 + n, :, COLS:XCOLS] = jnp.zeros((8, 128), F32)


def widen(ends, right, left, far_right, far_left, after):
    inside = pl.BlockSpec(memory_space=pltpu.VMEM)
    return pl.pallas_call(
        widen_kernel,
        in_specs=[inside] * 5 + [ORDER],
        out_shape=(jax.ShapeDtypeStruct((6, 8, XCOLS), F32),) * 2,
        compiler_params=params(4),
        cost_estimate=cost(10**5, MIB // 4),
        name="widen",
    )(ends, right, left, far_right, far_left, after)


ARRAYS = 11


def prepare_kernel(
    sea, forcing, weights, excess, mask, planes, left, right, up, down, halves
):
    lane = iota((8, 128), 1)
    low = lane < 64
    order = jnp.where(low, 2 * lane, 2 * lane - 127)
    swapped = jnp.where(low, 2 * lane + 1, 2 * lane - 128)

    def split(t, carry):
        rows = pl.ds(pl.multiple_of(8 * t, 8), 8)
        w = [weights[k, rows, :] for k in range(8)]
        total = ((w[0] + w[1]) + (w[2] + w[3])) + ((w[4] + w[5]) + (w[6] + w[7]))
        ocean = mask[rows, :] > 0
        inverse = jnp.where(ocean, 1.0 / ((1.0 + excess[rows, :]) * total), 0.0)
        arrays = [v * inverse for v in w]
        arrays += [inverse, forcing[rows, :], jnp.where(ocean, sea[rows, :], 0.0)]
        for n, array in enumerate(arrays):
            for h in range(2):
                a = lane_gather(array[:, 256 * h : 256 * h + 128], order)
                b = lane_gather(array[:, 256 * h + 128 : 256 * h + 256], swapped)
                halves[4 * n + h, rows, :] = jnp.where(low, a, b)
                halves[4 * n + 2 + h, rows, :] = pltpu.roll(jnp.where(low, b, a), 64, 1)
        return carry

    lax.fori_loop(0, 2 * ROWS // 8, split, 0)

    def pack(t, carry):
        out_rows = pl.ds(pl.multiple_of(8 * t, 8), 8)
        for py in range(2):
            rows = pl.ds(16 * t + py, 8, stride=2)
            packed = [[jnp.zeros((8, 128), F32)] * 2, [jnp.zeros((8, 128), F32)] * 2]
            for n in range(ARRAYS):
                for px in range(2):
                    for h in range(2):
                        value = halves[4 * n + 2 * px + h, rows, :]
                        planes[n, 2 * py + px, out_rows, 128 * h : 128 * h + 128] = value
                        item = 2 * n + px
                        shift = (8 * (item % 16) + (8 if h else 0)) % 128
                        moved = pltpu.roll(value, shift, 1) if shift else value
                        packed[h][item // 16] = jnp.where(lane // 8 == item % 16, moved, packed[h][item // 16])
            for g in range(2):
                left[py, out_rows, 128 * g : 128 * g + 128] = packed[0][g]
                right[py, out_rows, 128 * g : 128 * g + 128] = packed[1][g]
        return carry

    lax.fori_loop(0, ROWS // 8, pack, 0)
    top = iota((8, 256), 0) < 4
    for n in range(ARRAYS):
        for px in range(2):
            even, odd = (jnp.where(top, planes[n, p, 0:8], planes[n, p, 56:64]) for p in (px, 2 + px))
            up[n, px], down[n, px] = pack_rows(even, odd, top)


def prepare(sea, forcing, weights, excess, mask):
    return pl.pallas_call(
        prepare_kernel,
        out_shape=(
            jax.ShapeDtypeStruct((ARRAYS, 4, ROWS, COLS), F32),
            jax.ShapeDtypeStruct((2, ROWS, 256), F32),
            jax.ShapeDtypeStruct((2, ROWS, 256), F32),
            jax.ShapeDtypeStruct((ARRAYS, 2, 8, COLS), F32),
            jax.ShapeDtypeStruct((ARRAYS, 2, 8, COLS), F32),
        ),
        scratch_shapes=[pltpu.VMEM((4 * ARRAYS, 2 * ROWS, 128), F32)],
        compiler_params=params(60),
        cost_estimate=cost(10**7, 7 * MIB),
        name="prepare",
    )(sea, forcing, weights, excess, mask)


def place_edges(n, p, right, left, lane):
    slot = (2 * n + p % 2) % 16
    r = pltpu.roll(right, (128 - 8 * slot) % 128, 1) if slot else right
    s = pltpu.roll(left, (120 - 8 * slot) % 128, 1) if slot != 15 else left
    return jnp.where(lane < 8, r, jnp.where(lane >= 120, s, 0.0))


def packed_at(n, p):
    group = (2 * n + p % 2) // 16
    return slice(128 * group, 128 * group + 128)


def extend_kernel(planes, right, left, _, out):
    lane = iota((ROWS, 128), 1)
    for n in range(ARRAYS):
        for p in range(4):
            span = packed_at(n, p)
            out[n, p, :, 0:COLS] = planes[n, p]
            out[n, p, :, COLS:XCOLS] = place_edges(n, p, right[p // 2, :, span], left[p // 2, :, span], lane)


def extend(planes, right, left, after):
    inside = pl.BlockSpec(memory_space=pltpu.VMEM)
    return pl.pallas_call(
        extend_kernel,
        in_specs=[inside] * 3 + [ORDER],
        out_shape=jax.ShapeDtypeStruct((ARRAYS, 4, ROWS, XCOLS), F32),
        compiler_params=params(20),
        cost_estimate=cost(10**7, 8 * MIB),
        name="extend",
    )(planes, right, left, after)


def row_shift(value, step):
    return pltpu.roll(value, (-step) % XROWS, 0) if step else value


def col_shift(value, step):
    return pltpu.roll(value, (-step) % XCOLS, 1) if step else value


def neighbour(step, parity):
    return (step + parity) // 2


def sweep_kernel(
    operator, far_below, far_above, stress, right, left, below, above, out, wide, source, field, natural, rim
):
    lane = iota((ROWS, 128), 1)
    top = iota((8, XCOLS), 0) < 4
    for c in range(2):
        for p in range(4):
            item = 4 * c + p
            r = pltpu.roll(right[...], (128 - 8 * item) % 128, 1) if item else right[...]
            s = pltpu.roll(left[...], (56 - 8 * item) % 128, 1) if item != 7 else left[...]
            wide[c, p, 0:ROWS, 0:COLS] = stress[c, p]
            wide[c, p, 0:ROWS, COLS:XCOLS] = jnp.where(lane < 64, r, s)
            wide[c, p, ROWS:XROWS, :] = unpack_rows(p // 2, below[2 * c + p % 2], above[2 * c + p % 2], top)
    corners = [[unpack_rows(py, below[4 + n], above[4 + n], top) for n in range(2)] for py in range(2)]
    for n in range(ARRAYS):
        for p in range(4):
            span = packed_at(n, p)
            far_right, far_left = corners[p // 2]
            rim[n, p, :, 0:COLS] = unpack_rows(p // 2, far_below[n, p % 2], far_above[n, p % 2], top[:, :COLS])
            rim[n, p, :, COLS:XCOLS] = place_edges(n, p, far_right[:, span], far_left[:, span], lane[:8])

    def entry(n, p):
        return jnp.concatenate([operator[n, p], rim[n, p]], axis=0)

    for p in range(4):
        py, px = p // 2, p % 2
        north = wide[1, 2 * py + 1 - px]
        east = wide[0, 2 * (1 - py) + px]
        zonal = col_shift(north, neighbour(1, px)) - col_shift(north, neighbour(-1, px))
        meridional = row_shift(east, neighbour(1, py)) - row_shift(east, neighbour(-1, py))
        source[p] = (entry(9, p) + zonal - meridional) * entry(8, p)
        field[p] = entry(10, p)
    for colour in COLOURS:
        py, px = colour // 2, colour % 2
        value = source[colour]
        for k, (dy, dx) in enumerate(STEPS):
            plane = 2 * (py ^ (dy & 1)) + (px ^ (dx & 1))
            v = field[plane]
            if dy:
                v = row_shift(v, neighbour(dy, py))
            if dx:
                v = col_shift(v, neighbour(dx, px))
            value = value + entry(k, colour) * v
        field[colour] = value
    lane = iota((ROWS, 128), 1)
    even_lane = lane % 2 == 0
    first = lane // 2
    for py in range(2):
        for h in range(2):
            even = field[2 * py, 0:ROWS, 128 * h : 128 * h + 128]
            odd = field[2 * py + 1, 0:ROWS, 128 * h : 128 * h + 128]
            for b in range(2):
                for t in range(ROWS // 8):
                    index = first[:8] + 64 * b
                    e = lane_gather(even[8 * t : 8 * t + 8], index)
                    o = lane_gather(odd[8 * t : 8 * t + 8], index)
                    natural[2 * h + b, pl.ds(16 * t + py, 8, stride=2), :] = jnp.where(even_lane[:8], e, o)
    for k in range(4):
        out[:, 128 * k : 128 * k + 128] = natural[k]


def sweep(*arrays):
    return pl.pallas_call(
        sweep_kernel,
        out_shape=jax.ShapeDtypeStruct((128, 512), F32),
        scratch_shapes=[
            pltpu.VMEM((2, 4, XROWS, XCOLS), F32),
            pltpu.VMEM((4, XROWS, XCOLS), F32),
            pltpu.VMEM((4, XROWS, XCOLS), F32),
            pltpu.VMEM((4, 128, 128), F32),
            pltpu.VMEM((ARRAYS, 4, 8, XCOLS), F32),
        ],
        compiler_params=params(20),
        cost_estimate=cost(10**8, 6 * MIB),
        name="sweep",
    )(*arrays)


AXES = ("zon", "mer")


def exchange(values):
    return lax.all_to_all(values, AXES, split_axis=0, concat_axis=0, tiled=True)


def from_neighbour(values, dz, dm):
    nz, nm = lax.axis_size("zon"), lax.axis_size("mer")
    pairs = [
        (((z + dz) % nz) * nm + m + dm, z * nm + m)
        for z in range(nz)
        for m in range(nm)
        if 0 <= m + dm < nm
    ]
    return lax.ppermute(values, AXES, pairs)


def local(
    sea_level,
    forcing,
    link_weights,
    excess,
    ocean_mask,
    current,
    intersection_block,
    intersection_cols,
    ice_mass,
    coriolis,
    ice_start,
    wind_stress,
):
    blocks = intersection_block[0]
    cols = intersection_cols[0]
    slots = blocks.size
    row, part = blocks >> 2, blocks & 3
    scatter_key = jnp.where(blocks >= 0, part * 128 + (row & 1) * 64 + (row >> 1), -1).reshape(1, slots)
    by_slot = jnp.pad(blocks.T, ((0, 0), (0, 128 - blocks.shape[0])), constant_values=-1)

    sent = send(current, by_slot, cols, ice_mass[0], coriolis[0], ice_start[:, 0], wind_stress[:, 0])
    received = exchange(sent)
    planes, left_edge, right_edge, far_up, far_down = prepare(sea_level, forcing, link_weights, excess, ocean_mask)
    far_right, far_left = from_neighbour(left_edge, 1, 0), from_neighbour(right_edge, -1, 0)
    far_below, far_above = from_neighbour(far_up, 0, 1), from_neighbour(far_down, 0, -1)
    inverse, hot = invert(cols, scatter_key)
    stress, side, ends = stresses(received, sent, inverse, hot, (left_edge,))
    right, left = from_neighbour(side, 1, 0), from_neighbour(side, -1, 0)
    velocity, done = velocities(sent, received, stress)
    up, down = widen(ends, right, left, far_right, far_left, done)
    operator = extend(planes, far_right, far_left, up)
    below, above = from_neighbour(up, 0, 1), from_neighbour(down, 0, -1)
    surface = sweep(operator, far_below, far_above, stress, right, left, below, above)
    return surface, velocity[:, None]


def solution(mesh):
    return jax.shard_map(
        local,
        mesh=mesh,
        in_specs=(
            P("mer", "zon"),
            P("mer", "zon"),
            P(None, "mer", "zon"),
            P("mer", "zon"),
            P("mer", "zon"),
            P(None, "mer", "zon"),
            P(("zon", "mer"), None, None),
            P(("zon", "mer"), None, None, None),
            P(("zon", "mer"), None, None, None),
            P(("zon", "mer"), None, None, None),
            P(None, ("zon", "mer"), None, None, None),
            P(None, ("zon", "mer"), None, None, None),
        ),
        out_specs=(P("mer", "zon"), P(None, ("zon", "mer"), None, None, None)),
        check_vma=False,
    )
```

```python
import jax
import jax.numpy as jnp
from jax import lax
from jax.experimental import pallas as pl
from jax.experimental.pallas import tpu as pltpu
from jax.sharding import PartitionSpec as P

SWEEPS = 2
ICE_SWEEPS = 3
DRAG = 1.0
LINK = 0.5
STEPS = ((0, 1), (0, -1), (1, 0), (-1, 0), (1, 1), (1, -1), (-1, 1), (-1, -1))
COLOURS = (0,) + (1, 2, 3, 2, 1, 0) * SWEEPS
F32, BF16, I32 = jnp.float32, jnp.bfloat16, jnp.int32
MIB = 1 << 20
ROWS, COLS, XROWS, XCOLS = 64, 256, 72, 384


def params(vmem=48):
    return pltpu.CompilerParams(vmem_limit_bytes=vmem * MIB)


def cost(flops, moved):
    return pl.CostEstimate(flops=flops, bytes_accessed=moved, transcendentals=0)


def iota(shape, dim):
    return lax.broadcasted_iota(I32, shape, dim)


def lane_gather(values, index):
    return jnp.take_along_axis(values, index, axis=1, mode="promise_in_bounds")


def split3(values):
    high = values.astype(BF16)
    rest = values - high.astype(F32)
    middle = rest.astype(BF16)
    low = (rest - middle.astype(F32)).astype(BF16)
    return high, middle, low


def half_turn(tile):
    return pltpu.roll(tile, 4, 0)


def pack_rows(even_rows, odd_rows, top):
    return (
        jnp.where(top, even_rows, half_turn(odd_rows)),
        jnp.where(top, half_turn(even_rows), odd_rows),
    )


def unpack_rows(py, below, above, top):
    if py:
        return jnp.where(top, half_turn(below), above)
    return jnp.where(top, below, half_turn(above))


def dot(a, b):
    return jnp.dot(a, b, preferred_element_type=F32)


def beside(values, lane):
    before = jnp.where(lane == 0, 0.0, pltpu.roll(values, 1, 1))
    after = jnp.where(lane == 127, 0.0, pltpu.roll(values, 127, 1))
    return LINK * (before + after)


def turn(a, t, east, north):
    return a * east + t * north, a * north - t * east


def sweep_ice(a, t, east, north, base_east, base_north, lane):
    return turn(a, t, base_east + beside(east, lane), base_north + beside(north, lane))


def respond(a, t, current_east, current_north, lane):
    first_east, first_north = east, north = turn(a, t, current_east, current_north)
    for _ in range(ICE_SWEEPS - 1):
        more_east, more_north = turn(a, t, beside(east, lane), beside(north, lane))
        east, north = first_east + more_east, first_north + more_north
    return east, north


PIECE = 32


def send_kernel(current_in, blocks, *refs):
    ice_in, sent, (current, table, rows, hot), ice, out, (first, arrived, gone) = (
        refs[:5],
        refs[5],
        refs[6:10],
        refs[10:15],
        refs[15],
        refs[16:],
    )
    count = out.shape[0]
    piece = min(count, PIECE)
    current_copy = pltpu.make_async_copy(current_in, current, first.at[0])
    current_copy.start()

    def arrive(p):
        span = pl.ds(piece * p, piece)
        return [
            pltpu.make_async_copy(source.at[span], target.at[span], arrived.at[n, p])
            if n < 3
            else pltpu.make_async_copy(source.at[:, span], target.at[:, span], arrived.at[n, p])
            for n, (source, target) in enumerate(zip(ice_in, ice))
        ]

    def leave(p):
        span = pl.ds(piece * p, piece)
        return pltpu.make_async_copy(out.at[span], sent.at[span], gone.at[p])

    for p in range(count // piece):
        for copy in arrive(p):
            copy.start()

    key = jnp.where(blocks[...] >= 0, (blocks[...] & 3) * 128 + (blocks[...] >> 2), -1)
    key = jnp.transpose(jnp.concatenate([key, jnp.zeros((120, 128), I32)], axis=0))
    place = iota((128, 512), 1)
    for s in range(8):
        hot[128 * s : 128 * s + 128] = jnp.where(key[:, s : s + 1] == place, 1.0, 0.0).astype(BF16)
    current_copy.wait()
    for c in range(2):
        for k in range(4):
            parts = split3(current[c, :, 128 * k : 128 * k + 128])
            for part in range(3):
                first = 512 * part + 128 * k
                table[first : first + 128, 128 * c : 128 * c + 128] = parts[part]
    for q in range(4):
        span = slice(256 * q, 256 * q + 256)
        got = dot(jnp.concatenate([hot[span]] * 3, axis=1), table[...])
        rows[0, span] = got[:, :128]
        rows[1, span] = got[:, 128:]

    tall = 8 * piece
    lane = iota((tall, 128), 1)
    cols, mass_ref, coriolis_ref, start_ref, wind_ref = ice

    def body(g):
        group = pl.ds(piece * g, piece)
        index = cols[group].reshape(tall, 128)
        inside = jnp.maximum(index, 0)
        for c in range(2):
            got = jnp.concatenate(
                [
                    lane_gather(rows[c, pl.ds(piece * g + i, 8, stride=128), :], inside[8 * i : 8 * i + 8])
                    for i in range(piece)
                ],
                axis=0,
            )
            out[group, 4 + c] = jnp.where(index >= 0, DRAG * got, 0.0).reshape(piece, 8, 128)
        mass = mass_ref[group].reshape(tall, 128)
        a = mass + DRAG + 2.0 * LINK
        t = coriolis_ref[group].reshape(tall, 128) * mass
        inverse = 1.0 / (a * a + t * t)
        a = a * inverse
        t = t * inverse
        east = start_ref[0, group].reshape(tall, 128)
        north = start_ref[1, group].reshape(tall, 128)
        base_east = mass * east + wind_ref[0, group].reshape(tall, 128)
        base_north = mass * north + wind_ref[1, group].reshape(tall, 128)
        for _ in range(ICE_SWEEPS):
            east, north = sweep_ice(a, t, east, north, base_east, base_north, lane)
        for n, value in enumerate((east, north, a, t)):
            out[group, n] = value.reshape(piece, 8, 128)

    def move(p, carry):
        for copy in arrive(p):
            copy.wait()
        body(p)
        leave(p).start()
        return carry

    lax.fori_loop(0, count // piece, move, 0)
    for p in range(count // piece):
        leave(p).wait()


ORDER = pl.BlockSpec(memory_space=pl.ANY)


def chunked(count):
    step = min(count, 64)
    one = pl.BlockSpec((step, 8, 128), lambda i: (i, 0, 0))
    two = pl.BlockSpec((2, step, 8, 128), lambda i: (0, i, 0, 0))
    response = pl.BlockSpec((step, 4, 8, 128), lambda i: (i, 0, 0, 0))
    current = pl.BlockSpec((step, 2, 8, 128), lambda i: (i, 2, 0, 0))
    return step, count // step, one, two, response, current


def send(current, blocks, cols, mass, coriolis, start, wind):
    count = cols.shape[0]
    pieces = count // min(count, PIECE)
    one, two = (count, 8, 128), (2, count, 8, 128)
    return pl.pallas_call(
        send_kernel,
        in_specs=[ORDER, pl.BlockSpec(memory_space=pltpu.VMEM)] + [ORDER] * 5,
        out_specs=ORDER,
        out_shape=jax.ShapeDtypeStruct((count, 6, 8, 128), F32),
        scratch_shapes=[
            pltpu.VMEM((2, 128, 512), F32),
            pltpu.VMEM((1536, 256), BF16),
            pltpu.VMEM((2, 1024, 128), F32),
            pltpu.VMEM((1024, 512), BF16),
            pltpu.VMEM(one, I32),
            pltpu.VMEM(one, F32),
            pltpu.VMEM(one, F32),
            pltpu.VMEM(two, F32),
            pltpu.VMEM(two, F32),
            pltpu.VMEM((count, 6, 8, 128), F32),
            pltpu.SemaphoreType.DMA((1,)),
            pltpu.SemaphoreType.DMA((5, pieces)),
            pltpu.SemaphoreType.DMA((pieces,)),
        ],
        compiler_params=params(60),
        cost_estimate=cost(10**9, 8 * MIB),
        name="send",
    )(current, blocks, cols, mass, coriolis, start, wind)


def velocity_kernel(response, current_ref, _, out):
    piece = min(response.shape[0], PIECE)
    tall = 8 * piece
    lane = iota((tall, 128), 1)

    def body(g, carry):
        group = pl.ds(piece * g, piece)
        base_east, base_north, a, t = (response[group, n].reshape(tall, 128) for n in range(4))
        current = [current_ref[group, c].reshape(tall, 128) for c in range(2)]
        east, north = respond(a, t, *current, lane)
        out[0, group] = (base_east + east).reshape(piece, 8, 128)
        out[1, group] = (base_north + north).reshape(piece, 8, 128)
        return carry

    lax.fori_loop(0, response.shape[0] // piece, body, 0)


def velocities(sent, received, after):
    count = sent.shape[0]
    _, grid, _, two, response, current = chunked(count)
    return pl.pallas_call(
        velocity_kernel,
        grid=(grid,),
        in_specs=[response, current, ORDER],
        out_specs=two,
        out_shape=jax.ShapeDtypeStruct((2, count, 8, 128), F32),
        compiler_params=params(50),
        cost_estimate=cost(10**7, 4 * MIB),
        name="velocities",
    )(sent, received, after)


def invert_kernel(cols, key, inverse, hot):
    count = cols.shape[0]
    hot[...] = jnp.where(iota((512, 8 * count), 0) == key[...], 1.0, 0.0).astype(BF16)
    lane = iota((8, 1024), 1)
    weights = jnp.where(lane // 128 == iota((8, 1024), 0), lane % 128 + 1, 0).astype(F32).astype(BF16)
    place = iota((128, 128), 0).astype(F32).astype(BF16)
    one, zero = jnp.ones((128, 128), BF16), jnp.zeros((128, 128), BF16)

    def body(i, carry):
        index = cols[i]
        target = jnp.where(index >= 0, (index >> 1) + 64 * (index & 1), -1).astype(F32)
        masks = []
        for s in range(8):
            row = jnp.broadcast_to(target[s : s + 1], (16, 128)).astype(BF16)
            masks.append(jnp.where(place == jnp.concatenate([row] * 8, axis=0), one, zero))
        found = lax.dot_general(
            weights, jnp.concatenate(masks, axis=1), (((1,), (1,)), ((), ())), preferred_element_type=F32
        )
        inverse[i] = found.astype(I32) - 1
        return carry

    lax.fori_loop(0, count, body, 0, unroll=8)


def invert(cols, key):
    count = cols.shape[0]
    return pl.pallas_call(
        invert_kernel,
        out_shape=(jax.ShapeDtypeStruct((count, 8, 128), I32), jax.ShapeDtypeStruct((512, 8 * count), BF16)),
        compiler_params=params(60),
        cost_estimate=cost(10**10, 2 * MIB),
        name="invert",
    )(cols, key)


def stress_kernel(response_in, sent_in, inverse_in, hot_in, *refs):
    planes, side, up, down, parts, response, current_ref, inverse, hot, arrived, listed = refs[-11:]
    count = inverse.shape[0]
    piece = min(count, PIECE)

    def transfer(p):
        span = pl.ds(piece * p, piece)
        return (
            pltpu.make_async_copy(response_in.at[span, pl.ds(0, 4)], response.at[span], arrived.at[0, p]),
            pltpu.make_async_copy(sent_in.at[span, pl.ds(4, 2)], current_ref.at[span], arrived.at[1, p]),
        )

    inverse_copy = pltpu.make_async_copy(inverse_in, inverse, listed.at[0])
    hot_copy = pltpu.make_async_copy(hot_in, hot, listed.at[1])
    for p in range(count // piece):
        for copy in transfer(p):
            copy.start()
        if p == 0:
            inverse_copy.start()
    hot_copy.start()
    inverse_copy.wait()
    tall = 8 * piece
    lane = iota((tall, 128), 1)

    def body(g):
        group = pl.ds(piece * g, piece)
        base_east, base_north, a, t = (response[group, n].reshape(tall, 128) for n in range(4))
        current = [current_ref[group, c].reshape(tall, 128) for c in range(2)]
        east, north = respond(a, t, *current, lane)
        index = inverse[group].reshape(tall, 128)
        inside = jnp.maximum(index, 0)
        for c, drag in enumerate((base_east + east - current[0], base_north + north - current[1])):
            drag = DRAG * drag
            got = jnp.concatenate(
                [lane_gather(drag[8 * i : 8 * i + 8], inside[8 * i : 8 * i + 8]) for i in range(piece)], axis=0
            )
            pieces = split3(jnp.where(index >= 0, got, 0.0))
            for part in range(3):
                rows = pl.ds(pl.multiple_of(8 * count * part + tall * g, tall), tall)
                parts[rows, 128 * c : 128 * c + 128] = pieces[part]

    def move(p, carry):
        for copy in transfer(p):
            copy.wait()
        body(p)
        return carry

    lax.fori_loop(0, count // piece, move, 0)
    hot_copy.wait()
    total = dot(jnp.concatenate([hot[...]] * 3, axis=1), parts[...])
    lane = iota((ROWS, 128), 1)
    low = lane < 64
    top = iota((8, 128), 0) < 4
    edge = jnp.zeros((ROWS, 128), F32)
    for c in range(2):
        ends = {}
        for py in range(2):
            for h in range(2):
                first = 256 * h + 64 * py
                a = total[first : first + 64, 128 * c : 128 * c + 128]
                b = total[first + 128 : first + 192, 128 * c : 128 * c + 128]
                even = jnp.where(low, a, pltpu.roll(b, 64, 1))
                odd = jnp.where(low, pltpu.roll(a, 64, 1), b)
                for px, value in ((0, even), (1, odd)):
                    plane = 2 * py + px
                    planes[c, plane, :, 128 * h : 128 * h + 128] = value
                    ends[plane, h] = jnp.where(top, value[:8], value[56:])
                    item = 4 * c + plane
                    if h == 0:
                        moved = pltpu.roll(value, 8 * item, 1) if item else value
                        edge = jnp.where(lane // 8 == item, moved, edge)
                    else:
                        moved = pltpu.roll(value, (64 + 8 * item + 8) % 128, 1) if item != 7 else value
                        edge = jnp.where(lane // 8 == 8 + item, moved, edge)
        for px in range(2):
            for h in range(2):
                span = slice(128 * h, 128 * h + 128)
                up[2 * c + px, :, span], down[2 * c + px, :, span] = pack_rows(ends[px, h], ends[2 + px, h], top)
    side[...] = edge


def stresses(received, sent, inverse, hot, after):
    count = inverse.shape[0]
    inside = pl.BlockSpec(memory_space=pltpu.VMEM)
    shapes = ((2, 4, ROWS, COLS), (ROWS, 128), (4, 8, COLS), (4, 8, COLS))
    return pl.pallas_call(
        stress_kernel,
        in_specs=[ORDER] * (4 + len(after)),
        out_specs=(inside,) * 4,
        out_shape=tuple(jax.ShapeDtypeStruct(shape, F32) for shape in shapes),
        scratch_shapes=[
            pltpu.VMEM((24 * count, 256), BF16),
            pltpu.VMEM((count, 4, 8, 128), F32),
            pltpu.VMEM((count, 2, 8, 128), F32),
            pltpu.VMEM((count, 8, 128), I32),
            pltpu.VMEM((512, 8 * count), BF16),
            pltpu.SemaphoreType.DMA((2, count // min(count, PIECE))),
            pltpu.SemaphoreType.DMA((2,)),
        ],
        compiler_params=params(60),
        cost_estimate=cost(10**9, 4 * MIB),
        name="stresses",
    )(received, sent, inverse, hot, *after)


MESSAGE = XROWS + 32


def widen_kernel(side, below, above, far_below, far_above, to_left, to_right):
    lane = iota((8, 128), 1)
    top = iota((8, COLS), 0) < 4
    edge = jnp.zeros((8, 128), F32)
    for c in range(2):
        for p in range(4):
            item = 4 * c + p
            rows = unpack_rows(p // 2, below[2 * c + p % 2], above[2 * c + p % 2], top)
            first = pltpu.roll(rows[:, :128], 8 * item, 1) if item else rows[:, :128]
            last = pltpu.roll(rows[:, 128:], (72 + 8 * item) % 128, 1) if item != 7 else rows[:, 128:]
            edge = jnp.where(lane // 8 == item, first, jnp.where(lane // 8 == 8 + item, last, edge))
    corners = [jnp.zeros((8, 128), F32)] * 8
    for n in range(ARRAYS):
        for p in range(4):
            group, slot = divmod(2 * n + p % 2, 16)
            rows = unpack_rows(p // 2, far_below[n, p % 2], far_above[n, p % 2], top)
            first = pltpu.roll(rows[:, :128], 8 * slot, 1) if slot else rows[:, :128]
            last = pltpu.roll(rows[:, 128:], (8 * slot + 8) % 128, 1) if slot != 15 else rows[:, 128:]
            at = 2 * (p // 2) + group
            corners[at] = jnp.where(lane // 8 == slot, first, corners[at])
            corners[4 + at] = jnp.where(lane // 8 == slot, last, corners[4 + at])
    for n, out in enumerate((to_left, to_right)):
        out[0:ROWS] = side[...]
        out[ROWS:XROWS] = edge
        for at in range(4):
            out[XROWS + 8 * at : XROWS + 8 * at + 8] = corners[4 * n + at]


def widen(*arrays):
    return pl.pallas_call(
        widen_kernel,
        out_shape=(jax.ShapeDtypeStruct((MESSAGE, 128), F32),) * 2,
        compiler_params=params(4),
        cost_estimate=cost(10**5, MIB // 2),
        name="widen",
    )(*arrays)


ARRAYS = 11


def prepare_kernel(
    sea, forcing, weights, excess, mask, planes, left, right, up, down, halves
):
    lane = iota((8, 128), 1)
    low = lane < 64
    order = jnp.where(low, 2 * lane, 2 * lane - 127)
    swapped = jnp.where(low, 2 * lane + 1, 2 * lane - 128)

    def split(t, carry):
        rows = pl.ds(pl.multiple_of(8 * t, 8), 8)
        w = [weights[k, rows, :] for k in range(8)]
        total = ((w[0] + w[1]) + (w[2] + w[3])) + ((w[4] + w[5]) + (w[6] + w[7]))
        ocean = mask[rows, :] > 0
        inverse = jnp.where(ocean, 1.0 / ((1.0 + excess[rows, :]) * total), 0.0)
        arrays = [v * inverse for v in w]
        arrays += [inverse, forcing[rows, :], jnp.where(ocean, sea[rows, :], 0.0)]
        for n, array in enumerate(arrays):
            for h in range(2):
                a = lane_gather(array[:, 256 * h : 256 * h + 128], order)
                b = lane_gather(array[:, 256 * h + 128 : 256 * h + 256], swapped)
                halves[4 * n + h, rows, :] = jnp.where(low, a, b)
                halves[4 * n + 2 + h, rows, :] = pltpu.roll(jnp.where(low, b, a), 64, 1)
        return carry

    lax.fori_loop(0, 2 * ROWS // 8, split, 0)

    def pack(t, carry):
        out_rows = pl.ds(pl.multiple_of(8 * t, 8), 8)
        for py in range(2):
            rows = pl.ds(16 * t + py, 8, stride=2)
            packed = [[jnp.zeros((8, 128), F32)] * 2, [jnp.zeros((8, 128), F32)] * 2]
            for n in range(ARRAYS):
                for px in range(2):
                    for h in range(2):
                        value = halves[4 * n + 2 * px + h, rows, :]
                        planes[n, 2 * py + px, out_rows, 128 * h : 128 * h + 128] = value
                        item = 2 * n + px
                        shift = (8 * (item % 16) + (8 if h else 0)) % 128
                        moved = pltpu.roll(value, shift, 1) if shift else value
                        packed[h][item // 16] = jnp.where(lane // 8 == item % 16, moved, packed[h][item // 16])
            for g in range(2):
                left[py, out_rows, 128 * g : 128 * g + 128] = packed[0][g]
                right[py, out_rows, 128 * g : 128 * g + 128] = packed[1][g]
        return carry

    lax.fori_loop(0, ROWS // 8, pack, 0)
    top = iota((8, 256), 0) < 4
    for n in range(ARRAYS):
        for px in range(2):
            even, odd = (jnp.where(top, planes[n, p, 0:8], planes[n, p, 56:64]) for p in (px, 2 + px))
            up[n, px], down[n, px] = pack_rows(even, odd, top)


def prepare(sea, forcing, weights, excess, mask):
    return pl.pallas_call(
        prepare_kernel,
        out_shape=(
            jax.ShapeDtypeStruct((ARRAYS, 4, ROWS, COLS), F32),
            jax.ShapeDtypeStruct((2, ROWS, 256), F32),
            jax.ShapeDtypeStruct((2, ROWS, 256), F32),
            jax.ShapeDtypeStruct((ARRAYS, 2, 8, COLS), F32),
            jax.ShapeDtypeStruct((ARRAYS, 2, 8, COLS), F32),
        ),
        scratch_shapes=[pltpu.VMEM((4 * ARRAYS, 2 * ROWS, 128), F32)],
        compiler_params=params(60),
        cost_estimate=cost(10**7, 7 * MIB),
        name="prepare",
    )(sea, forcing, weights, excess, mask)


def place_edges(n, p, right, left, lane):
    slot = (2 * n + p % 2) % 16
    r = pltpu.roll(right, (128 - 8 * slot) % 128, 1) if slot else right
    s = pltpu.roll(left, (120 - 8 * slot) % 128, 1) if slot != 15 else left
    return jnp.where(lane < 8, r, jnp.where(lane >= 120, s, 0.0))


def packed_at(n, p):
    group = (2 * n + p % 2) // 16
    return slice(128 * group, 128 * group + 128)


def extend_kernel(planes, right, left, _, out):
    lane = iota((ROWS, 128), 1)
    for n in range(ARRAYS):
        for p in range(4):
            span = packed_at(n, p)
            out[n, p, :, 0:COLS] = planes[n, p]
            out[n, p, :, COLS:XCOLS] = place_edges(n, p, right[p // 2, :, span], left[p // 2, :, span], lane)


def extend(planes, right, left, after):
    inside = pl.BlockSpec(memory_space=pltpu.VMEM)
    return pl.pallas_call(
        extend_kernel,
        in_specs=[inside] * 3 + [ORDER],
        out_shape=jax.ShapeDtypeStruct((ARRAYS, 4, ROWS, XCOLS), F32),
        compiler_params=params(20),
        cost_estimate=cost(10**7, 8 * MIB),
        name="extend",
    )(planes, right, left, after)


def row_shift(value, step):
    return pltpu.roll(value, (-step) % XROWS, 0) if step else value


def col_shift(value, step):
    return pltpu.roll(value, (-step) % XCOLS, 1) if step else value


def neighbour(step, parity):
    return (step + parity) // 2


def sweep_kernel(
    operator, far_below, far_above, stress, right, left, below, above, out, wide, source, field, natural, rim
):
    lane = iota((XROWS, 128), 1)
    top = iota((8, COLS), 0) < 4
    from_right, from_left = right[0:XROWS], left[0:XROWS]
    for c in range(2):
        for p in range(4):
            item = 4 * c + p
            r = pltpu.roll(from_right, (128 - 8 * item) % 128, 1) if item else from_right
            s = pltpu.roll(from_left, (56 - 8 * item) % 128, 1) if item != 7 else from_left
            wide[c, p, 0:ROWS, 0:COLS] = stress[c, p]
            wide[c, p, ROWS:XROWS, 0:COLS] = unpack_rows(p // 2, below[2 * c + p % 2], above[2 * c + p % 2], top)
            wide[c, p, :, COLS:XCOLS] = jnp.where(lane < 64, r, s)
    for n in range(ARRAYS):
        for p in range(4):
            first = XROWS + 8 * (2 * (p // 2) + (2 * n + p % 2) // 16)
            rim[n, p, :, 0:COLS] = unpack_rows(p // 2, far_below[n, p % 2], far_above[n, p % 2], top)
            rim[n, p, :, COLS:XCOLS] = place_edges(n, p, right[first : first + 8], left[first : first + 8], lane[:8])

    def entry(n, p):
        return jnp.concatenate([operator[n, p], rim[n, p]], axis=0)

    for p in range(4):
        py, px = p // 2, p % 2
        north = wide[1, 2 * py + 1 - px]
        east = wide[0, 2 * (1 - py) + px]
        zonal = col_shift(north, neighbour(1, px)) - col_shift(north, neighbour(-1, px))
        meridional = row_shift(east, neighbour(1, py)) - row_shift(east, neighbour(-1, py))
        source[p] = (entry(9, p) + zonal - meridional) * entry(8, p)
        field[p] = entry(10, p)
    for colour in COLOURS:
        py, px = colour // 2, colour % 2
        value = source[colour]
        for k, (dy, dx) in enumerate(STEPS):
            plane = 2 * (py ^ (dy & 1)) + (px ^ (dx & 1))
            v = field[plane]
            if dy:
                v = row_shift(v, neighbour(dy, py))
            if dx:
                v = col_shift(v, neighbour(dx, px))
            value = value + entry(k, colour) * v
        field[colour] = value
    lane = iota((ROWS, 128), 1)
    even_lane = lane % 2 == 0
    first = lane // 2
    for py in range(2):
        for h in range(2):
            even = field[2 * py, 0:ROWS, 128 * h : 128 * h + 128]
            odd = field[2 * py + 1, 0:ROWS, 128 * h : 128 * h + 128]
            for b in range(2):
                for t in range(ROWS // 8):
                    index = first[:8] + 64 * b
                    e = lane_gather(even[8 * t : 8 * t + 8], index)
                    o = lane_gather(odd[8 * t : 8 * t + 8], index)
                    natural[2 * h + b, pl.ds(16 * t + py, 8, stride=2), :] = jnp.where(even_lane[:8], e, o)
    for k in range(4):
        out[:, 128 * k : 128 * k + 128] = natural[k]


def sweep(*arrays):
    return pl.pallas_call(
        sweep_kernel,
        out_shape=jax.ShapeDtypeStruct((128, 512), F32),
        scratch_shapes=[
            pltpu.VMEM((2, 4, XROWS, XCOLS), F32),
            pltpu.VMEM((4, XROWS, XCOLS), F32),
            pltpu.VMEM((4, XROWS, XCOLS), F32),
            pltpu.VMEM((4, 128, 128), F32),
            pltpu.VMEM((ARRAYS, 4, 8, XCOLS), F32),
        ],
        compiler_params=params(20),
        cost_estimate=cost(10**8, 6 * MIB),
        name="sweep",
    )(*arrays)


AXES = ("zon", "mer")


def exchange(values):
    return lax.all_to_all(values, AXES, split_axis=0, concat_axis=0, tiled=True)


def from_neighbour(values, dz, dm):
    nz, nm = lax.axis_size("zon"), lax.axis_size("mer")
    pairs = [
        (((z + dz) % nz) * nm + m + dm, z * nm + m)
        for z in range(nz)
        for m in range(nm)
        if 0 <= m + dm < nm
    ]
    return lax.ppermute(values, AXES, pairs)


def local(
    sea_level,
    forcing,
    link_weights,
    excess,
    ocean_mask,
    current,
    intersection_block,
    intersection_cols,
    ice_mass,
    coriolis,
    ice_start,
    wind_stress,
):
    blocks = intersection_block[0]
    cols = intersection_cols[0]
    slots = blocks.size
    row, part = blocks >> 2, blocks & 3
    scatter_key = jnp.where(blocks >= 0, part * 128 + (row & 1) * 64 + (row >> 1), -1).reshape(1, slots)
    by_slot = jnp.pad(blocks.T, ((0, 0), (0, 128 - blocks.shape[0])), constant_values=-1)

    sent = send(current, by_slot, cols, ice_mass[0], coriolis[0], ice_start[:, 0], wind_stress[:, 0])
    received = exchange(sent)
    planes, left_edge, right_edge, far_up, far_down = prepare(sea_level, forcing, link_weights, excess, ocean_mask)
    far_right, far_left = from_neighbour(left_edge, 1, 0), from_neighbour(right_edge, -1, 0)
    far_below, far_above = from_neighbour(far_up, 0, 1), from_neighbour(far_down, 0, -1)
    inverse, hot = invert(cols, scatter_key)
    stress, side, up, down = stresses(received, sent, inverse, hot, (left_edge,))
    below, above = from_neighbour(up, 0, 1), from_neighbour(down, 0, -1)
    to_left, to_right = widen(side, below, above, far_below, far_above)
    right, left = from_neighbour(to_left, 1, 0), from_neighbour(to_right, -1, 0)
    velocity = velocities(sent, received, to_left)
    operator = extend(planes, far_right, far_left, to_left)
    surface = sweep(operator, far_below, far_above, stress, right, left, below, above)
    return surface, velocity[:, None]


def solution(mesh):
    return jax.shard_map(
        local,
        mesh=mesh,
        in_specs=(
            P("mer", "zon"),
            P("mer", "zon"),
            P(None, "mer", "zon"),
            P("mer", "zon"),
            P("mer", "zon"),
            P(None, "mer", "zon"),
            P(("zon", "mer"), None, None),
            P(("zon", "mer"), None, None, None),
            P(("zon", "mer"), None, None, None),
            P(("zon", "mer"), None, None, None),
            P(None, ("zon", "mer"), None, None, None),
            P(None, ("zon", "mer"), None, None, None),
        ),
        out_specs=(P("mer", "zon"), P(None, ("zon", "mer"), None, None, None)),
        check_vma=False,
    )
```

```python
import jax
import jax.numpy as jnp
from jax import lax
from jax.experimental import pallas as pl
from jax.experimental.pallas import tpu as pltpu
from jax.sharding import PartitionSpec as P

SWEEPS = 2
ICE_SWEEPS = 3
DRAG = 1.0
LINK = 0.5
STEPS = ((0, 1), (0, -1), (1, 0), (-1, 0), (1, 1), (1, -1), (-1, 1), (-1, -1))
COLOURS = (0,) + (1, 2, 3, 2, 1, 0) * SWEEPS
F32, BF16, I32 = jnp.float32, jnp.bfloat16, jnp.int32
MIB = 1 << 20
ROWS, COLS, XROWS, XCOLS = 64, 256, 72, 384


def params(vmem=48):
    return pltpu.CompilerParams(vmem_limit_bytes=vmem * MIB)


def cost(flops, moved):
    return pl.CostEstimate(flops=flops, bytes_accessed=moved, transcendentals=0)


def iota(shape, dim):
    return lax.broadcasted_iota(I32, shape, dim)


def lane_gather(values, index):
    return jnp.take_along_axis(values, index, axis=1, mode="promise_in_bounds")


def split3(values):
    high = values.astype(BF16)
    rest = values - high.astype(F32)
    middle = rest.astype(BF16)
    low = (rest - middle.astype(F32)).astype(BF16)
    return high, middle, low


def half_turn(tile):
    return pltpu.roll(tile, 4, 0)


def pack_rows(even_rows, odd_rows, top):
    return (
        jnp.where(top, even_rows, half_turn(odd_rows)),
        jnp.where(top, half_turn(even_rows), odd_rows),
    )


def unpack_rows(py, below, above, top):
    if py:
        return jnp.where(top, half_turn(below), above)
    return jnp.where(top, below, half_turn(above))


def dot(a, b):
    return jnp.dot(a, b, preferred_element_type=F32)


def beside(values, lane):
    before = jnp.where(lane == 0, 0.0, pltpu.roll(values, 1, 1))
    after = jnp.where(lane == 127, 0.0, pltpu.roll(values, 127, 1))
    return LINK * (before + after)


def turn(a, t, east, north):
    return a * east + t * north, a * north - t * east


def sweep_ice(a, t, east, north, base_east, base_north, lane):
    return turn(a, t, base_east + beside(east, lane), base_north + beside(north, lane))


def respond(a, t, current_east, current_north, lane):
    first_east, first_north = east, north = turn(a, t, current_east, current_north)
    for _ in range(ICE_SWEEPS - 1):
        more_east, more_north = turn(a, t, beside(east, lane), beside(north, lane))
        east, north = first_east + more_east, first_north + more_north
    return east, north


PIECE = 32


def send_kernel(current_in, blocks, *refs):
    ice_in, sent, (current, table, rows, hot), ice, out, (first, arrived, gone) = (
        refs[:5],
        refs[5],
        refs[6:10],
        refs[10:15],
        refs[15],
        refs[16:],
    )
    count = out.shape[0]
    piece = min(count, PIECE)
    current_copy = pltpu.make_async_copy(current_in, current, first.at[0])
    current_copy.start()

    def arrive(p):
        span = pl.ds(piece * p, piece)
        return [
            pltpu.make_async_copy(source.at[span], target.at[span], arrived.at[n, p])
            if n < 3
            else pltpu.make_async_copy(source.at[:, span], target.at[:, span], arrived.at[n, p])
            for n, (source, target) in enumerate(zip(ice_in, ice))
        ]

    def leave(p):
        span = pl.ds(piece * p, piece)
        return pltpu.make_async_copy(out.at[span], sent.at[span], gone.at[p])

    for p in range(count // piece):
        for copy in arrive(p):
            copy.start()

    key = jnp.where(blocks[...] >= 0, (blocks[...] & 3) * 128 + (blocks[...] >> 2), -1)
    key = jnp.transpose(jnp.concatenate([key, jnp.zeros((120, 128), I32)], axis=0))
    place = iota((128, 512), 1)
    for s in range(8):
        hot[128 * s : 128 * s + 128] = jnp.where(key[:, s : s + 1] == place, 1.0, 0.0).astype(BF16)
    current_copy.wait()
    for c in range(2):
        for k in range(4):
            parts = split3(current[c, :, 128 * k : 128 * k + 128])
            for part in range(3):
                first = 512 * part + 128 * k
                table[first : first + 128, 128 * c : 128 * c + 128] = parts[part]
    for q in range(4):
        span = slice(256 * q, 256 * q + 256)
        got = dot(jnp.concatenate([hot[span]] * 3, axis=1), table[...])
        rows[0, span] = got[:, :128]
        rows[1, span] = got[:, 128:]

    tall = 8 * piece
    lane = iota((tall, 128), 1)
    cols, mass_ref, coriolis_ref, start_ref, wind_ref = ice

    def body(g):
        group = pl.ds(piece * g, piece)
        index = cols[group].reshape(tall, 128)
        inside = jnp.maximum(index, 0)
        for c in range(2):
            got = jnp.concatenate(
                [
                    lane_gather(rows[c, pl.ds(piece * g + i, 8, stride=128), :], inside[8 * i : 8 * i + 8])
                    for i in range(piece)
                ],
                axis=0,
            )
            out[group, 4 + c] = jnp.where(index >= 0, DRAG * got, 0.0).reshape(piece, 8, 128)
        mass = mass_ref[group].reshape(tall, 128)
        a = mass + DRAG + 2.0 * LINK
        t = coriolis_ref[group].reshape(tall, 128) * mass
        inverse = 1.0 / (a * a + t * t)
        a = a * inverse
        t = t * inverse
        east = start_ref[0, group].reshape(tall, 128)
        north = start_ref[1, group].reshape(tall, 128)
        base_east = mass * east + wind_ref[0, group].reshape(tall, 128)
        base_north = mass * north + wind_ref[1, group].reshape(tall, 128)
        for _ in range(ICE_SWEEPS):
            east, north = sweep_ice(a, t, east, north, base_east, base_north, lane)
        for n, value in enumerate((east, north, a, t)):
            out[group, n] = value.reshape(piece, 8, 128)

    def move(p, carry):
        for copy in arrive(p):
            copy.wait()
        body(p)
        leave(p).start()
        return carry

    lax.fori_loop(0, count // piece, move, 0)
    for p in range(count // piece):
        leave(p).wait()


ORDER = pl.BlockSpec(memory_space=pl.ANY)


def chunked(count):
    step = min(count, 64)
    one = pl.BlockSpec((step, 8, 128), lambda i: (i, 0, 0))
    two = pl.BlockSpec((2, step, 8, 128), lambda i: (0, i, 0, 0))
    response = pl.BlockSpec((step, 4, 8, 128), lambda i: (i, 0, 0, 0))
    current = pl.BlockSpec((step, 2, 8, 128), lambda i: (i, 2, 0, 0))
    return step, count // step, one, two, response, current


def send(current, blocks, cols, mass, coriolis, start, wind):
    count = cols.shape[0]
    pieces = count // min(count, PIECE)
    one, two = (count, 8, 128), (2, count, 8, 128)
    return pl.pallas_call(
        send_kernel,
        in_specs=[ORDER, pl.BlockSpec(memory_space=pltpu.VMEM)] + [ORDER] * 5,
        out_specs=ORDER,
        out_shape=jax.ShapeDtypeStruct((count, 6, 8, 128), F32),
        scratch_shapes=[
            pltpu.VMEM((2, 128, 512), F32),
            pltpu.VMEM((1536, 256), BF16),
            pltpu.VMEM((2, 1024, 128), F32),
            pltpu.VMEM((1024, 512), BF16),
            pltpu.VMEM(one, I32),
            pltpu.VMEM(one, F32),
            pltpu.VMEM(one, F32),
            pltpu.VMEM(two, F32),
            pltpu.VMEM(two, F32),
            pltpu.VMEM((count, 6, 8, 128), F32),
            pltpu.SemaphoreType.DMA((1,)),
            pltpu.SemaphoreType.DMA((5, pieces)),
            pltpu.SemaphoreType.DMA((pieces,)),
        ],
        compiler_params=params(60),
        cost_estimate=cost(10**9, 8 * MIB),
        name="send",
    )(current, blocks, cols, mass, coriolis, start, wind)


def velocity_kernel(response, current_ref, _, out):
    piece = min(response.shape[0], PIECE)
    tall = 8 * piece
    lane = iota((tall, 128), 1)

    def body(g, carry):
        group = pl.ds(piece * g, piece)
        base_east, base_north, a, t = (response[group, n].reshape(tall, 128) for n in range(4))
        current = [current_ref[group, c].reshape(tall, 128) for c in range(2)]
        east, north = respond(a, t, *current, lane)
        out[0, group] = (base_east + east).reshape(piece, 8, 128)
        out[1, group] = (base_north + north).reshape(piece, 8, 128)
        return carry

    lax.fori_loop(0, response.shape[0] // piece, body, 0)


def velocities(sent, received, after):
    count = sent.shape[0]
    _, grid, _, two, response, current = chunked(count)
    return pl.pallas_call(
        velocity_kernel,
        grid=(grid,),
        in_specs=[response, current, ORDER],
        out_specs=two,
        out_shape=jax.ShapeDtypeStruct((2, count, 8, 128), F32),
        compiler_params=params(50),
        cost_estimate=cost(10**7, 4 * MIB),
        name="velocities",
    )(sent, received, after)


def invert_kernel(cols, key, inverse, hot):
    count = cols.shape[0]
    hot[...] = jnp.where(iota((512, 8 * count), 0) == key[...], 1.0, 0.0).astype(BF16)
    lane = iota((8, 1024), 1)
    weights = jnp.where(lane // 128 == iota((8, 1024), 0), lane % 128 + 1, 0).astype(F32).astype(BF16)
    place = iota((128, 128), 0).astype(F32).astype(BF16)
    one, zero = jnp.ones((128, 128), BF16), jnp.zeros((128, 128), BF16)

    def body(i, carry):
        index = cols[i]
        target = jnp.where(index >= 0, (index >> 1) + 64 * (index & 1), -1).astype(F32)
        masks = []
        for s in range(8):
            row = jnp.broadcast_to(target[s : s + 1], (16, 128)).astype(BF16)
            masks.append(jnp.where(place == jnp.concatenate([row] * 8, axis=0), one, zero))
        found = lax.dot_general(
            weights, jnp.concatenate(masks, axis=1), (((1,), (1,)), ((), ())), preferred_element_type=F32
        )
        inverse[i] = found.astype(I32) - 1
        return carry

    lax.fori_loop(0, count, body, 0, unroll=8)


def invert(cols, key):
    count = cols.shape[0]
    return pl.pallas_call(
        invert_kernel,
        out_shape=(jax.ShapeDtypeStruct((count, 8, 128), I32), jax.ShapeDtypeStruct((512, 8 * count), BF16)),
        compiler_params=params(60),
        cost_estimate=cost(10**10, 2 * MIB),
        name="invert",
    )(cols, key)


def stress_kernel(response_in, sent_in, inverse_in, hot_in, *refs):
    planes, side, up, down, parts, response, current_ref, inverse, hot, arrived, listed = refs[-11:]
    count = inverse.shape[0]
    piece = min(count, PIECE)

    def transfer(p):
        span = pl.ds(piece * p, piece)
        return (
            pltpu.make_async_copy(response_in.at[span, pl.ds(0, 4)], response.at[span], arrived.at[0, p]),
            pltpu.make_async_copy(sent_in.at[span, pl.ds(4, 2)], current_ref.at[span], arrived.at[1, p]),
        )

    inverse_copy = pltpu.make_async_copy(inverse_in, inverse, listed.at[0])
    hot_copy = pltpu.make_async_copy(hot_in, hot, listed.at[1])
    for p in range(count // piece):
        for copy in transfer(p):
            copy.start()
        if p == 0:
            inverse_copy.start()
    hot_copy.start()
    inverse_copy.wait()
    tall = 8 * piece
    lane = iota((tall, 128), 1)

    def body(g):
        group = pl.ds(piece * g, piece)
        base_east, base_north, a, t = (response[group, n].reshape(tall, 128) for n in range(4))
        current = [current_ref[group, c].reshape(tall, 128) for c in range(2)]
        east, north = respond(a, t, *current, lane)
        index = inverse[group].reshape(tall, 128)
        inside = jnp.maximum(index, 0)
        for c, drag in enumerate((base_east + east - current[0], base_north + north - current[1])):
            drag = DRAG * drag
            got = jnp.concatenate(
                [lane_gather(drag[8 * i : 8 * i + 8], inside[8 * i : 8 * i + 8]) for i in range(piece)], axis=0
            )
            pieces = split3(jnp.where(index >= 0, got, 0.0))
            for part in range(3):
                rows = pl.ds(pl.multiple_of(8 * count * part + tall * g, tall), tall)
                parts[rows, 128 * c : 128 * c + 128] = pieces[part]

    def move(p, carry):
        for copy in transfer(p):
            copy.wait()
        body(p)
        return carry

    lax.fori_loop(0, count // piece, move, 0)
    hot_copy.wait()
    total = dot(jnp.concatenate([hot[...]] * 3, axis=1), parts[...])
    lane = iota((ROWS, 128), 1)
    low = lane < 64
    top = iota((8, 128), 0) < 4
    edge = jnp.zeros((ROWS, 128), F32)
    for c in range(2):
        ends = {}
        for py in range(2):
            for h in range(2):
                first = 256 * h + 64 * py
                a = total[first : first + 64, 128 * c : 128 * c + 128]
                b = total[first + 128 : first + 192, 128 * c : 128 * c + 128]
                even = jnp.where(low, a, pltpu.roll(b, 64, 1))
                odd = jnp.where(low, pltpu.roll(a, 64, 1), b)
                for px, value in ((0, even), (1, odd)):
                    plane = 2 * py + px
                    planes[c, plane, :, 128 * h : 128 * h + 128] = value
                    ends[plane, h] = jnp.where(top, value[:8], value[56:])
                    item = 4 * c + plane
                    if h == 0:
                        moved = pltpu.roll(value, 8 * item, 1) if item else value
                        edge = jnp.where(lane // 8 == item, moved, edge)
                    else:
                        moved = pltpu.roll(value, (64 + 8 * item + 8) % 128, 1) if item != 7 else value
                        edge = jnp.where(lane // 8 == 8 + item, moved, edge)
        for px in range(2):
            for h in range(2):
                span = slice(128 * h, 128 * h + 128)
                up[2 * c + px, :, span], down[2 * c + px, :, span] = pack_rows(ends[px, h], ends[2 + px, h], top)
    side[...] = edge


def stresses(received, sent, inverse, hot, after):
    count = inverse.shape[0]
    inside = pl.BlockSpec(memory_space=pltpu.VMEM)
    shapes = ((2, 4, ROWS, COLS), (ROWS, 128), (4, 8, COLS), (4, 8, COLS))
    return pl.pallas_call(
        stress_kernel,
        in_specs=[ORDER] * (4 + len(after)),
        out_specs=(inside,) * 4,
        out_shape=tuple(jax.ShapeDtypeStruct(shape, F32) for shape in shapes),
        scratch_shapes=[
            pltpu.VMEM((24 * count, 256), BF16),
            pltpu.VMEM((count, 4, 8, 128), F32),
            pltpu.VMEM((count, 2, 8, 128), F32),
            pltpu.VMEM((count, 8, 128), I32),
            pltpu.VMEM((512, 8 * count), BF16),
            pltpu.SemaphoreType.DMA((2, count // min(count, PIECE))),
            pltpu.SemaphoreType.DMA((2,)),
        ],
        compiler_params=params(60),
        cost_estimate=cost(10**9, 4 * MIB),
        name="stresses",
    )(received, sent, inverse, hot, *after)


MESSAGE = XROWS + 32


def pack_kernel(side, far_below, far_above, to_left, to_right):
    lane = iota((8, 128), 1)
    top = iota((8, COLS), 0) < 4
    corners = [jnp.zeros((8, 128), F32)] * 8
    for n in range(ARRAYS):
        for p in range(4):
            group, slot = divmod(2 * n + p % 2, 16)
            rows = unpack_rows(p // 2, far_below[n, p % 2], far_above[n, p % 2], top)
            first = pltpu.roll(rows[:, :128], 8 * slot, 1) if slot else rows[:, :128]
            last = pltpu.roll(rows[:, 128:], (8 * slot + 8) % 128, 1) if slot != 15 else rows[:, 128:]
            at = 2 * (p // 2) + group
            corners[at] = jnp.where(lane // 8 == slot, first, corners[at])
            corners[4 + at] = jnp.where(lane // 8 == slot, last, corners[4 + at])
    for n, out in enumerate((to_left, to_right)):
        out[0:ROWS] = side[...]
        out[ROWS:XROWS] = jnp.zeros((8, 128), F32)
        for at in range(4):
            out[XROWS + 8 * at : XROWS + 8 * at + 8] = corners[4 * n + at]


def widen_kernel(packed_left, packed_right, below, above, to_left, to_right):
    lane = iota((8, 128), 1)
    top = iota((8, COLS), 0) < 4
    edge = jnp.zeros((8, 128), F32)
    for c in range(2):
        for p in range(4):
            item = 4 * c + p
            rows = unpack_rows(p // 2, below[2 * c + p % 2], above[2 * c + p % 2], top)
            first = pltpu.roll(rows[:, :128], 8 * item, 1) if item else rows[:, :128]
            last = pltpu.roll(rows[:, 128:], (72 + 8 * item) % 128, 1) if item != 7 else rows[:, 128:]
            edge = jnp.where(lane // 8 == item, first, jnp.where(lane // 8 == 8 + item, last, edge))
    for packed, out in ((packed_left, to_left), (packed_right, to_right)):
        out[0:ROWS] = packed[0:ROWS]
        out[ROWS:XROWS] = edge
        out[XROWS:MESSAGE] = packed[XROWS:MESSAGE]


MESSAGE = XROWS + 32


def messages(kernel, name, *arrays):
    return pl.pallas_call(
        kernel,
        out_shape=(jax.ShapeDtypeStruct((MESSAGE, 128), F32),) * 2,
        compiler_params=params(4),
        cost_estimate=cost(10**5, MIB // 2),
        name=name,
    )(*arrays)


ARRAYS = 11


def prepare_kernel(
    sea, forcing, weights, excess, mask, planes, left, right, up, down, halves
):
    lane = iota((8, 128), 1)
    low = lane < 64
    order = jnp.where(low, 2 * lane, 2 * lane - 127)
    swapped = jnp.where(low, 2 * lane + 1, 2 * lane - 128)

    def split(t, carry):
        rows = pl.ds(pl.multiple_of(8 * t, 8), 8)
        w = [weights[k, rows, :] for k in range(8)]
        total = ((w[0] + w[1]) + (w[2] + w[3])) + ((w[4] + w[5]) + (w[6] + w[7]))
        ocean = mask[rows, :] > 0
        inverse = jnp.where(ocean, 1.0 / ((1.0 + excess[rows, :]) * total), 0.0)
        arrays = [v * inverse for v in w]
        arrays += [inverse, forcing[rows, :], jnp.where(ocean, sea[rows, :], 0.0)]
        for n, array in enumerate(arrays):
            for h in range(2):
                a = lane_gather(array[:, 256 * h : 256 * h + 128], order)
                b = lane_gather(array[:, 256 * h + 128 : 256 * h + 256], swapped)
                halves[4 * n + h, rows, :] = jnp.where(low, a, b)
                halves[4 * n + 2 + h, rows, :] = pltpu.roll(jnp.where(low, b, a), 64, 1)
        return carry

    lax.fori_loop(0, 2 * ROWS // 8, split, 0)

    def pack(t, carry):
        out_rows = pl.ds(pl.multiple_of(8 * t, 8), 8)
        for py in range(2):
            rows = pl.ds(16 * t + py, 8, stride=2)
            packed = [[jnp.zeros((8, 128), F32)] * 2, [jnp.zeros((8, 128), F32)] * 2]
            for n in range(ARRAYS):
                for px in range(2):
                    for h in range(2):
                        value = halves[4 * n + 2 * px + h, rows, :]
                        planes[n, 2 * py + px, out_rows, 128 * h : 128 * h + 128] = value
                        item = 2 * n + px
                        shift = (8 * (item % 16) + (8 if h else 0)) % 128
                        moved = pltpu.roll(value, shift, 1) if shift else value
                        packed[h][item // 16] = jnp.where(lane // 8 == item % 16, moved, packed[h][item // 16])
            for g in range(2):
                left[py, out_rows, 128 * g : 128 * g + 128] = packed[0][g]
                right[py, out_rows, 128 * g : 128 * g + 128] = packed[1][g]
        return carry

    lax.fori_loop(0, ROWS // 8, pack, 0)
    top = iota((8, 256), 0) < 4
    for n in range(ARRAYS):
        for px in range(2):
            even, odd = (jnp.where(top, planes[n, p, 0:8], planes[n, p, 56:64]) for p in (px, 2 + px))
            up[n, px], down[n, px] = pack_rows(even, odd, top)


def prepare(sea, forcing, weights, excess, mask):
    return pl.pallas_call(
        prepare_kernel,
        out_shape=(
            jax.ShapeDtypeStruct((ARRAYS, 4, ROWS, COLS), F32),
            jax.ShapeDtypeStruct((2, ROWS, 256), F32),
            jax.ShapeDtypeStruct((2, ROWS, 256), F32),
            jax.ShapeDtypeStruct((ARRAYS, 2, 8, COLS), F32),
            jax.ShapeDtypeStruct((ARRAYS, 2, 8, COLS), F32),
        ),
        scratch_shapes=[pltpu.VMEM((4 * ARRAYS, 2 * ROWS, 128), F32)],
        compiler_params=params(60),
        cost_estimate=cost(10**7, 7 * MIB),
        name="prepare",
    )(sea, forcing, weights, excess, mask)


def place_edges(n, p, right, left, lane):
    slot = (2 * n + p % 2) % 16
    r = pltpu.roll(right, (128 - 8 * slot) % 128, 1) if slot else right
    s = pltpu.roll(left, (120 - 8 * slot) % 128, 1) if slot != 15 else left
    return jnp.where(lane < 8, r, jnp.where(lane >= 120, s, 0.0))


def packed_at(n, p):
    group = (2 * n + p % 2) // 16
    return slice(128 * group, 128 * group + 128)


def extend_kernel(planes, right, left, _, out):
    lane = iota((ROWS, 128), 1)
    for n in range(ARRAYS):
        for p in range(4):
            span = packed_at(n, p)
            out[n, p, :, 0:COLS] = planes[n, p]
            out[n, p, :, COLS:XCOLS] = place_edges(n, p, right[p // 2, :, span], left[p // 2, :, span], lane)


def extend(planes, right, left, after):
    inside = pl.BlockSpec(memory_space=pltpu.VMEM)
    return pl.pallas_call(
        extend_kernel,
        in_specs=[inside] * 3 + [ORDER],
        out_shape=jax.ShapeDtypeStruct((ARRAYS, 4, ROWS, XCOLS), F32),
        compiler_params=params(20),
        cost_estimate=cost(10**7, 8 * MIB),
        name="extend",
    )(planes, right, left, after)


def row_shift(value, step):
    return pltpu.roll(value, (-step) % XROWS, 0) if step else value


def col_shift(value, step):
    return pltpu.roll(value, (-step) % XCOLS, 1) if step else value


def neighbour(step, parity):
    return (step + parity) // 2


def versions_read(plane, start):
    versions = set()
    for colour in COLOURS[start:]:
        if colour == plane:
            break
        across, along = colour // 2 != plane // 2, colour % 2 != plane % 2
        versions |= {1, 2, 3} if across and along else {2} if across else {1}
    return versions


def sweep_kernel(
    operator, far_below, far_above, stress, right, left, below, above, out, wide, source, field, natural, rim
):
    lane = iota((XROWS, 128), 1)
    top = iota((8, COLS), 0) < 4
    from_right, from_left = right[0:XROWS], left[0:XROWS]
    for c in range(2):
        for p in range(4):
            item = 4 * c + p
            r = pltpu.roll(from_right, (128 - 8 * item) % 128, 1) if item else from_right
            s = pltpu.roll(from_left, (56 - 8 * item) % 128, 1) if item != 7 else from_left
            wide[c, p, 0:ROWS, 0:COLS] = stress[c, p]
            wide[c, p, ROWS:XROWS, 0:COLS] = unpack_rows(p // 2, below[2 * c + p % 2], above[2 * c + p % 2], top)
            wide[c, p, :, COLS:XCOLS] = jnp.where(lane < 64, r, s)
    for n in range(ARRAYS):
        for p in range(4):
            first = XROWS + 8 * (2 * (p // 2) + (2 * n + p % 2) // 16)
            rim[n, p, :, 0:COLS] = unpack_rows(p // 2, far_below[n, p % 2], far_above[n, p % 2], top)
            rim[n, p, :, COLS:XCOLS] = place_edges(n, p, right[first : first + 8], left[first : first + 8], lane[:8])

    def entry(n, p):
        return jnp.concatenate([operator[n, p], rim[n, p]], axis=0)

    def publish(p, value, versions):
        field[p, 0] = value
        across, along = (-1 if p // 2 else 1), (-1 if p % 2 else 1)
        if 1 in versions:
            field[p, 1] = col_shift(value, along)
        if 2 in versions:
            moved = row_shift(value, across)
            field[p, 2] = moved
            if 3 in versions:
                field[p, 3] = col_shift(moved, along)

    for p in range(4):
        py, px = p // 2, p % 2
        north = wide[1, 2 * py + 1 - px]
        east = wide[0, 2 * (1 - py) + px]
        zonal = col_shift(north, neighbour(1, px)) - col_shift(north, neighbour(-1, px))
        meridional = row_shift(east, neighbour(1, py)) - row_shift(east, neighbour(-1, py))
        source[p] = (entry(9, p) + zonal - meridional) * entry(8, p)
        publish(p, entry(10, p), versions_read(p, 0))
    for turn_at, colour in enumerate(COLOURS):
        py, px = colour // 2, colour % 2
        value = source[colour]
        for k, (dy, dx) in enumerate(STEPS):
            plane = 2 * (py ^ (dy & 1)) + (px ^ (dx & 1))
            moved = (2 if dy and neighbour(dy, py) else 0) + (1 if dx and neighbour(dx, px) else 0)
            value = value + entry(k, colour) * field[plane, moved]
        publish(colour, value, versions_read(colour, turn_at + 1))
    lane = iota((ROWS, 128), 1)
    even_lane = lane % 2 == 0
    first = lane // 2
    for py in range(2):
        for h in range(2):
            even = field[2 * py, 0, 0:ROWS, 128 * h : 128 * h + 128]
            odd = field[2 * py + 1, 0, 0:ROWS, 128 * h : 128 * h + 128]
            for b in range(2):
                for t in range(ROWS // 8):
                    index = first[:8] + 64 * b
                    e = lane_gather(even[8 * t : 8 * t + 8], index)
                    o = lane_gather(odd[8 * t : 8 * t + 8], index)
                    natural[2 * h + b, pl.ds(16 * t + py, 8, stride=2), :] = jnp.where(even_lane[:8], e, o)
    for k in range(4):
        out[:, 128 * k : 128 * k + 128] = natural[k]


def sweep(*arrays):
    return pl.pallas_call(
        sweep_kernel,
        out_shape=jax.ShapeDtypeStruct((128, 512), F32),
        scratch_shapes=[
            pltpu.VMEM((2, 4, XROWS, XCOLS), F32),
            pltpu.VMEM((4, XROWS, XCOLS), F32),
            pltpu.VMEM((4, 4, XROWS, XCOLS), F32),
            pltpu.VMEM((4, 128, 128), F32),
            pltpu.VMEM((ARRAYS, 4, 8, XCOLS), F32),
        ],
        compiler_params=params(20),
        cost_estimate=cost(10**8, 6 * MIB),
        name="sweep",
    )(*arrays)


AXES = ("zon", "mer")


def exchange(values):
    return lax.all_to_all(values, AXES, split_axis=0, concat_axis=0, tiled=True)


def from_neighbour(values, dz, dm):
    nz, nm = lax.axis_size("zon"), lax.axis_size("mer")
    pairs = [
        (((z + dz) % nz) * nm + m + dm, z * nm + m)
        for z in range(nz)
        for m in range(nm)
        if 0 <= m + dm < nm
    ]
    return lax.ppermute(values, AXES, pairs)


def local(
    sea_level,
    forcing,
    link_weights,
    excess,
    ocean_mask,
    current,
    intersection_block,
    intersection_cols,
    ice_mass,
    coriolis,
    ice_start,
    wind_stress,
):
    blocks = intersection_block[0]
    cols = intersection_cols[0]
    slots = blocks.size
    row, part = blocks >> 2, blocks & 3
    scatter_key = jnp.where(blocks >= 0, part * 128 + (row & 1) * 64 + (row >> 1), -1).reshape(1, slots)
    by_slot = jnp.pad(blocks.T, ((0, 0), (0, 128 - blocks.shape[0])), constant_values=-1)

    sent = send(current, by_slot, cols, ice_mass[0], coriolis[0], ice_start[:, 0], wind_stress[:, 0])
    received = exchange(sent)
    planes, left_edge, right_edge, far_up, far_down = prepare(sea_level, forcing, link_weights, excess, ocean_mask)
    far_right, far_left = from_neighbour(left_edge, 1, 0), from_neighbour(right_edge, -1, 0)
    far_below, far_above = from_neighbour(far_up, 0, 1), from_neighbour(far_down, 0, -1)
    inverse, hot = invert(cols, scatter_key)
    stress, side, up, down = stresses(received, sent, inverse, hot, (left_edge,))
    below, above = from_neighbour(up, 0, 1), from_neighbour(down, 0, -1)
    packed = messages(pack_kernel, "pack", side, far_below, far_above)
    to_left, to_right = messages(widen_kernel, "widen", *packed, below, above)
    right, left = from_neighbour(to_left, 1, 0), from_neighbour(to_right, -1, 0)
    velocity = velocities(sent, received, to_left)
    operator = extend(planes, far_right, far_left, to_left)
    surface = sweep(operator, far_below, far_above, stress, right, left, below, above)
    return surface, velocity[:, None]


def solution(mesh):
    return jax.shard_map(
        local,
        mesh=mesh,
        in_specs=(
            P("mer", "zon"),
            P("mer", "zon"),
            P(None, "mer", "zon"),
            P("mer", "zon"),
            P("mer", "zon"),
            P(None, "mer", "zon"),
            P(("zon", "mer"), None, None),
            P(("zon", "mer"), None, None, None),
            P(("zon", "mer"), None, None, None),
            P(("zon", "mer"), None, None, None),
            P(None, ("zon", "mer"), None, None, None),
            P(None, ("zon", "mer"), None, None, None),
        ),
        out_specs=(P("mer", "zon"), P(None, ("zon", "mer"), None, None, None)),
        check_vma=False,
    )
```

```python
import jax
import jax.numpy as jnp
from jax import lax
from jax.experimental import pallas as pl
from jax.experimental.pallas import tpu as pltpu
from jax.sharding import PartitionSpec as P

SWEEPS = 2
ICE_SWEEPS = 3
DRAG = 1.0
LINK = 0.5
STEPS = ((0, 1), (0, -1), (1, 0), (-1, 0), (1, 1), (1, -1), (-1, 1), (-1, -1))
COLOURS = (0,) + (1, 2, 3, 2, 1, 0) * SWEEPS
F32, BF16, I32 = jnp.float32, jnp.bfloat16, jnp.int32
MIB = 1 << 20
ROWS, COLS, XROWS, XCOLS = 64, 256, 72, 384


def params(vmem=48):
    return pltpu.CompilerParams(vmem_limit_bytes=vmem * MIB)


def cost(flops, moved):
    return pl.CostEstimate(flops=flops, bytes_accessed=moved, transcendentals=0)


def iota(shape, dim):
    return lax.broadcasted_iota(I32, shape, dim)


def lane_gather(values, index):
    return jnp.take_along_axis(values, index, axis=1, mode="promise_in_bounds")


def split3(values):
    high = values.astype(BF16)
    rest = values - high.astype(F32)
    middle = rest.astype(BF16)
    low = (rest - middle.astype(F32)).astype(BF16)
    return high, middle, low


def half_turn(tile):
    return pltpu.roll(tile, 4, 0)


def pack_rows(even_rows, odd_rows, top):
    return (
        jnp.where(top, even_rows, half_turn(odd_rows)),
        jnp.where(top, half_turn(even_rows), odd_rows),
    )


def unpack_rows(py, below, above, top):
    if py:
        return jnp.where(top, half_turn(below), above)
    return jnp.where(top, below, half_turn(above))


def by_parity(axis, a, b):
    odd = jnp.full(a.shape, lax.rem(lax.axis_index(axis), 2), I32) == 1
    return jnp.where(odd, b, a), jnp.where(odd, a, b)


def dot(a, b):
    return jnp.dot(a, b, preferred_element_type=F32)


def beside(values, lane):
    before = jnp.where(lane == 0, 0.0, pltpu.roll(values, 1, 1))
    after = jnp.where(lane == 127, 0.0, pltpu.roll(values, 127, 1))
    return LINK * (before + after)


def turn(a, t, east, north):
    return a * east + t * north, a * north - t * east


def sweep_ice(a, t, east, north, base_east, base_north, lane):
    return turn(a, t, base_east + beside(east, lane), base_north + beside(north, lane))


def respond(a, t, current_east, current_north, lane):
    first_east, first_north = east, north = turn(a, t, current_east, current_north)
    for _ in range(ICE_SWEEPS - 1):
        more_east, more_north = turn(a, t, beside(east, lane), beside(north, lane))
        east, north = first_east + more_east, first_north + more_north
    return east, north


PIECE = 32


def send_kernel(current_in, blocks, *refs):
    ice_in, sent, (current, table, rows, hot), ice, out, (first, arrived, gone) = (
        refs[:5],
        refs[5],
        refs[6:10],
        refs[10:15],
        refs[15],
        refs[16:],
    )
    count = out.shape[0]
    piece = min(count, PIECE)
    current_copy = pltpu.make_async_copy(current_in, current, first.at[0])
    current_copy.start()

    def arrive(p):
        span = pl.ds(piece * p, piece)
        return [
            pltpu.make_async_copy(source.at[span], target.at[span], arrived.at[n, p])
            if n < 3
            else pltpu.make_async_copy(source.at[:, span], target.at[:, span], arrived.at[n, p])
            for n, (source, target) in enumerate(zip(ice_in, ice))
        ]

    def leave(p):
        span = pl.ds(piece * p, piece)
        return pltpu.make_async_copy(out.at[span], sent.at[span], gone.at[p])

    for p in range(count // piece):
        for copy in arrive(p):
            copy.start()

    key = jnp.where(blocks[...] >= 0, (blocks[...] & 3) * 128 + (blocks[...] >> 2), -1)
    key = jnp.transpose(jnp.concatenate([key, jnp.zeros((120, 128), I32)], axis=0))
    place = iota((128, 512), 1)
    for s in range(8):
        hot[128 * s : 128 * s + 128] = jnp.where(key[:, s : s + 1] == place, 1.0, 0.0).astype(BF16)
    current_copy.wait()
    for c in range(2):
        for k in range(4):
            parts = split3(current[c, :, 128 * k : 128 * k + 128])
            for part in range(3):
                first = 512 * part + 128 * k
                table[first : first + 128, 128 * c : 128 * c + 128] = parts[part]
    for q in range(4):
        span = slice(256 * q, 256 * q + 256)
        got = dot(jnp.concatenate([hot[span]] * 3, axis=1), table[...])
        rows[0, span] = got[:, :128]
        rows[1, span] = got[:, 128:]

    tall = 8 * piece
    lane = iota((tall, 128), 1)
    cols, mass_ref, coriolis_ref, start_ref, wind_ref = ice

    def body(g):
        group = pl.ds(piece * g, piece)
        index = cols[group].reshape(tall, 128)
        inside = jnp.maximum(index, 0)
        for c in range(2):
            got = jnp.concatenate(
                [
                    lane_gather(rows[c, pl.ds(piece * g + i, 8, stride=128), :], inside[8 * i : 8 * i + 8])
                    for i in range(piece)
                ],
                axis=0,
            )
            out[group, 4 + c] = jnp.where(index >= 0, DRAG * got, 0.0).reshape(piece, 8, 128)
        mass = mass_ref[group].reshape(tall, 128)
        a = mass + DRAG + 2.0 * LINK
        t = coriolis_ref[group].reshape(tall, 128) * mass
        inverse = 1.0 / (a * a + t * t)
        a = a * inverse
        t = t * inverse
        east = start_ref[0, group].reshape(tall, 128)
        north = start_ref[1, group].reshape(tall, 128)
        base_east = mass * east + wind_ref[0, group].reshape(tall, 128)
        base_north = mass * north + wind_ref[1, group].reshape(tall, 128)
        for _ in range(ICE_SWEEPS):
            east, north = sweep_ice(a, t, east, north, base_east, base_north, lane)
        for n, value in enumerate((east, north, a, t)):
            out[group, n] = value.reshape(piece, 8, 128)

    def move(p, carry):
        for copy in arrive(p):
            copy.wait()
        body(p)
        leave(p).start()
        return carry

    lax.fori_loop(0, count // piece, move, 0)
    for p in range(count // piece):
        leave(p).wait()


ORDER = pl.BlockSpec(memory_space=pl.ANY)


def chunked(count):
    step = min(count, 64)
    one = pl.BlockSpec((step, 8, 128), lambda i: (i, 0, 0))
    two = pl.BlockSpec((2, step, 8, 128), lambda i: (0, i, 0, 0))
    response = pl.BlockSpec((step, 4, 8, 128), lambda i: (i, 0, 0, 0))
    current = pl.BlockSpec((step, 2, 8, 128), lambda i: (i, 2, 0, 0))
    return step, count // step, one, two, response, current


def send(current, blocks, cols, mass, coriolis, start, wind):
    count = cols.shape[0]
    pieces = count // min(count, PIECE)
    one, two = (count, 8, 128), (2, count, 8, 128)
    return pl.pallas_call(
        send_kernel,
        in_specs=[ORDER, pl.BlockSpec(memory_space=pltpu.VMEM)] + [ORDER] * 5,
        out_specs=ORDER,
        out_shape=jax.ShapeDtypeStruct((count, 6, 8, 128), F32),
        scratch_shapes=[
            pltpu.VMEM((2, 128, 512), F32),
            pltpu.VMEM((1536, 256), BF16),
            pltpu.VMEM((2, 1024, 128), F32),
            pltpu.VMEM((1024, 512), BF16),
            pltpu.VMEM(one, I32),
            pltpu.VMEM(one, F32),
            pltpu.VMEM(one, F32),
            pltpu.VMEM(two, F32),
            pltpu.VMEM(two, F32),
            pltpu.VMEM((count, 6, 8, 128), F32),
            pltpu.SemaphoreType.DMA((1,)),
            pltpu.SemaphoreType.DMA((5, pieces)),
            pltpu.SemaphoreType.DMA((pieces,)),
        ],
        compiler_params=params(60),
        cost_estimate=cost(10**9, 8 * MIB),
        name="send",
    )(current, blocks, cols, mass, coriolis, start, wind)


def velocity_kernel(response, current_ref, _, out):
    piece = min(response.shape[0], PIECE)
    tall = 8 * piece
    lane = iota((tall, 128), 1)

    def body(g, carry):
        group = pl.ds(piece * g, piece)
        base_east, base_north, a, t = (response[group, n].reshape(tall, 128) for n in range(4))
        current = [current_ref[group, c].reshape(tall, 128) for c in range(2)]
        east, north = respond(a, t, *current, lane)
        out[0, group] = (base_east + east).reshape(piece, 8, 128)
        out[1, group] = (base_north + north).reshape(piece, 8, 128)
        return carry

    lax.fori_loop(0, response.shape[0] // piece, body, 0)


def velocities(sent, received, after):
    count = sent.shape[0]
    _, grid, _, two, response, current = chunked(count)
    return pl.pallas_call(
        velocity_kernel,
        grid=(grid,),
        in_specs=[response, current, ORDER],
        out_specs=two,
        out_shape=jax.ShapeDtypeStruct((2, count, 8, 128), F32),
        compiler_params=params(50),
        cost_estimate=cost(10**7, 4 * MIB),
        name="velocities",
    )(sent, received, after)


def invert_kernel(cols, key, inverse, hot):
    count = cols.shape[0]
    hot[...] = jnp.where(iota((512, 8 * count), 0) == key[...], 1.0, 0.0).astype(BF16)
    lane = iota((8, 1024), 1)
    weights = jnp.where(lane // 128 == iota((8, 1024), 0), lane % 128 + 1, 0).astype(F32).astype(BF16)
    place = iota((128, 128), 0).astype(F32).astype(BF16)
    one, zero = jnp.ones((128, 128), BF16), jnp.zeros((128, 128), BF16)

    def body(i, carry):
        index = cols[i]
        target = jnp.where(index >= 0, (index >> 1) + 64 * (index & 1), -1).astype(F32)
        masks = []
        for s in range(8):
            row = jnp.broadcast_to(target[s : s + 1], (16, 128)).astype(BF16)
            masks.append(jnp.where(place == jnp.concatenate([row] * 8, axis=0), one, zero))
        found = lax.dot_general(
            weights, jnp.concatenate(masks, axis=1), (((1,), (1,)), ((), ())), preferred_element_type=F32
        )
        inverse[i] = found.astype(I32) - 1
        return carry

    lax.fori_loop(0, count, body, 0, unroll=8)


def invert(cols, key):
    count = cols.shape[0]
    return pl.pallas_call(
        invert_kernel,
        out_shape=(jax.ShapeDtypeStruct((count, 8, 128), I32), jax.ShapeDtypeStruct((512, 8 * count), BF16)),
        compiler_params=params(60),
        cost_estimate=cost(10**10, 2 * MIB),
        name="invert",
    )(cols, key)


def stress_kernel(response_in, sent_in, inverse_in, hot_in, *refs):
    planes, side, first, second, parts, response, current_ref, inverse, hot, arrived, listed = refs[-11:]
    count = inverse.shape[0]
    piece = min(count, PIECE)

    def transfer(p):
        span = pl.ds(piece * p, piece)
        return (
            pltpu.make_async_copy(response_in.at[span, pl.ds(0, 4)], response.at[span], arrived.at[0, p]),
            pltpu.make_async_copy(sent_in.at[span, pl.ds(4, 2)], current_ref.at[span], arrived.at[1, p]),
        )

    inverse_copy = pltpu.make_async_copy(inverse_in, inverse, listed.at[0])
    hot_copy = pltpu.make_async_copy(hot_in, hot, listed.at[1])
    for p in range(count // piece):
        for copy in transfer(p):
            copy.start()
        if p == 0:
            inverse_copy.start()
    hot_copy.start()
    inverse_copy.wait()
    tall = 8 * piece
    lane = iota((tall, 128), 1)

    def body(g):
        group = pl.ds(piece * g, piece)
        base_east, base_north, a, t = (response[group, n].reshape(tall, 128) for n in range(4))
        current = [current_ref[group, c].reshape(tall, 128) for c in range(2)]
        east, north = respond(a, t, *current, lane)
        index = inverse[group].reshape(tall, 128)
        inside = jnp.maximum(index, 0)
        for c, drag in enumerate((base_east + east - current[0], base_north + north - current[1])):
            drag = DRAG * drag
            got = jnp.concatenate(
                [lane_gather(drag[8 * i : 8 * i + 8], inside[8 * i : 8 * i + 8]) for i in range(piece)], axis=0
            )
            pieces = split3(jnp.where(index >= 0, got, 0.0))
            for part in range(3):
                rows = pl.ds(pl.multiple_of(8 * count * part + tall * g, tall), tall)
                parts[rows, 128 * c : 128 * c + 128] = pieces[part]

    def move(p, carry):
        for copy in transfer(p):
            copy.wait()
        body(p)
        return carry

    lax.fori_loop(0, count // piece, move, 0)
    hot_copy.wait()
    total = dot(jnp.concatenate([hot[...]] * 3, axis=1), parts[...])
    lane = iota((ROWS, 128), 1)
    low = lane < 64
    top = iota((8, 128), 0) < 4
    edge = jnp.zeros((ROWS, 128), F32)
    for c in range(2):
        ends = {}
        for py in range(2):
            for h in range(2):
                at = 256 * h + 64 * py
                a = total[at : at + 64, 128 * c : 128 * c + 128]
                b = total[at + 128 : at + 192, 128 * c : 128 * c + 128]
                even = jnp.where(low, a, pltpu.roll(b, 64, 1))
                odd = jnp.where(low, pltpu.roll(a, 64, 1), b)
                for px, value in ((0, even), (1, odd)):
                    plane = 2 * py + px
                    planes[c, plane, :, 128 * h : 128 * h + 128] = value
                    ends[plane, h] = jnp.where(top, value[:8], value[56:])
                    item = 4 * c + plane
                    if h == 0:
                        moved = pltpu.roll(value, 8 * item, 1) if item else value
                        edge = jnp.where(lane // 8 == item, moved, edge)
                    else:
                        moved = pltpu.roll(value, (64 + 8 * item + 8) % 128, 1) if item != 7 else value
                        edge = jnp.where(lane // 8 == 8 + item, moved, edge)
        for px in range(2):
            for h in range(2):
                span = slice(128 * h, 128 * h + 128)
                up, down = pack_rows(ends[px, h], ends[2 + px, h], top)
                first[2 * c + px, :, span], second[2 * c + px, :, span] = by_parity("mer", up, down)
    side[...] = edge


def stresses(received, sent, inverse, hot, after):
    count = inverse.shape[0]
    inside = pl.BlockSpec(memory_space=pltpu.VMEM)
    shapes = ((2, 4, ROWS, COLS), (ROWS, 128), (4, 8, COLS), (4, 8, COLS))
    return pl.pallas_call(
        stress_kernel,
        in_specs=[ORDER] * (4 + len(after)),
        out_specs=(inside,) * 4,
        out_shape=tuple(jax.ShapeDtypeStruct(shape, F32) for shape in shapes),
        scratch_shapes=[
            pltpu.VMEM((24 * count, 256), BF16),
            pltpu.VMEM((count, 4, 8, 128), F32),
            pltpu.VMEM((count, 2, 8, 128), F32),
            pltpu.VMEM((count, 8, 128), I32),
            pltpu.VMEM((512, 8 * count), BF16),
            pltpu.SemaphoreType.DMA((2, count // min(count, PIECE))),
            pltpu.SemaphoreType.DMA((2,)),
        ],
        compiler_params=params(60),
        cost_estimate=cost(10**9, 4 * MIB),
        name="stresses",
    )(received, sent, inverse, hot, *after)


MESSAGE = XROWS + 32


def pack_kernel(side, far_below, far_above, to_left, to_right):
    lane = iota((8, 128), 1)
    top = iota((8, COLS), 0) < 4
    corners = [jnp.zeros((8, 128), F32)] * 8
    for n in range(ARRAYS):
        for p in range(4):
            group, slot = divmod(2 * n + p % 2, 16)
            rows = unpack_rows(p // 2, far_below[n, p % 2], far_above[n, p % 2], top)
            first = pltpu.roll(rows[:, :128], 8 * slot, 1) if slot else rows[:, :128]
            last = pltpu.roll(rows[:, 128:], (8 * slot + 8) % 128, 1) if slot != 15 else rows[:, 128:]
            at = 2 * (p // 2) + group
            corners[at] = jnp.where(lane // 8 == slot, first, corners[at])
            corners[4 + at] = jnp.where(lane // 8 == slot, last, corners[4 + at])
    for n, out in enumerate((to_left, to_right)):
        out[0:ROWS] = side[...]
        out[ROWS:XROWS] = jnp.zeros((8, 128), F32)
        for at in range(4):
            out[XROWS + 8 * at : XROWS + 8 * at + 8] = corners[4 * n + at]


def widen_kernel(packed_left, packed_right, got_first, got_second, first_out, second_out):
    lane = iota((8, 128), 1)
    top = iota((8, COLS), 0) < 4
    edge = jnp.zeros((8, 128), F32)
    for c in range(2):
        for p in range(4):
            item = 4 * c + p
            above, below = by_parity("mer", got_first[2 * c + p % 2], got_second[2 * c + p % 2])
            rows = unpack_rows(p // 2, below, above, top)
            first = pltpu.roll(rows[:, :128], 8 * item, 1) if item else rows[:, :128]
            last = pltpu.roll(rows[:, 128:], (72 + 8 * item) % 128, 1) if item != 7 else rows[:, 128:]
            edge = jnp.where(lane // 8 == item, first, jnp.where(lane // 8 == 8 + item, last, edge))
    for out, packed in zip((first_out, second_out), by_parity("zon", packed_right[...], packed_left[...])):
        out[0:ROWS] = packed[0:ROWS]
        out[ROWS:XROWS] = edge
        out[XROWS:MESSAGE] = packed[XROWS:MESSAGE]


MESSAGE = XROWS + 32


def messages(kernel, name, *arrays):
    return pl.pallas_call(
        kernel,
        out_shape=(jax.ShapeDtypeStruct((MESSAGE, 128), F32),) * 2,
        compiler_params=params(4),
        cost_estimate=cost(10**5, MIB // 2),
        name=name,
    )(*arrays)


ARRAYS = 11


def prepare_kernel(
    sea, forcing, weights, excess, mask, planes, left, right, up, down, halves
):
    lane = iota((8, 128), 1)
    low = lane < 64
    order = jnp.where(low, 2 * lane, 2 * lane - 127)
    swapped = jnp.where(low, 2 * lane + 1, 2 * lane - 128)

    def split(t, carry):
        rows = pl.ds(pl.multiple_of(8 * t, 8), 8)
        w = [weights[k, rows, :] for k in range(8)]
        total = ((w[0] + w[1]) + (w[2] + w[3])) + ((w[4] + w[5]) + (w[6] + w[7]))
        ocean = mask[rows, :] > 0
        inverse = jnp.where(ocean, 1.0 / ((1.0 + excess[rows, :]) * total), 0.0)
        arrays = [v * inverse for v in w]
        arrays += [inverse, forcing[rows, :], jnp.where(ocean, sea[rows, :], 0.0)]
        for n, array in enumerate(arrays):
            for h in range(2):
                a = lane_gather(array[:, 256 * h : 256 * h + 128], order)
                b = lane_gather(array[:, 256 * h + 128 : 256 * h + 256], swapped)
                halves[4 * n + h, rows, :] = jnp.where(low, a, b)
                halves[4 * n + 2 + h, rows, :] = pltpu.roll(jnp.where(low, b, a), 64, 1)
        return carry

    lax.fori_loop(0, 2 * ROWS // 8, split, 0)

    def pack(t, carry):
        out_rows = pl.ds(pl.multiple_of(8 * t, 8), 8)
        for py in range(2):
            rows = pl.ds(16 * t + py, 8, stride=2)
            packed = [[jnp.zeros((8, 128), F32)] * 2, [jnp.zeros((8, 128), F32)] * 2]
            for n in range(ARRAYS):
                for px in range(2):
                    for h in range(2):
                        value = halves[4 * n + 2 * px + h, rows, :]
                        planes[n, 2 * py + px, out_rows, 128 * h : 128 * h + 128] = value
                        item = 2 * n + px
                        shift = (8 * (item % 16) + (8 if h else 0)) % 128
                        moved = pltpu.roll(value, shift, 1) if shift else value
                        packed[h][item // 16] = jnp.where(lane // 8 == item % 16, moved, packed[h][item // 16])
            for g in range(2):
                left[py, out_rows, 128 * g : 128 * g + 128] = packed[0][g]
                right[py, out_rows, 128 * g : 128 * g + 128] = packed[1][g]
        return carry

    lax.fori_loop(0, ROWS // 8, pack, 0)
    top = iota((8, 256), 0) < 4
    for n in range(ARRAYS):
        for px in range(2):
            even, odd = (jnp.where(top, planes[n, p, 0:8], planes[n, p, 56:64]) for p in (px, 2 + px))
            up[n, px], down[n, px] = pack_rows(even, odd, top)


def prepare(sea, forcing, weights, excess, mask):
    return pl.pallas_call(
        prepare_kernel,
        out_shape=(
            jax.ShapeDtypeStruct((ARRAYS, 4, ROWS, COLS), F32),
            jax.ShapeDtypeStruct((2, ROWS, 256), F32),
            jax.ShapeDtypeStruct((2, ROWS, 256), F32),
            jax.ShapeDtypeStruct((ARRAYS, 2, 8, COLS), F32),
            jax.ShapeDtypeStruct((ARRAYS, 2, 8, COLS), F32),
        ),
        scratch_shapes=[pltpu.VMEM((4 * ARRAYS, 2 * ROWS, 128), F32)],
        compiler_params=params(60),
        cost_estimate=cost(10**7, 7 * MIB),
        name="prepare",
    )(sea, forcing, weights, excess, mask)


def place_edges(n, p, right, left, lane):
    slot = (2 * n + p % 2) % 16
    r = pltpu.roll(right, (128 - 8 * slot) % 128, 1) if slot else right
    s = pltpu.roll(left, (120 - 8 * slot) % 128, 1) if slot != 15 else left
    return jnp.where(lane < 8, r, jnp.where(lane >= 120, s, 0.0))


def packed_at(n, p):
    group = (2 * n + p % 2) // 16
    return slice(128 * group, 128 * group + 128)


def extend_kernel(planes, right, left, _, out):
    lane = iota((ROWS, 128), 1)
    for n in range(ARRAYS):
        for p in range(4):
            span = packed_at(n, p)
            out[n, p, :, 0:COLS] = planes[n, p]
            out[n, p, :, COLS:XCOLS] = place_edges(n, p, right[p // 2, :, span], left[p // 2, :, span], lane)


def extend(planes, right, left, after):
    inside = pl.BlockSpec(memory_space=pltpu.VMEM)
    return pl.pallas_call(
        extend_kernel,
        in_specs=[inside] * 3 + [ORDER],
        out_shape=jax.ShapeDtypeStruct((ARRAYS, 4, ROWS, XCOLS), F32),
        compiler_params=params(20),
        cost_estimate=cost(10**7, 8 * MIB),
        name="extend",
    )(planes, right, left, after)


def row_shift(value, step):
    return pltpu.roll(value, (-step) % XROWS, 0) if step else value


def col_shift(value, step):
    return pltpu.roll(value, (-step) % XCOLS, 1) if step else value


def neighbour(step, parity):
    return (step + parity) // 2


def versions_read(plane, start):
    versions = set()
    for colour in COLOURS[start:]:
        if colour == plane:
            break
        across, along = colour // 2 != plane // 2, colour % 2 != plane % 2
        versions |= {1, 2, 3} if across and along else {2} if across else {1}
    return versions


def sweep_kernel(
    operator, far_below, far_above, stress, side_first, side_second, row_first, row_second, out, wide, source, field, natural, rim
):
    lane = iota((XROWS, 128), 1)
    top = iota((8, COLS), 0) < 4
    right, left = by_parity("zon", side_first[...], side_second[...])
    from_right, from_left = right[0:XROWS], left[0:XROWS]
    rows = [by_parity("mer", row_first[n], row_second[n]) for n in range(4)]
    for c in range(2):
        for p in range(4):
            item = 4 * c + p
            r = pltpu.roll(from_right, (128 - 8 * item) % 128, 1) if item else from_right
            s = pltpu.roll(from_left, (56 - 8 * item) % 128, 1) if item != 7 else from_left
            wide[c, p, 0:ROWS, 0:COLS] = stress[c, p]
            above, below = rows[2 * c + p % 2]
            wide[c, p, ROWS:XROWS, 0:COLS] = unpack_rows(p // 2, below, above, top)
            wide[c, p, :, COLS:XCOLS] = jnp.where(lane < 64, r, s)
    for n in range(ARRAYS):
        for p in range(4):
            first = XROWS + 8 * (2 * (p // 2) + (2 * n + p % 2) // 16)
            rim[n, p, :, 0:COLS] = unpack_rows(p // 2, far_below[n, p % 2], far_above[n, p % 2], top)
            rim[n, p, :, COLS:XCOLS] = place_edges(n, p, right[first : first + 8], left[first : first + 8], lane[:8])

    def entry(n, p):
        return jnp.concatenate([operator[n, p], rim[n, p]], axis=0)

    def publish(p, value, versions):
        field[p, 0] = value
        across, along = (-1 if p // 2 else 1), (-1 if p % 2 else 1)
        if 1 in versions:
            field[p, 1] = col_shift(value, along)
        if 2 in versions:
            moved = row_shift(value, across)
            field[p, 2] = moved
            if 3 in versions:
                field[p, 3] = col_shift(moved, along)

    for p in range(4):
        py, px = p // 2, p % 2
        north = wide[1, 2 * py + 1 - px]
        east = wide[0, 2 * (1 - py) + px]
        zonal = col_shift(north, neighbour(1, px)) - col_shift(north, neighbour(-1, px))
        meridional = row_shift(east, neighbour(1, py)) - row_shift(east, neighbour(-1, py))
        source[p] = (entry(9, p) + zonal - meridional) * entry(8, p)
        publish(p, entry(10, p), versions_read(p, 0))
    for turn_at, colour in enumerate(COLOURS):
        py, px = colour // 2, colour % 2
        value = source[colour]
        for k, (dy, dx) in enumerate(STEPS):
            plane = 2 * (py ^ (dy & 1)) + (px ^ (dx & 1))
            moved = (2 if dy and neighbour(dy, py) else 0) + (1 if dx and neighbour(dx, px) else 0)
            value = value + entry(k, colour) * field[plane, moved]
        publish(colour, value, versions_read(colour, turn_at + 1))
    lane = iota((ROWS, 128), 1)
    even_lane = lane % 2 == 0
    first = lane // 2
    for py in range(2):
        for h in range(2):
            even = field[2 * py, 0, 0:ROWS, 128 * h : 128 * h + 128]
            odd = field[2 * py + 1, 0, 0:ROWS, 128 * h : 128 * h + 128]
            for b in range(2):
                for t in range(ROWS // 8):
                    index = first[:8] + 64 * b
                    e = lane_gather(even[8 * t : 8 * t + 8], index)
                    o = lane_gather(odd[8 * t : 8 * t + 8], index)
                    natural[2 * h + b, pl.ds(16 * t + py, 8, stride=2), :] = jnp.where(even_lane[:8], e, o)
    for k in range(4):
        out[:, 128 * k : 128 * k + 128] = natural[k]


def sweep(*arrays):
    return pl.pallas_call(
        sweep_kernel,
        out_shape=jax.ShapeDtypeStruct((128, 512), F32),
        scratch_shapes=[
            pltpu.VMEM((2, 4, XROWS, XCOLS), F32),
            pltpu.VMEM((4, XROWS, XCOLS), F32),
            pltpu.VMEM((4, 4, XROWS, XCOLS), F32),
            pltpu.VMEM((4, 128, 128), F32),
            pltpu.VMEM((ARRAYS, 4, 8, XCOLS), F32),
        ],
        compiler_params=params(20),
        cost_estimate=cost(10**8, 6 * MIB),
        name="sweep",
    )(*arrays)


AXES = ("zon", "mer")


def exchange(values):
    return lax.all_to_all(values, AXES, split_axis=0, concat_axis=0, tiled=True)


def from_neighbour(values, dz, dm):
    nz, nm = lax.axis_size("zon"), lax.axis_size("mer")
    pairs = [
        (((z + dz) % nz) * nm + m + dm, z * nm + m)
        for z in range(nz)
        for m in range(nm)
        if 0 <= m + dm < nm
    ]
    return lax.ppermute(values, AXES, pairs)


def swap(values, axis, start, wrap):
    count = lax.axis_size(axis)
    pairs = [(i, (i + 1) % count) for i in range(start, count if wrap else count - 1, 2)]
    return lax.ppermute(values, axis, pairs + [(j, i) for i, j in pairs])


def local(
    sea_level,
    forcing,
    link_weights,
    excess,
    ocean_mask,
    current,
    intersection_block,
    intersection_cols,
    ice_mass,
    coriolis,
    ice_start,
    wind_stress,
):
    blocks = intersection_block[0]
    cols = intersection_cols[0]
    slots = blocks.size
    row, part = blocks >> 2, blocks & 3
    scatter_key = jnp.where(blocks >= 0, part * 128 + (row & 1) * 64 + (row >> 1), -1).reshape(1, slots)
    by_slot = jnp.pad(blocks.T, ((0, 0), (0, 128 - blocks.shape[0])), constant_values=-1)

    sent = send(current, by_slot, cols, ice_mass[0], coriolis[0], ice_start[:, 0], wind_stress[:, 0])
    received = exchange(sent)
    planes, left_edge, right_edge, far_up, far_down = prepare(sea_level, forcing, link_weights, excess, ocean_mask)
    far_right, far_left = from_neighbour(left_edge, 1, 0), from_neighbour(right_edge, -1, 0)
    far_below, far_above = from_neighbour(far_up, 0, 1), from_neighbour(far_down, 0, -1)
    inverse, hot = invert(cols, scatter_key)
    stress, side, row_first, row_second = stresses(received, sent, inverse, hot, (left_edge,))
    rows = swap(row_first, "mer", 1, False), swap(row_second, "mer", 0, False)
    packed = messages(pack_kernel, "pack", side, far_below, far_above)
    side_first, side_second = messages(widen_kernel, "widen", *packed, *rows)
    sides = swap(side_first, "zon", 0, True), swap(side_second, "zon", 1, True)
    velocity = velocities(sent, received, side_first)
    operator = extend(planes, far_right, far_left, side_first)
    surface = sweep(operator, far_below, far_above, stress, *sides, *rows)
    return surface, velocity[:, None]


def solution(mesh):
    return jax.shard_map(
        local,
        mesh=mesh,
        in_specs=(
            P("mer", "zon"),
            P("mer", "zon"),
            P(None, "mer", "zon"),
            P("mer", "zon"),
            P("mer", "zon"),
            P(None, "mer", "zon"),
            P(("zon", "mer"), None, None),
            P(("zon", "mer"), None, None, None),
            P(("zon", "mer"), None, None, None),
            P(("zon", "mer"), None, None, None),
            P(None, ("zon", "mer"), None, None, None),
            P(None, ("zon", "mer"), None, None, None),
        ),
        out_specs=(P("mer", "zon"), P(None, ("zon", "mer"), None, None, None)),
        check_vma=False,
    )
```
